32 devices in a mesh: context: 8 (over z, y), fsdp: 4 (over x, core).
Axes of the slice: x: 2, y: 2, z: 4, core: 2. Of those that a mesh axis runs over, the one named last changes fastest.
Arguments:
- layer_input: bfloat16 [3, 2048, 1280], P(None, ('context', 'fsdp')), may hold values from -6 to 6
- output_cotangent: bfloat16 [3, 2048, 1280], P(None, ('context', 'fsdp')), may hold values from -6 to 6
- qkv_weight: bfloat16 [3, 1280, 1280], P(None, None, 'fsdp'), may hold values from -0.15625 to 0.15625
- out_weight: bfloat16 [1280, 1280], P('fsdp'), may hold values from -2 to 2
- in_weight: bfloat16 [1280, 1280], P(None, 'fsdp'), may hold values from -0.15625 to 0.15625
- down_weight: bfloat16 [1280, 1280], P('fsdp'), may hold values from -0.15625 to 0.15625
- qv_bias: float32 [2, 1280], P(None, 'fsdp'), may hold values from -0.6 to 0.6
- in_bias: float32 [1280], P('fsdp'), may hold values from -1.5 to 1.5
- out_bias: float32 [2, 1280], replicated, may hold values from -1.5 to 1.5
- norm_gains: float32 [2, 1280], replicated, may hold values from 0.5 to 1.5
- query_scale: float32 [80], replicated, may hold values from -1 to 1.5
- block_table: int32 [8, 2], replicated, may hold values from 0 to 15, as said below
- block_marks: int32 [3, 2048], replicated, may hold values from 0 to 15, never falling along the last dimension, each value on 1 to 256 neighbouring positions
Outputs:
- layer_output: bfloat16 [3, 2048, 1280], P(None, ('context', 'fsdp'))
- input_grad: bfloat16 [3, 2048, 1280], P(None, ('context', 'fsdp'))
- qkv_weight_grad: float32 [3, 1280, 1280], P(None, None, 'fsdp')
- out_weight_grad: float32 [1280, 1280], P('fsdp')
- in_weight_grad: float32 [1280, 1280], P(None, 'fsdp')
- down_weight_grad: float32 [1280, 1280], P('fsdp')
- qv_bias_grad: float32 [2, 1280], P(None, 'fsdp')
- in_bias_grad: float32 [1280], P('fsdp')
- out_bias_grad: float32 [2, 1280], replicated
- gains_grad: float32 [2, 1280], replicated
- scale_grad: float32 [80], replicated
The draws below stay inside these ranges and needn't reach their ends.
Inputs may be any that keep to these rules, and one draw needn't show every extreme that they name: `block_table`: row r is a piece a and its mirror 16 - 1 - a; the first column is a permutation of 0 to 7. `block_marks`: along a row the marks never fall and start at 0; each mark covers 1 to 256 consecutive positions, one exactly 256.
All inputs are finite; a program needn't handle non-finite values.
Results may differ from the reference program's by a relative error of at most 0.015.
Values may be sent and summed in bfloat16 or wider, within the bound.
No kernel may reach another device: no remote copies, remote signals or barrier semaphores. Data moves between devices by JAX's collectives and lax.ppermute only.
A program may use at most 448 MiB of HBM per device.

```python
import math
import jax
import jax.numpy as jnp
import numpy as np
from jax import lax

D = 1280
HEADS = 16
HEAD_DIM = 80
FF = 1280
PIECE = 128
MICRO = 3
MASK_BLOCK = 256
PIECES = 16
SEQ = 2048


def draw_block_table(key, part):
    key = jax.random.fold_in(key, 11)
    first_half = jax.random.permutation(key, PIECES // 2).astype(jnp.int32)
    return jnp.stack([first_half, PIECES - 1 - first_half], axis=1)


def block_scale(rng, shape, shards, smallest, top_value):
    def one(position, shards_of):
        draws = jax.random.uniform(jax.random.fold_in(jax.random.fold_in(rng, 6), position), (shards_of,), jnp.float32, smallest / len(shards), top_value / len(shards))
        return jnp.repeat(jnp.exp(draws), shape[position] // shards_of).reshape((-1,) + (1,) * (len(shape) - position - 1))

    factor_of = one(*shards[0])
    for cut in shards[1:]:
        factor_of = factor_of * one(*cut)
    return factor_of


def length_profile(amount, total, limit, lean):
    weights = [(1 << 20) // math.isqrt(rank ** lean) + 1 for rank in range(2, amount + 1)]
    surplus, holding = total - limit - (amount - 1), [1] * (amount - 1)
    while surplus > 0:
        movable = [i for i in range(amount - 1) if holding[i] < limit]
        mass, budget = sum([weights[i] for i in movable]), surplus
        for i in movable:
            addition = min(limit - holding[i], max(1, budget * weights[i] // mass), surplus)
            holding[i] = holding[i] + addition
            surplus = surplus - addition
    return np.array([limit] + holding)


def uneven(own_key, number_of, total, limit, skew):
    if number_of == 2:
        one = jax.random.randint(own_key, (), max(1, total - limit), min(limit, total - 1) + 1)
        return jnp.stack([one, total - one])
    sizes = jnp.asarray(length_profile(number_of, total, limit, skew), jnp.int32)
    twos = (number_of - 1) // 2
    donor, taker = sizes[1:1 + 2 * twos:2], sizes[2:2 + 2 * twos:2]
    room = jnp.minimum(donor - 1, limit - taker)
    shifted = jax.random.randint(jax.random.fold_in(own_key, 1), (twos,), 0, 1 << 20) % (room + 1)
    sizes = sizes.at[1:1 + 2 * twos:2].set(donor - shifted).at[2:2 + 2 * twos:2].set(taker + shifted)
    return sizes[jax.random.permutation(jax.random.fold_in(own_key, 2), number_of)]


def bell_draw(rng, dims, width, most, cuts=(), kind=jnp.bfloat16):
    values = width * jax.random.normal(rng, dims, jnp.float32)
    if cuts:
        values = values * block_scale(rng, dims, cuts, -0.22, 0.18)
    return jnp.clip(values, -most, most).astype(kind)


def setup_inputs(seed: int = 0) -> dict:
    splits = jax.random.split(jax.random.key(seed), 14)
    layer_input = bell_draw(splits[0], (MICRO, SEQ, D), 1.0, 6.0, ((1, 32),))
    output_cotangent = bell_draw(splits[1], (MICRO, SEQ, D), 1.0, 6.0, ((1, 32),))
    qkv_weight = bell_draw(splits[2], (3, D, D), D ** -0.5, 0.15625, ((2, 4),))
    out_weight = bell_draw(splits[3], (D, D), 8 ** -0.5, 2.0, ((0, 4),))
    in_weight = bell_draw(splits[4], (D, FF), D ** -0.5, 0.15625, ((1, 4),))
    down_weight = bell_draw(splits[5], (FF, D), FF ** -0.5, 0.15625, ((0, 4),))
    qv_bias = bell_draw(splits[6], (2, D), 0.1, 0.6, ((1, 4),), jnp.float32)
    in_bias = bell_draw(splits[7], (FF,), 0.3, 1.5, ((0, 4),), jnp.float32)
    out_bias = bell_draw(splits[8], (2, D), 0.3, 1.5, (), jnp.float32)
    norm_gains = jnp.clip(1.0 + 0.1 * jax.random.normal(splits[9], (2, D), jnp.float32), 0.5, 1.5)
    query_scale = jnp.clip(jax.random.uniform(splits[10], (HEAD_DIM,), jnp.float32, -1.0, 1.5), -1.0, 1.5)
    block_table = draw_block_table(jax.random.fold_in(splits[13], 71), 0)
    block_marks = jax.vmap(lambda own: jnp.searchsorted(jnp.cumsum(uneven(own, 2 * SEQ // MASK_BLOCK, SEQ, MASK_BLOCK, 1)), jnp.arange(SEQ), side="right"))(jax.random.split(splits[12], MICRO)).reshape((MICRO, SEQ)).astype(jnp.int32)
    return {"layer_input": layer_input, "output_cotangent": output_cotangent, "qkv_weight": qkv_weight, "out_weight": out_weight, "in_weight": in_weight, "down_weight": down_weight, "qv_bias": qv_bias, "in_bias": in_bias, "out_bias": out_bias, "norm_gains": norm_gains, "query_scale": query_scale, "block_table": block_table, "block_marks": block_marks}


@jax.custom_vjp
def low(v):
    return lax.optimization_barrier(v.astype(jnp.bfloat16)).astype(jnp.float32)

@jax.custom_vjp
def low_back(v):
    return v

def low_keep(v):
    return (low(v), None)

def low_pass(kept, grad):
    return (grad,)

def back_keep(v):
    return (v, None)

def back_low(kept, grad):
    return (low(grad),)
low.defvjp(low_keep, low_pass)
low_back.defvjp(back_keep, back_low)
epsilon = 1e-06
negative = -1e+30
base_rate = 1.442695041
highest = lax.Precision.HIGHEST

def matmul(left, right):
    return jnp.dot(left, right, precision=highest, preferred_element_type=jnp.float32)

def rms_norm(values, gain):
    return values * lax.rsqrt(lax.optimization_barrier(jnp.mean(values * values, axis=-1, keepdims=True)) + epsilon) * gain

def layer(inputs, qkv_weight, out_weight, in_weight, down_weight, qv_bias, in_bias, out_bias, norm_gains, query_scale, marks):
    seq_rows = inputs.shape[0]
    block_rows = 2 * PIECE
    normed = low(rms_norm(inputs, norm_gains[0]))
    query = matmul(normed, qkv_weight[0]) + qv_bias[0]
    keys = low_back(low(matmul(normed, qkv_weight[1])))
    values = low_back(low(matmul(normed, qkv_weight[2]) + qv_bias[1]))
    factor = jnp.tile(base_rate / math.sqrt(HEAD_DIM) * jax.nn.softplus(query_scale), HEADS)
    scaled = low(low_back(query) * factor)
    key_heads = keys.reshape(seq_rows, HEADS, HEAD_DIM)
    value_heads = values.reshape(seq_rows, HEADS, HEAD_DIM)
    query_blocks = scaled.reshape(seq_rows // block_rows, block_rows, HEADS, HEAD_DIM)
    mark_blocks = marks.reshape(seq_rows // block_rows, block_rows)

    def attend_block(pair):
        query_block, query_marks = pair
        scores = low_back(jnp.einsum('qhd,khd->hqk', query_block, key_heads, precision=highest))
        scores = jnp.where(marks[None, None, :] <= query_marks[None, :, None], scores, negative)
        probability = jnp.exp(scores - jax.nn.logsumexp(scores, axis=-1, keepdims=True))
        return jnp.einsum('hqk,khd->qhd', low(probability), value_heads, precision=highest)
    attended = lax.map(jax.checkpoint(attend_block), (query_blocks, mark_blocks))
    attended = low_back(low(attended.reshape(seq_rows, HEADS * HEAD_DIM)))
    hidden_one = inputs + low_back(matmul(attended, out_weight)) + out_bias[0]
    normed_two = low(rms_norm(hidden_one, norm_gains[1]))
    hidden = low_back(matmul(normed_two, in_weight) + in_bias)
    activated = low(jax.nn.silu(hidden))
    return hidden_one + matmul(activated, down_weight) + out_bias[1]

def reference(layer_input, output_cotangent, qkv_weight, out_weight, in_weight, down_weight, qv_bias, in_bias, out_bias, norm_gains, query_scale, block_table, block_marks):
    flat_table = block_table.reshape(-1).astype(jnp.int32)
    positions = (flat_table[:, None] * PIECE + jnp.arange(PIECE, dtype=jnp.int32)[None, :]).reshape(-1)
    params = tuple((p.astype(jnp.float32) for p in (qkv_weight, out_weight, in_weight, down_weight, qv_bias, in_bias, out_bias, norm_gains, query_scale)))
    totals = tuple((jnp.zeros_like(p) for p in params))
    outputs = []
    input_grads = []
    for batch_index in range(MICRO):
        marks = block_marks[batch_index][positions]
        inputs = layer_input[batch_index].astype(jnp.float32)

        def forward(inputs, *weights):
            return layer(inputs, *weights, marks)
        result, pullback = jax.vjp(forward, inputs, *params)
        grads = pullback(output_cotangent[batch_index].astype(jnp.float32))
        outputs.append(result.astype(jnp.bfloat16))
        input_grads.append(grads[0].astype(jnp.bfloat16))
        totals = tuple((a + b for a, b in zip(totals, grads[1:])))
    return (jnp.stack(outputs), jnp.stack(input_grads), totals[0], totals[1], totals[2], totals[3], totals[4], totals[5], totals[6], totals[7], totals[8])
```

```python
import functools
import math

import jax
import jax.numpy as jnp
from jax import lax
from jax.experimental import pallas as pl
from jax.experimental.pallas import tpu as pltpu
from jax.sharding import PartitionSpec as P

epsilon = 1e-06
negative = -1e30
base_rate = 1.442695041
key_tile = 2048
vmem_bytes = 60 * 1024 * 1024
loop_tile = 1024
bf16 = jnp.bfloat16
f32 = jnp.float32

rows_cols = (((1,), (0,)), ((), ()))
cols_cols = (((1,), (1,)), ((), ()))
rows_rows = (((0,), (0,)), ((), ()))


def mm(left, right, dims=rows_cols):
    return lax.dot_general(left, right, dims, preferred_element_type=f32)


def call(kernel, out_shape, operands, scalars, scratch=(), flops=0, trans=0, tokens=()):
    moved = sum(o.size * o.dtype.itemsize for o in operands)
    moved += sum(o.size * o.dtype.itemsize for o in out_shape)
    specs = [pl.BlockSpec(memory_space=pltpu.SMEM)]
    specs += [pl.BlockSpec(memory_space=pltpu.VMEM)] * len(operands)
    specs += [pl.BlockSpec(memory_space=pl.ANY)] * len(tokens)
    used = 1 + len(operands)
    return pl.pallas_call(
        lambda *refs: kernel(*refs[:used], *refs[used + len(tokens) :]),
        out_shape=tuple(out_shape),
        in_specs=specs,
        out_specs=tuple(pl.BlockSpec(memory_space=pltpu.VMEM) for _ in out_shape),
        scratch_shapes=list(scratch),
        compiler_params=pltpu.CompilerParams(vmem_limit_bytes=vmem_bytes),
        cost_estimate=pl.CostEstimate(flops=flops, bytes_accessed=moved, transcendentals=trans),
    )(scalars, *operands, *tokens)


def loop(count, body):
    if count <= 16:
        for i in range(count):
            body(i)
    else:
        lax.fori_loop(0, count, lambda i, c: (body(i), c)[1], 0)


def shape(dims, kind):
    return jax.ShapeDtypeStruct(tuple(dims), kind)


def exchange(values, axis, size, bit):
    return lax.ppermute(values, axis, [(i, i ^ (1 << bit)) for i in range(size)])


def bits_of(size):
    return size.bit_length() - 1


def after(values, *tokens):
    leaves, tree = jax.tree.flatten(values)
    marks = jax.tree.leaves(tokens)
    anywhere = pl.BlockSpec(memory_space=pl.ANY)
    kept = pl.pallas_call(
        lambda *refs: None,
        out_shape=tuple(shape(v.shape, v.dtype) for v in leaves),
        in_specs=[anywhere] * (len(leaves) + len(marks)),
        out_specs=tuple(anywhere for _ in leaves),
        input_output_aliases={i: i for i in range(len(leaves))},
        cost_estimate=pl.CostEstimate(flops=0, bytes_accessed=0, transcendentals=0),
    )(*leaves, *marks)
    return jax.tree.unflatten(tree, kept)


def scatter_rows(parts, axis, size, tokens=()):
    held = dict(enumerate(parts))
    for bit in range(bits_of(size)):
        step = 1 << bit
        got = {k: exchange(held[k | step], axis, size, bit) for k in reversed(held) if not k & step}
        if bit < len(tokens):
            got = after(got, tokens[bit])
        held = {k: held[k].astype(f32) + got[k].astype(f32) for k in held if not k & step}
        held = {k: v.astype(bf16) if k else v for k, v in held.items()}
    return held[0]


def gather_rows(own, axis, size):
    held = {0: own}
    for bit in reversed(range(bits_of(size))):
        held.update({k | (1 << bit): exchange(v, axis, size, bit) for k, v in list(held.items())})
    return [held[k] for k in range(size)]


def swap_parts(parts, axis, size):
    return [parts[0]] + [lax.ppermute(parts[k], axis, [(i, i ^ k) for i in range(size)]) for k in range(1, size)]


def swap_all(parts, axis):
    return lax.all_to_all(parts, axis, 0, 0, tiled=True)


def summing(streams, axis, size):
    bits = bits_of(size)
    orders = []
    for index in range(len(streams)):
        order = list(range(bits))
        if index % 2 == 1 and bits > 1:
            order[0], order[1] = order[1], order[0]
        orders.append(order)
    held, sizes = list(streams), []
    for step in range(bits):
        sizes.append([h.shape[0] for h in held])
        keep, send = [], []
        for h, order in zip(held, orders):
            half = h.shape[0] // 2
            if h.shape[0] % 2:
                keep.append(h)
                send.append(h)
                continue
            mine = (lax.axis_index(axis) >> order[step]) & 1
            keep.append(lax.dynamic_slice_in_dim(h, mine * half, half, 0))
            send.append(lax.dynamic_slice_in_dim(h, (1 - mine) * half, half, 0))
        got = yield [exchange(v, axis, size, o[step]) for v, o in zip(send, orders)]
        held = [(k.astype(f32) + g.astype(f32)).astype(bf16) for k, g in zip(keep, got)]
    for step in reversed(range(bits)):
        wide = [h.shape[0] < r for h, r in zip(held, sizes[step])]
        got = yield [exchange(h, axis, size, o[step]) if w else h for h, o, w in zip(held, orders, wide)]
        for i, order in enumerate(orders):
            if wide[i]:
                low = ((lax.axis_index(axis) >> order[step]) & 1) == 0
                pair = (jnp.where(low, held[i], got[i]), jnp.where(low, got[i], held[i]))
                held[i] = jnp.concatenate(pair)
    return held


class Flow:
    def __init__(self, steps):
        self.steps, self.result = steps, None
        self.got = next(steps)

    def go(self, *tokens):
        if self.result is None:
            try:
                self.got = self.steps.send(after(self.got, *tokens) if tokens else self.got)
            except StopIteration as end:
                self.result = end.value
        return self.result

    def finish(self):
        while self.result is None:
            self.go()
        return self.result


def chunk(k, rows):
    return pl.ds(pl.multiple_of((k ^ lax.axis_index("fsdp")) * rows, rows), rows)


def first_parity(table):
    return lax.rem(table[0, lax.axis_index("context")], 2)


def invert(table, inverse_ref):
    def note(i):
        half = i % 2 if isinstance(i, int) else lax.rem(i, 2)
        inverse_ref[table[half, i // 2]] = i

    loop(2 * table.shape[1], note)


def store_parts(plan, parity, t, out_ref, b, kind):
    size, heads, group, members, dim, piece, batches = plan
    for h in range(heads):
        block = t[h * dim : (h + 1) * dim]
        cut = [block[:, s * piece : (s + 1) * piece] for s in range(2)]
        if b < batches - 1:
            for u in range(members):
                for s in range(2):
                    out_ref[h * group + b * members + u, 2 * kind + s] = cut[s]
        else:
            base = out_ref.shape[1] // 2 + 1
            for e in range(group):
                if kind == 0:
                    out_ref[h * group + e, base] = jnp.where(parity == e % 2, cut[0], cut[1])
                else:
                    for s in range(2):
                        out_ref[h * group + e, base + 2 * kind - 1 + s] = cut[s]


def project_kernel(plan, spread, sc, *refs):
    x_refs, (w_ref, gain_ref, bias_ref, factor_ref, n1_ref, send_ref) = refs[:spread], refs[spread:]
    batches = plan[6]
    rows = x_refs[0].shape[1]
    parity = first_parity(sc)
    for b in range(batches):
        for k in range(spread):
            x = x_refs[k][b].astype(f32)
            r = lax.rsqrt(jnp.mean(x * x, axis=-1, keepdims=True) + epsilon)
            n1_ref[b, chunk(k, rows), :] = (x * r * gain_ref[...]).astype(bf16)
    n1 = n1_ref[...].reshape(-1, n1_ref.shape[2])
    for i in range(3):
        y = mm(n1, w_ref[i], cols_cols)
        if i == 0:
            y = (y + bias_ref[0:1]) * factor_ref[...]
        elif i == 2:
            y = y + bias_ref[1:2]
        for b in range(batches):
            part = y[b * spread * rows : (b + 1) * spread * rows]
            store_parts(plan, parity, part.T.astype(bf16), send_ref, b, i)


def place(inverse_ref, index):
    slot = inverse_ref[index]
    return slot // 2, lax.rem(slot, 2)


def turned(block):
    filled = jnp.concatenate([block, jnp.zeros((128 - block.shape[0], block.shape[1]), block.dtype)], 0)
    return filled.T


def key_parts(block_index, stride, piece, seq):
    free = 2 * block_index * stride * piece
    last = min(((2 * block_index + 2) * stride + 2) * piece, seq)
    return free, last


def attend_kernel(plans, sc, got_ref, *refs):
    units = len(plans)
    ends, o_ref, outs, scratch = refs[:units], refs[units], refs[units + 1 : -4], refs[-4:]
    invert(sc, scratch[0])
    for i, plan in enumerate(plans):
        attend_unit(plan, got_ref, ends[i], o_ref, outs[2 * i], outs[2 * i + 1], *scratch)


def attend_unit(plan, got_ref, end_ref, o_ref, wide_ref, lse_ref, inverse_ref, k_ref, vt_ref, qt_ref):
    pieces, piece, dim, stride, q_parts, base, o_base = plan
    offset = lax.rem(lax.axis_index("context"), stride)
    seq = pieces * piece
    asked = pieces // stride

    def fill(p):
        at, which = place(inverse_ref, p)
        span = pl.ds(p * piece if isinstance(p, int) else pl.multiple_of(p * piece, piece), piece)
        k_ref[span, :] = turned(got_ref[at, base + q_parts + which])
        vt_ref[:, span] = got_ref[at, base + q_parts + 2 + which]

    loop(pieces, fill)
    for j in range(asked):
        at, which = place(inverse_ref, j * stride + offset)
        qt_ref[0:dim, j * piece : (j + 1) * piece] = got_ref[at, base + (which if q_parts == 2 else 0)]
    qt_ref[dim:, :] = jnp.zeros_like(qt_ref[dim:, :])
    if asked != o_ref.shape[0] * q_parts:
        for part in range(q_parts):
            o_ref[:, o_base + part] = jnp.zeros_like(o_ref[:, o_base + part])
    wide = 2 * piece
    for i in range(asked // 2):
        span = slice(i * wide, (i + 1) * wide)
        qt = qt_ref[:, span]
        end = end_ref[:, span]
        free, last = key_parts(i, stride, piece, seq)
        if last <= key_tile:
            masked = mm(k_ref[free:last, :], qt)
            at = lax.broadcasted_iota(jnp.int32, masked.shape, 0) + free
            masked = jnp.where(at < end, masked, negative)
            top = jnp.max(masked, axis=0, keepdims=True)
            if free:
                plain = mm(k_ref[0:free, :], qt)
                top = jnp.maximum(top, jnp.max(plain, axis=0, keepdims=True))
            weight = jnp.exp(masked - top)
            total = jnp.sum(weight, axis=0, keepdims=True)
            out = mm(vt_ref[:, free:last], weight.astype(bf16))
            if free:
                weight = jnp.exp(plain - top)
                total = total + jnp.sum(weight, axis=0, keepdims=True)
                out = out + mm(vt_ref[:, 0:free], weight.astype(bf16))
        else:

            def tile(t, carry):
                top, total, out = carry
                first = pl.multiple_of(t * loop_tile, loop_tile)
                scores = mm(k_ref[pl.ds(first, loop_tile), :], qt)
                at = lax.broadcasted_iota(jnp.int32, scores.shape, 0) + first
                scores = jnp.where(at < end, scores, negative)
                new = jnp.maximum(top, jnp.max(scores, axis=0, keepdims=True))
                weight = jnp.exp(scores - new)
                change = jnp.exp(top - new)
                total = total * change + jnp.sum(weight, axis=0, keepdims=True)
                out = out * change + mm(vt_ref[:, pl.ds(first, loop_tile)], weight.astype(bf16))
                return new, total, out

            start = (jnp.full((1, wide), negative, f32), jnp.zeros((1, wide), f32), jnp.zeros((dim, wide), f32))
            tiles = min(-(-last // loop_tile), seq // loop_tile)
            top, total, out = lax.fori_loop(0, tiles, tile, start)
        out = out / total
        wide_ref[:, span] = out
        lse_ref[:, span] = top + jnp.log(total)
        for s in range(2):
            at, which = place(inverse_ref, (2 * i + s) * stride + offset)
            o_ref[at, o_base + (which if q_parts == 2 else 0)] = out[:, s * piece : (s + 1) * piece].astype(bf16)


def attend_back_kernel(plans, sc, got_ref, do_ref, factor_ref, *refs):
    units = len(plans)
    saved, d_ref, scale_ref, scratch = refs[: 3 * units], refs[3 * units], refs[3 * units + 1], refs[3 * units + 2 :]
    scale = 0.0
    invert(sc, scratch[0])
    for i, plan in enumerate(plans):
        own = saved[3 * i : 3 * i + 3]
        scale = scale + attend_back_unit(plan, got_ref, do_ref, factor_ref, *own, d_ref, *scratch)
    scale_ref[...] = scale


def attend_back_unit(
    plan, got_ref, do_ref, factor_ref, end_ref, wide_ref, lse_ref, d_ref,
    inverse_ref, k_ref, kt_ref, v_ref, qt_ref, q_ref, dot_ref, dor_ref, dk_ref, dv_ref,
):
    pieces, piece, dim, stride, q_parts, base, o_base = plan
    offset = lax.rem(lax.axis_index("context"), stride)
    seq = pieces * piece
    asked = pieces // stride

    def fill(p):
        at, which = place(inverse_ref, p)
        span = pl.ds(p * piece if isinstance(p, int) else pl.multiple_of(p * piece, piece), piece)
        kt = got_ref[at, base + q_parts + which]
        if seq <= key_tile:
            kt_ref[:, span] = kt
        k_ref[span, :] = turned(kt)
        v_ref[span, :] = turned(got_ref[at, base + q_parts + 2 + which])

    loop(pieces, fill)
    for j in range(asked):
        at, which = place(inverse_ref, j * stride + offset)
        span = slice(j * piece, (j + 1) * piece)
        qt = got_ref[at, base + (which if q_parts == 2 else 0)]
        qt_ref[0:dim, span] = qt
        q_ref[span, :] = turned(qt)
        do = do_ref[at, o_base + (which if q_parts == 2 else 0)]
        dot_ref[0:dim, span] = do
        dor_ref[span, :] = turned(do)
    qt_ref[dim:, :] = jnp.zeros_like(qt_ref[dim:, :])
    dot_ref[dim:, :] = jnp.zeros_like(dot_ref[dim:, :])
    dk_ref[...] = jnp.zeros_like(dk_ref)
    dv_ref[...] = jnp.zeros_like(dv_ref)
    if asked != d_ref.shape[0] * q_parts:
        for part in range(q_parts):
            d_ref[:, base + part] = jnp.zeros_like(d_ref[:, base + part])
    wide = 2 * piece
    scale = jnp.zeros((dim, 1), f32)
    for i in range(asked // 2):
        span = slice(i * wide, (i + 1) * wide)
        qt, q, do, dor = qt_ref[:, span], q_ref[span, :], dot_ref[:, span], dor_ref[span, :]
        end, lse = end_ref[:, span], lse_ref[:, span]
        delta = jnp.sum(do[0:dim].astype(f32) * wide_ref[:, span], axis=0, keepdims=True)
        free, last = key_parts(i, stride, piece, seq)

        def visit(keys, masked_from):
            scores = mm(k_ref[keys, :], qt)
            if masked_from is not None:
                at = lax.broadcasted_iota(jnp.int32, scores.shape, 0) + masked_from
                scores = jnp.where(at < end, scores, negative)
            prob = jnp.exp(scores - lse)
            ds = (prob * (mm(v_ref[keys, :], do) - delta)).astype(bf16)
            dv_ref[keys, :] += mm(prob.astype(bf16), dor)
            dk_ref[keys, :] += mm(ds, q)
            return mm(kt_ref[:, keys] if seq <= key_tile else k_ref[keys, :].T[0:dim], ds)

        if last <= key_tile:
            dq = visit(pl.ds(free, last - free), free)
            if free:
                dq = dq + visit(pl.ds(0, free), None)
        else:

            def tile(t, dq):
                first = pl.multiple_of(t * loop_tile, loop_tile)
                return dq + visit(pl.ds(first, loop_tile), first)

            tiles = min(-(-last // loop_tile), seq // loop_tile)
            dq = lax.fori_loop(0, tiles, tile, jnp.zeros((dim, wide), f32))
        scale = scale + jnp.sum(dq * qt[0:dim].astype(f32), axis=1, keepdims=True)
        dq = (dq * factor_ref[...]).astype(bf16)
        for s in range(2):
            at, which = place(inverse_ref, (2 * i + s) * stride + offset)
            d_ref[at, base + (which if q_parts == 2 else 0)] = dq[:, s * piece : (s + 1) * piece]

    def give(p):
        at, which = place(inverse_ref, p)
        span = pl.ds(p * piece if isinstance(p, int) else pl.multiple_of(p * piece, piece), piece)
        d_ref[at, base + q_parts + which] = dk_ref[span, :].T[0:dim].astype(bf16)
        d_ref[at, base + q_parts + 2 + which] = dv_ref[span, :].T[0:dim].astype(bf16)

    loop(pieces, give)
    return scale


def total_of(blocks):
    if len(blocks) == 1:
        return blocks[0]
    return sum(b.astype(f32) for b in blocks[1:]) + blocks[0].astype(f32)


def collect(plan, even, got_ref, b, which, kind):
    size, heads, group, members, dim, piece, batches = plan
    base = got_ref.shape[1] // 2 + 1
    parts = []
    for h in range(heads):
        if b < batches - 1:
            blocks = [got_ref[h * group + b * members + u, 2 * kind + which] for u in range(members)]
        elif kind == 0:
            parity = even if which == 0 else 1 - even
            blocks = [got_ref[h * group + 2 * u + parity, base] for u in range(group // 2)]
        else:
            blocks = [got_ref[h * group + e, base + 2 * kind - 1 + which] for e in range(group)]
        parts.append(total_of(blocks).astype(bf16))
    return jnp.concatenate(parts, axis=0).T


def give_rows(value, held_ref, out_refs):
    batches, rows, _ = out_refs[0].shape
    held_ref[...] = value.astype(bf16).reshape(held_ref.shape)
    for k, out_ref in enumerate(out_refs):
        for b in range(batches):
            out_ref[b] = held_ref[b, chunk(k, rows), :]


def flat(ref):
    return ref[...].reshape(-1, ref.shape[-1])


def rows_kernel(plan, sc, got_ref, *refs):
    piece, batches = plan[5], plan[6]
    *out_refs, held_ref = refs
    rows = out_refs[0].shape[1]
    even = first_parity(sc)
    for b in range(batches):
        for s in range(2):
            held_ref[b, s * piece : (s + 1) * piece] = collect(plan, even, got_ref, b, s, 0)
        for k, out_ref in enumerate(out_refs):
            out_ref[b] = held_ref[b, chunk(k, rows), :]


def middle_kernel(spread, sc, *refs):
    o_refs, w_refs, bias_refs, refs = refs[:spread], refs[spread : 2 * spread], refs[2 * spread : 3 * spread], refs[3 * spread :]
    x_ref, g_ref, gain_ref, out_bias_ref, out_ref, grad_ref, n2_ref, dy_ref, sums_ref, du_sum_ref = refs[:10]
    a_refs, du_refs, do_refs = [refs[10 + i * spread : 10 + (i + 1) * spread] for i in range(3)]
    local = w_refs[0].shape[0] // 3
    kind = out_ref.shape
    wo = [w[0:local] for w in w_refs]
    wi = [w[local : 2 * local] for w in w_refs]
    wd = [w[2 * local :] for w in w_refs]
    h1 = flat(x_ref).astype(f32) + out_bias_ref[0:1]
    for k in range(spread):
        h1 = h1 + mm(flat(o_refs[k]), wo[k])
    r2 = lax.rsqrt(jnp.mean(h1 * h1, axis=-1, keepdims=True) + epsilon)
    n2 = (h1 * r2 * gain_ref[1:2]).astype(bf16)
    n2_ref[...] = n2.reshape(kind)
    g = flat(g_ref)
    out = h1 + out_bias_ref[1:2]
    dn2 = 0.0
    for k in range(spread):
        u = mm(n2, wi[k], cols_cols) + bias_refs[k][...]
        gate = 1.0 / (1.0 + jnp.exp(-u))
        a = (u * gate).astype(bf16)
        out = out + mm(a, wd[k])
        ga = mm(g, wd[k], cols_cols)
        du = (ga * gate * (1.0 + u * (1.0 - gate))).astype(bf16)
        dn2 = dn2 + mm(du, wi[k])
        a_refs[k][...] = a
        du_refs[k][...] = du
        du_sum_ref[pl.ds(k ^ lax.axis_index("fsdp"), 1), :] = jnp.sum(du.astype(f32), axis=0, keepdims=True)
    out_ref[...] = out.astype(bf16).reshape(kind)
    z2 = gain_ref[1:2] * dn2
    g = g.astype(f32)
    grad = g + r2 * z2 - h1 * (r2 * r2 * r2 * jnp.mean(z2 * h1, axis=-1, keepdims=True))
    grad_ref[...] = grad.reshape(kind)
    dy = grad.astype(bf16)
    dy_ref[...] = dy.reshape(kind)
    sums_ref[0:1] = jnp.sum(dn2 * h1 * r2, axis=0, keepdims=True)
    sums_ref[1:2] = jnp.sum(grad, axis=0, keepdims=True)
    sums_ref[2:3] = jnp.sum(g, axis=0, keepdims=True)
    for k in range(spread):
        do_refs[k][...] = mm(dy, wo[k], cols_cols).astype(bf16).reshape(do_refs[k].shape)


def grads_kernel(spread, sc, *refs):
    o_refs, du_refs, a_refs = [refs[i * spread : (i + 1) * spread] for i in range(3)]
    dy_ref, n2_ref, g_ref = refs[3 * spread : 3 * spread + 3]
    out_refs = refs[3 * spread + 3 :]
    for k in range(spread):
        local = du_refs[k].shape[1]
        out_refs[k][0:local] = mm(flat(o_refs[k]), flat(dy_ref), rows_rows).astype(bf16)
        out_refs[k][local : 2 * local] = mm(du_refs[k][...], flat(n2_ref), rows_rows).astype(bf16)
        out_refs[k][2 * local :] = mm(a_refs[k][...], flat(g_ref), rows_rows).astype(bf16)


def ahead_kernel(plan, spread, sc, *refs):
    do_refs, (send_ref, held_ref) = refs[:spread], refs[spread:]
    rows = do_refs[0].shape[1]
    parity = first_parity(sc)
    for b in range(plan[6]):
        for k in range(spread):
            held_ref[b, chunk(k, rows), :] = do_refs[k][b]
        store_parts(plan, parity, held_ref[b].T, send_ref, b, 0)


def back_kernel(plan, sc, got_ref, w_ref, n1_ref, gain_ref, d_ref, bias_ref, gain_sum_ref, *refs):
    *out_refs, held_ref = refs
    piece = plan[5]
    even = first_parity(sc)
    total = 0.0
    for kind in range(3):
        for b in range(plan[6]):
            for s in range(2):
                d_ref[kind, b, s * piece : (s + 1) * piece] = collect(plan, even, got_ref, b, s, kind)
        rows = d_ref[kind].reshape(-1, d_ref.shape[3])
        if kind != 1:
            bias_ref[kind // 2 : kind // 2 + 1] = jnp.sum(rows.astype(f32), axis=0, keepdims=True)
        total = total + mm(rows, w_ref[kind])
    give_rows(total, held_ref, out_refs)
    gain_sum_ref[...] = jnp.sum(total * flat(n1_ref).astype(f32), axis=0, keepdims=True) / gain_ref[...]


def shards(
    layer_input, output_cotangent, qkv_weight, out_weight, in_weight, down_weight, qv_bias, in_bias,
    out_bias, norm_gains, query_scale, block_table, block_marks,
):
    batches, own, width = layer_input.shape
    local = qkv_weight.shape[2]
    dim = query_scale.shape[0]
    heads = local // dim
    size = lax.axis_size("context")
    spread = lax.axis_size("fsdp")
    pieces = block_table.shape[0] * 2
    seq = block_marks.shape[1]
    piece = seq // pieces
    group = size // heads
    members = group // (batches - 1)
    plan = (size, heads, group, members, dim, piece, batches)
    rows = own * spread
    me = lax.axis_index("context")
    member = me % group
    scalars = block_table.T
    here = jnp.arange(1, seq + 1, dtype=jnp.int32)
    closing = jnp.concatenate([block_marks[:, 1:] != block_marks[:, :-1], jnp.ones((batches, 1), bool)], axis=1)
    ends = lax.cummin(jnp.where(closing, here, seq), axis=1, reverse=True)
    main_end = lax.dynamic_index_in_dim(ends, member // members, 0, keepdims=False)
    main_end = main_end.reshape(-1, members, piece)
    main_end = lax.dynamic_index_in_dim(main_end, member % members, 1, keepdims=False).reshape(1, -1)
    last_end = ends[batches - 1].reshape(-1, group, piece)
    last_end = lax.dynamic_index_in_dim(last_end, member, 1, keepdims=False).reshape(1, -1)
    factor = base_rate / math.sqrt(dim) * jax.nn.softplus(query_scale)
    factor_row = jnp.tile(factor, heads).reshape(1, local)
    factor_col = factor.reshape(dim, 1)
    gain_one, gain_two = norm_gains[0:1], norm_gains[1:2]

    tokens = batches * rows
    weight_flops = 2 * tokens * width * local
    qkv_turned = jnp.swapaxes(qkv_weight, 1, 2)
    in_turned = in_weight.T
    whole = shape((batches, rows, width), bf16)
    narrow = shape((batches, rows, local), bf16)
    parts = [shape((batches, own, width), bf16)] * spread
    thin_parts = [shape((batches, own, local), bf16)] * spread
    held = [pltpu.VMEM((batches, rows, width), bf16)]
    thin_held = [pltpu.VMEM((batches, rows, local), bf16)]
    asked = [pieces // members * piece, pieces // group * piece]
    mine = batches * own

    x_parts = gather_rows(layer_input, "fsdp", spread)
    n1, send = call(
        functools.partial(project_kernel, plan, spread),
        [whole, shape((size, 11, dim, piece), bf16)],
        [*x_parts, qkv_turned, gain_one, qv_bias, factor_row],
        scalars,
        flops=3 * weight_flops,
    )
    packed = jnp.concatenate([out_weight, in_turned, down_weight])
    w_parts = gather_rows(after(packed, x_parts[-1]), "fsdp", spread)
    bias_parts = gather_rows(after(in_bias.reshape(1, local), x_parts[-1]), "fsdp", spread)
    got = swap_all(send, "context")
    plans = [(pieces, piece, dim, members, 2, 0, 0), (pieces, piece, dim, group, 1, 6, 2)]
    o_send, main_wide, main_lse, last_wide, last_lse = call(
        functools.partial(attend_kernel, plans),
        [shape((size, 3, dim, piece), bf16)] + [shape((r, a), f32) for a in asked for r in (dim, 1)],
        [got, main_end, last_end],
        scalars,
        [
            pltpu.SMEM((pieces,), jnp.int32), pltpu.VMEM((seq, 128), bf16), pltpu.VMEM((dim, seq), bf16),
            pltpu.VMEM((128, asked[0]), bf16),
        ],
        flops=3 * sum(asked) * seq * dim,
        trans=sum(asked) * seq,
    )
    o_parts = call(
        functools.partial(rows_kernel, plan), thin_parts, [swap_all(o_send, "context")], scalars, thin_held
    )
    o_parts = swap_parts(o_parts, "fsdp", spread)
    own_kind = shape((batches, own, width), bf16)
    layer_output, grad_one, n2, dy, sums, du_sum, *rest = call(
        functools.partial(middle_kernel, spread),
        [own_kind, shape((batches, own, width), f32), own_kind, own_kind, shape((3, width), f32), shape((spread, local), f32)]
        + [shape((mine, local), bf16)] * (2 * spread)
        + thin_parts,
        [*o_parts, *w_parts, *bias_parts, layer_input, output_cotangent, norm_gains, out_bias],
        scalars,
        flops=12 * mine * width * width,
        trans=mine * local * spread,
    )
    a_parts, du_parts, do_parts = [rest[i * spread : (i + 1) * spread] for i in range(3)]
    w_grads = call(
        functools.partial(grads_kernel, spread),
        [shape((3 * local, width), bf16)] * spread,
        [*o_parts, *du_parts, *a_parts, dy, n2, output_cotangent],
        scalars,
        flops=6 * mine * width * width,
    )
    do_parts = swap_parts(do_parts, "fsdp", spread)
    (do_send,) = call(
        functools.partial(ahead_kernel, plan, spread),
        [shape((size, 3, dim, piece), bf16)],
        do_parts,
        scalars,
        thin_held,
        tokens=w_grads[:1],
    )
    do_got = swap_all(do_send, "context")
    early = scatter_rows([w[None] for w in w_grads], "fsdp", spread)[0].astype(bf16)
    d_send, scale_sum = call(
        functools.partial(attend_back_kernel, plans),
        [shape((size, 11, dim, piece), bf16), shape((dim, 1), f32)],
        [got, do_got, factor_col, main_end, main_wide, main_lse, last_end, last_wide, last_lse],
        scalars,
        [
            pltpu.SMEM((pieces,), jnp.int32),
            pltpu.VMEM((seq, 128), bf16), pltpu.VMEM((dim, min(seq, key_tile)), bf16), pltpu.VMEM((seq, 128), bf16),
            pltpu.VMEM((128, asked[0]), bf16), pltpu.VMEM((asked[0], 128), bf16),
            pltpu.VMEM((128, asked[0]), bf16), pltpu.VMEM((asked[0], 128), bf16),
            pltpu.VMEM((seq, 128), f32), pltpu.VMEM((seq, 128), f32),
        ],
        flops=8 * sum(asked) * seq * dim,
        trans=sum(asked) * seq,
    )
    d_got = swap_all(d_send, "context")
    half = early.shape[0] // 2
    early = after(early, d_got)
    early_flow = Flow(summing([early[:half], early[half:]], "context", size))

    d_rows, qv_sum, gain_one_sum, *part = call(
        functools.partial(back_kernel, plan),
        [shape((3, batches, rows, local), bf16), shape((2, local), f32), shape((1, width), f32)] + parts,
        [d_got, qkv_turned, n1, gain_one],
        scalars,
        held,
        flops=3 * weight_flops,
    )
    flat_rows = lambda v: v.reshape(tokens, -1)
    qkv = lax.dot_general(
        d_rows.reshape(3, tokens, local), flat_rows(n1), (((1,), (0,)), ((), ())), preferred_element_type=f32
    ).astype(bf16).reshape(3 * local, width)
    half = 3 * local // 2
    qkv_flow = Flow(summing([qkv[:half], qkv[half:]], "context", size))

    scale_part = scale_sum.reshape(-1) / factor
    small = jnp.concatenate([gain_one_sum.reshape(-1), sums.reshape(-1), du_sum.reshape(-1), scale_part])
    steps = [("fsdp", spread, bit) for bit in range(bits_of(spread))]
    steps += [("context", size, bit) for bit in range(bits_of(size))]
    early_flow.go()
    grad_normed = scatter_rows(part, "fsdp", spread)
    for index, (axis, count, bit) in enumerate(steps):
        small = after(small, qkv_flow.got)
        if index == bits_of(spread):
            small = jnp.concatenate([qv_sum.reshape(-1), small])
        got_small = exchange(small, axis, count, bit)
        qkv_flow.go()
        early_flow.go()
        small = small + got_small
    early = jnp.concatenate(early_flow.finish()).astype(f32)
    qkv = jnp.concatenate(qkv_flow.finish()).astype(f32).reshape(3, local, width)
    out_grad = early[:local]
    feed_grads = [early[local : 2 * local], early[2 * local :]]
    qv_grad = small[: 2 * local].reshape(2, local)
    rest = small[2 * local :]
    gains_grad = rest[: 2 * width].reshape(2, width)
    out_bias_grad = rest[2 * width : 4 * width].reshape(2, width)
    rest = rest[4 * width :]
    in_bias_grad = rest[: spread * local].reshape(spread, local)
    in_bias_grad = lax.dynamic_index_in_dim(in_bias_grad, lax.axis_index("fsdp"), 0, keepdims=False)
    scale_grad = rest[spread * local :] * (base_rate / math.sqrt(dim)) * jax.nn.sigmoid(query_scale)

    x_own = layer_input.astype(f32)
    factor_one = lax.rsqrt(jnp.mean(x_own * x_own, axis=-1, keepdims=True) + epsilon)
    weighted = norm_gains[0] * grad_normed
    inner = jnp.mean(weighted * x_own, axis=-1, keepdims=True)
    input_grad = (grad_one + factor_one * weighted - x_own * factor_one**3 * inner).astype(bf16)
    return (
        layer_output,
        input_grad,
        jnp.swapaxes(qkv, 1, 2),
        out_grad,
        feed_grads[0].T,
        feed_grads[1],
        qv_grad,
        in_bias_grad,
        out_bias_grad,
        gains_grad,
        scale_grad,
    )


def solution(mesh):
    in_specs = (
        P(None, ("context", "fsdp"), None),
        P(None, ("context", "fsdp"), None),
        P(None, None, "fsdp"),
        P("fsdp", None),
        P(None, "fsdp"),
        P("fsdp", None),
        P(None, "fsdp"),
        P("fsdp"),
        P(),
        P(),
        P(),
        P(),
        P(),
    )
    out_specs = (
        P(None, ("context", "fsdp"), None),
        P(None, ("context", "fsdp"), None),
        P(None, None, "fsdp"),
        P("fsdp", None),
        P(None, "fsdp"),
        P("fsdp", None),
        P(None, "fsdp"),
        P("fsdp"),
        P(),
        P(),
        P(),
    )
    return jax.shard_map(shards, mesh=mesh, in_specs=in_specs, out_specs=out_specs, check_vma=False)
```

```python
import functools
import math

import jax
import jax.numpy as jnp
from jax import lax
from jax.experimental import pallas as pl
from jax.experimental.pallas import tpu as pltpu
from jax.sharding import PartitionSpec as P

epsilon = 1e-06
negative = -1e30
base_rate = 1.442695041
key_tile = 2048
vmem_bytes = 60 * 1024 * 1024
loop_tile = 1024
kernel_us = {
    "project_kernel": 7, "attend_kernel": 11, "middle_kernel": 14, "attend_back_kernel": 15, "grads_kernel": 7, "back_kernel": 11,
}
ahead_rounds = 1
flops_per_us = 1153500000
bf16 = jnp.bfloat16
f32 = jnp.float32

rows_cols = (((1,), (0,)), ((), ()))
cols_cols = (((1,), (1,)), ((), ()))
rows_rows = (((0,), (0,)), ((), ()))


def mm(left, right, dims=rows_cols):
    return lax.dot_general(left, right, dims, preferred_element_type=f32)


def call(kernel, out_shape, operands, scalars, scratch=(), tokens=(), weight=1):
    specs = [pl.BlockSpec(memory_space=pltpu.SMEM)]
    specs += [pl.BlockSpec(memory_space=pltpu.VMEM)] * len(operands)
    specs += [pl.BlockSpec(memory_space=pl.ANY)] * len(tokens)
    used = 1 + len(operands)
    weight = kernel_us.get(getattr(kernel, "func", kernel).__name__, weight)
    return pl.pallas_call(
        lambda *refs: kernel(*refs[:used], *refs[used + len(tokens) :]),
        out_shape=tuple(out_shape),
        in_specs=specs,
        out_specs=tuple(pl.BlockSpec(memory_space=pltpu.VMEM) for _ in out_shape),
        scratch_shapes=list(scratch),
        compiler_params=pltpu.CompilerParams(vmem_limit_bytes=vmem_bytes),
        cost_estimate=pl.CostEstimate(flops=int(weight * flops_per_us), bytes_accessed=0, transcendentals=0),
    )(scalars, *operands, *tokens)


def loop(count, body):
    if count <= 16:
        for i in range(count):
            body(i)
    else:
        lax.fori_loop(0, count, lambda i, c: (body(i), c)[1], 0)


def shape(dims, kind):
    return jax.ShapeDtypeStruct(tuple(dims), kind)


def exchange(values, axis, size, bit):
    return lax.ppermute(values, axis, [(i, i ^ (1 << bit)) for i in range(size)])


def bits_of(size):
    return size.bit_length() - 1


def after(values, *tokens):
    leaves, tree = jax.tree.flatten(values)
    marks = jax.tree.leaves(tokens)
    anywhere = pl.BlockSpec(memory_space=pl.ANY)
    kept = pl.pallas_call(
        lambda *refs: None,
        out_shape=tuple(shape(v.shape, v.dtype) for v in leaves),
        in_specs=[anywhere] * (len(leaves) + len(marks)),
        out_specs=tuple(anywhere for _ in leaves),
        input_output_aliases={i: i for i in range(len(leaves))},
        cost_estimate=pl.CostEstimate(flops=0, bytes_accessed=0, transcendentals=0),
    )(*leaves, *marks)
    return jax.tree.unflatten(tree, kept)


def gather_rows(own, axis, size, token=None):
    held = {0: own}
    for bit in reversed(range(bits_of(size))):
        if token is not None:
            held = {k: after(v, token) if k else v for k, v in held.items()}
        held.update({k | (1 << bit): exchange(v, axis, size, bit) for k, v in list(held.items())})
    return [held[k] for k in range(size)]


def spread_rows(own, first, axis, size, token):
    top = bits_of(size) - 1
    held = {0: own}
    for bit in reversed(range(top)):
        held.update({k | (1 << bit): exchange(v, axis, size, bit) for k, v in list(held.items())})
    held[1 << top] = after(first, token)
    for bit in reversed(range(top)):
        more = [k for k in held if k >> top and not k & ((1 << (bit + 1)) - 1)]
        held.update({k | (1 << bit): exchange(held[k], axis, size, bit) for k in more})
    return [held[k] for k in range(size)]


def scatter_parts(parts, axis, size):
    held = {k: [v] for k, v in enumerate(parts)}
    sent = parts[0]
    for bit in range(bits_of(size)):
        step = 1 << bit
        for k in reversed([k for k in held if k & step]):
            terms = held.pop(k)
            if len(terms) > 1:
                terms = [sum(t.astype(f32) for t in terms).astype(bf16)]
            sent = terms[0]
            held[k ^ step].append(exchange(sent, axis, size, bit))
    return held[0], sent


def swap_parts(parts, axis, size):
    return [parts[0]] + [lax.ppermute(parts[k], axis, [(i, i ^ k) for i in range(size)]) for k in range(1, size)]


def swap_all(parts, axis):
    return lax.all_to_all(parts, axis, 0, 0, tiled=True)


def with_bit(index, place, bit):
    low = index & ((1 << place) - 1)
    return low | (bit << place) | ((index >> place) << (place + 1))


class Sums:
    def __init__(self, size, kinds, rows, lanes):
        self.size, self.bits = size, bits_of(size)
        self.block = (kinds, rows, lanes)
        first = list(range(self.bits))
        second = first[:]
        if self.bits > 1:
            second[0], second[1] = 1, 0
        self.orders = [first, second]
        self.step, self.result = 0, None

    def bit(self, stream, step):
        return self.orders[stream][step if step < self.bits else 2 * self.bits - 1 - step]

    def left(self, stream, step):
        order = self.orders[stream]
        return sorted(order[step + 1 :] if step < self.bits else order[2 * self.bits - step :])

    def groups(self, step):
        found = {}
        for stream in range(2):
            found.setdefault(self.bit(stream, step), []).append(stream)
        return [(bit, streams, 1 << len(self.left(streams[0], step))) for bit, streams in found.items()]

    def shapes(self, step):
        return [shape((len(streams) * count,) + self.block, bf16) for _, streams, count in self.groups(step)]

    def at(self, refs, stream, step, index):
        for ref, (_, streams, count) in zip(refs, self.groups(step)):
            if stream in streams:
                return ref.at[streams.index(stream) * count + index]

    def deal(self, read, send_refs, keep_refs, step):
        me = lax.axis_index("context")
        for stream in range(2):
            bit, left = self.bit(stream, step), self.left(stream, step)
            place = sorted(left + [bit]).index(bit)
            mine = (me >> bit) & 1
            for j in range(1 << len(left)):
                self.at(send_refs, stream, step, j)[...] = read(stream, with_bit(j, place, 1 - mine)).astype(bf16)
                self.at(keep_refs, stream, step, j)[...] = read(stream, with_bit(j, place, mine)).astype(bf16)

    def start(self, send, keep):
        self.keep = keep
        self.got = [exchange(v, "context", self.size, bit) for v, (bit, _, _) in zip(send, self.groups(self.step))]

    def fold(self, scalars, finals=(), extra=(), tokens=()):
        step, last = self.step, self.step == 2 * self.bits - 1
        halving = step + 1 < self.bits
        outs = list(finals) if last else self.shapes(step + 1) * (2 if halving else 1)
        count, width = len(self.keep), len(outs)

        def kernel(sc, *refs):
            keep, got = refs[:count], refs[count : 2 * count]
            pairs, out = refs[2 * count : 2 * count + 2 * len(extra)], refs[2 * count + 2 * len(extra) :]
            for i in range(len(extra)):
                out[width + i][...] = pairs[2 * i][...] + pairs[2 * i + 1][...]

            def total(stream, index):
                return self.at(keep, stream, step, index)[...].astype(f32) + self.at(got, stream, step, index)[...].astype(f32)

            if halving:
                half = len(outs) // 2
                self.deal(total, out[:half], out[half:width], step + 1)
                return
            me = lax.axis_index("context")
            for stream in range(2):
                if step < self.bits:
                    self.at(out, stream, step + 1, 0)[...] = total(stream, 0).astype(bf16)
                    continue
                bit, left = self.bit(stream, step), self.left(stream, step)
                place = sorted(left + [bit]).index(bit)
                mine = (me >> bit) & 1
                for j in range(1 << len(left)):
                    for refs_in, side in ((keep, mine), (got, 1 - mine)):
                        value = self.at(refs_in, stream, step, j)[...]
                        index = with_bit(j, place, side)
                        if not last:
                            self.at(out, stream, step + 1, index)[...] = value
                            continue
                        kinds, rows, lanes = self.block
                        span = pl.ds(pl.multiple_of(index * rows, rows), rows)
                        for kind in range(kinds):
                            to = out[kind] if width > 1 else out[0].at[kind]
                            to[span, stream * lanes : (stream + 1) * lanes] = value[kind].astype(f32)

        outs = outs + [shape(a.shape, a.dtype) for a, _ in extra]
        operands = [*self.keep, *self.got] + [v for pair in extra for v in pair]
        made = list(call(kernel, outs, operands, scalars, tokens=tokens, weight=8))
        self.step += 1
        self.token = made[0]
        if last:
            self.result = made[:width]
        elif halving:
            self.start(made[: width // 2], made[width // 2 : width])
        else:
            self.start(made[:width], made[:width])
        return made[width:]


def chunk(k, rows):
    return pl.ds(pl.multiple_of((k ^ lax.axis_index("fsdp")) * rows, rows), rows)


def first_parity(table):
    return lax.rem(table[0, lax.axis_index("context")], 2)


def invert(table, inverse_ref):
    def note(i):
        half = i % 2 if isinstance(i, int) else lax.rem(i, 2)
        inverse_ref[table[half, i // 2]] = i

    loop(2 * table.shape[1], note)


def store_parts(plan, parity, t, out_ref, b, kind):
    size, heads, group, members, dim, piece, batches = plan
    for h in range(heads):
        block = t[h * dim : (h + 1) * dim]
        cut = [block[:, s * piece : (s + 1) * piece] for s in range(2)]
        if b < batches - 1:
            for u in range(members):
                for s in range(2):
                    out_ref[h * group + b * members + u, 2 * kind + s] = cut[s]
        else:
            base = out_ref.shape[1] // 2 + 1
            for e in range(group):
                if kind == 0:
                    out_ref[h * group + e, base] = jnp.where(parity == e % 2, cut[0], cut[1])
                else:
                    for s in range(2):
                        out_ref[h * group + e, base + 2 * kind - 1 + s] = cut[s]


def project_kernel(plan, spread, sc, *refs):
    x_refs, (w_ref, gain_ref, bias_ref, factor_ref, n1_ref, send_ref) = refs[:spread], refs[spread:]
    batches = plan[6]
    rows = x_refs[0].shape[1]
    parity = first_parity(sc)
    for b in range(batches):
        for k in range(spread):
            x = x_refs[k][b].astype(f32)
            r = lax.rsqrt(jnp.mean(x * x, axis=-1, keepdims=True) + epsilon)
            n1_ref[b, chunk(k, rows), :] = (x * r * gain_ref[...]).astype(bf16)
    n1 = n1_ref[...].reshape(-1, n1_ref.shape[2])
    for i in range(3):
        y = mm(n1, w_ref[i], cols_cols)
        if i == 0:
            y = (y + bias_ref[0:1]) * factor_ref[...]
        elif i == 2:
            y = y + bias_ref[1:2]
        for b in range(batches):
            part = y[b * spread * rows : (b + 1) * spread * rows]
            store_parts(plan, parity, part.T.astype(bf16), send_ref, b, i)


def place(inverse_ref, index):
    slot = inverse_ref[index]
    return slot // 2, lax.rem(slot, 2)


def turned(block):
    filled = jnp.concatenate([block, jnp.zeros((128 - block.shape[0], block.shape[1]), block.dtype)], 0)
    return filled.T


def key_parts(block_index, stride, piece, seq):
    free = 2 * block_index * stride * piece
    last = min(((2 * block_index + 2) * stride + 2) * piece, seq)
    return free, last


def attend_kernel(plans, sc, got_ref, *refs):
    units = len(plans)
    ends, o_ref, outs, scratch = refs[:units], refs[units], refs[units + 1 : -4], refs[-4:]
    invert(sc, scratch[0])
    for i, plan in enumerate(plans):
        attend_unit(plan, got_ref, ends[i], o_ref, outs[2 * i], outs[2 * i + 1], *scratch)


def attend_unit(plan, got_ref, end_ref, o_ref, wide_ref, lse_ref, inverse_ref, k_ref, vt_ref, qt_ref):
    pieces, piece, dim, stride, q_parts, base, o_base = plan
    offset = lax.rem(lax.axis_index("context"), stride)
    seq = pieces * piece
    asked = pieces // stride

    def fill(p):
        at, which = place(inverse_ref, p)
        span = pl.ds(p * piece if isinstance(p, int) else pl.multiple_of(p * piece, piece), piece)
        k_ref[span, :] = turned(got_ref[at, base + q_parts + which])
        vt_ref[:, span] = got_ref[at, base + q_parts + 2 + which]

    loop(pieces, fill)
    for j in range(asked):
        at, which = place(inverse_ref, j * stride + offset)
        qt_ref[0:dim, j * piece : (j + 1) * piece] = got_ref[at, base + (which if q_parts == 2 else 0)]
    qt_ref[dim:, :] = jnp.zeros_like(qt_ref[dim:, :])
    if asked != o_ref.shape[0] * q_parts:
        for part in range(q_parts):
            o_ref[:, o_base + part] = jnp.zeros_like(o_ref[:, o_base + part])
    wide = 2 * piece
    for i in range(asked // 2):
        span = slice(i * wide, (i + 1) * wide)
        qt = qt_ref[:, span]
        end = end_ref[:, span]
        free, last = key_parts(i, stride, piece, seq)
        if last <= key_tile:
            masked = mm(k_ref[free:last, :], qt)
            at = lax.broadcasted_iota(jnp.int32, masked.shape, 0) + free
            masked = jnp.where(at < end, masked, negative)
            top = jnp.max(masked, axis=0, keepdims=True)
            if free:
                plain = mm(k_ref[0:free, :], qt)
                top = jnp.maximum(top, jnp.max(plain, axis=0, keepdims=True))
            weight = jnp.exp(masked - top)
            total = jnp.sum(weight, axis=0, keepdims=True)
            out = mm(vt_ref[:, free:last], weight.astype(bf16))
            if free:
                weight = jnp.exp(plain - top)
                total = total + jnp.sum(weight, axis=0, keepdims=True)
                out = out + mm(vt_ref[:, 0:free], weight.astype(bf16))
        else:

            def tile(t, carry):
                top, total, out = carry
                first = pl.multiple_of(t * loop_tile, loop_tile)
                scores = mm(k_ref[pl.ds(first, loop_tile), :], qt)
                at = lax.broadcasted_iota(jnp.int32, scores.shape, 0) + first
                scores = jnp.where(at < end, scores, negative)
                new = jnp.maximum(top, jnp.max(scores, axis=0, keepdims=True))
                weight = jnp.exp(scores - new)
                change = jnp.exp(top - new)
                total = total * change + jnp.sum(weight, axis=0, keepdims=True)
                out = out * change + mm(vt_ref[:, pl.ds(first, loop_tile)], weight.astype(bf16))
                return new, total, out

            start = (jnp.full((1, wide), negative, f32), jnp.zeros((1, wide), f32), jnp.zeros((dim, wide), f32))
            tiles = min(-(-last // loop_tile), seq // loop_tile)
            top, total, out = lax.fori_loop(0, tiles, tile, start)
        out = out / total
        wide_ref[:, span] = out
        lse_ref[:, span] = top + jnp.log(total)
        for s in range(2):
            at, which = place(inverse_ref, (2 * i + s) * stride + offset)
            o_ref[at, o_base + (which if q_parts == 2 else 0)] = out[:, s * piece : (s + 1) * piece].astype(bf16)


def attend_back_kernel(plans, sc, got_ref, do_ref, factor_ref, *refs):
    units = len(plans)
    saved, d_ref, scale_ref, scratch = refs[: 3 * units], refs[3 * units], refs[3 * units + 1], refs[3 * units + 2 :]
    scale = 0.0
    invert(sc, scratch[0])
    for i, plan in enumerate(plans):
        own = saved[3 * i : 3 * i + 3]
        scale = scale + attend_back_unit(plan, got_ref, do_ref, factor_ref, *own, d_ref, *scratch)
    scale_ref[...] = scale


def attend_back_unit(
    plan, got_ref, do_ref, factor_ref, end_ref, wide_ref, lse_ref, d_ref,
    inverse_ref, k_ref, kt_ref, v_ref, qt_ref, q_ref, dot_ref, dor_ref, dk_ref, dv_ref,
):
    pieces, piece, dim, stride, q_parts, base, o_base = plan
    offset = lax.rem(lax.axis_index("context"), stride)
    seq = pieces * piece
    asked = pieces // stride

    def fill(p):
        at, which = place(inverse_ref, p)
        span = pl.ds(p * piece if isinstance(p, int) else pl.multiple_of(p * piece, piece), piece)
        kt = got_ref[at, base + q_parts + which]
        if seq <= key_tile:
            kt_ref[:, span] = kt
        k_ref[span, :] = turned(kt)
        v_ref[span, :] = turned(got_ref[at, base + q_parts + 2 + which])

    loop(pieces, fill)
    for j in range(asked):
        at, which = place(inverse_ref, j * stride + offset)
        span = slice(j * piece, (j + 1) * piece)
        qt = got_ref[at, base + (which if q_parts == 2 else 0)]
        qt_ref[0:dim, span] = qt
        q_ref[span, :] = turned(qt)
        do = do_ref[at, o_base + (which if q_parts == 2 else 0)]
        dot_ref[0:dim, span] = do
        dor_ref[span, :] = turned(do)
    qt_ref[dim:, :] = jnp.zeros_like(qt_ref[dim:, :])
    dot_ref[dim:, :] = jnp.zeros_like(dot_ref[dim:, :])
    dk_ref[...] = jnp.zeros_like(dk_ref)
    dv_ref[...] = jnp.zeros_like(dv_ref)
    if asked != d_ref.shape[0] * q_parts:
        for part in range(q_parts):
            d_ref[:, base + part] = jnp.zeros_like(d_ref[:, base + part])
    wide = 2 * piece
    scale = jnp.zeros((dim, 1), f32)
    for i in range(asked // 2):
        span = slice(i * wide, (i + 1) * wide)
        qt, q, do, dor = qt_ref[:, span], q_ref[span, :], dot_ref[:, span], dor_ref[span, :]
        end, lse = end_ref[:, span], lse_ref[:, span]
        delta = jnp.sum(do[0:dim].astype(f32) * wide_ref[:, span], axis=0, keepdims=True)
        free, last = key_parts(i, stride, piece, seq)

        def visit(keys, masked_from):
            scores = mm(k_ref[keys, :], qt)
            if masked_from is not None:
                at = lax.broadcasted_iota(jnp.int32, scores.shape, 0) + masked_from
                scores = jnp.where(at < end, scores, negative)
            prob = jnp.exp(scores - lse)
            ds = (prob * (mm(v_ref[keys, :], do) - delta)).astype(bf16)
            dv_ref[keys, :] += mm(prob.astype(bf16), dor)
            dk_ref[keys, :] += mm(ds, q)
            return mm(kt_ref[:, keys] if seq <= key_tile else k_ref[keys, :].T[0:dim], ds)

        if last <= key_tile:
            dq = visit(pl.ds(free, last - free), free)
            if free:
                dq = dq + visit(pl.ds(0, free), None)
        else:

            def tile(t, dq):
                first = pl.multiple_of(t * loop_tile, loop_tile)
                return dq + visit(pl.ds(first, loop_tile), first)

            tiles = min(-(-last // loop_tile), seq // loop_tile)
            dq = lax.fori_loop(0, tiles, tile, jnp.zeros((dim, wide), f32))
        scale = scale + jnp.sum(dq * qt[0:dim].astype(f32), axis=1, keepdims=True)
        dq = (dq * factor_ref[...]).astype(bf16)
        for s in range(2):
            at, which = place(inverse_ref, (2 * i + s) * stride + offset)
            d_ref[at, base + (which if q_parts == 2 else 0)] = dq[:, s * piece : (s + 1) * piece]

    def give(p):
        at, which = place(inverse_ref, p)
        span = pl.ds(p * piece if isinstance(p, int) else pl.multiple_of(p * piece, piece), piece)
        d_ref[at, base + q_parts + which] = dk_ref[span, :].T[0:dim].astype(bf16)
        d_ref[at, base + q_parts + 2 + which] = dv_ref[span, :].T[0:dim].astype(bf16)

    loop(pieces, give)
    return scale


def total_of(blocks):
    if len(blocks) == 1:
        return blocks[0]
    return sum(b.astype(f32) for b in blocks[1:]) + blocks[0].astype(f32)


def collect(plan, even, got_ref, b, which, kind):
    size, heads, group, members, dim, piece, batches = plan
    base = got_ref.shape[1] // 2 + 1
    parts = []
    for h in range(heads):
        if b < batches - 1:
            blocks = [got_ref[h * group + b * members + u, 2 * kind + which] for u in range(members)]
        elif kind == 0:
            parity = even if which == 0 else 1 - even
            blocks = [got_ref[h * group + 2 * u + parity, base] for u in range(group // 2)]
        else:
            blocks = [got_ref[h * group + e, base + 2 * kind - 1 + which] for e in range(group)]
        parts.append(total_of(blocks).astype(bf16))
    return jnp.concatenate(parts, axis=0)


def give_rows(value, held_ref, out_refs):
    batches, rows, _ = out_refs[0].shape
    held_ref[...] = value.astype(bf16).reshape(held_ref.shape)
    for k, out_ref in enumerate(out_refs):
        for b in range(batches):
            out_ref[b] = held_ref[b, chunk(k, rows), :]


def flat(ref):
    return ref[...].reshape(-1, ref.shape[-1])


def rows_kernel(plan, sc, got_ref, *refs):
    piece, batches = plan[5], plan[6]
    *out_refs, held_ref = refs
    rows = out_refs[0].shape[1]
    even = first_parity(sc)
    for b in range(batches):
        for s in range(2):
            held_ref[b, s * piece : (s + 1) * piece] = collect(plan, even, got_ref, b, s, 0).T
        for k, out_ref in enumerate(out_refs):
            out_ref[b] = held_ref[b, chunk(k, rows), :]


def copy_kernel(sc, *refs):
    count = len(refs) // 2
    for source, target in zip(refs[:count], refs[count:]):
        target[...] = source[...]


def middle_kernel(spread, sc, *refs):
    o_refs, wo, wi, wd, bias_refs = [refs[i * spread : (i + 1) * spread] for i in range(5)]
    refs = refs[5 * spread :]
    x_ref, g_ref, gain_ref, out_bias_ref, out_ref, grad_ref, n2_ref, dy_ref, sums_ref, du_sum_ref = refs[:10]
    hidden_refs, do_refs = [refs[10 + i * spread : 10 + (i + 1) * spread] for i in range(2)]
    kind = out_ref.shape
    h1 = flat(x_ref).astype(f32) + out_bias_ref[0:1]
    for k in range(spread):
        h1 = h1 + mm(flat(o_refs[k]), wo[k][...])
    r2 = lax.rsqrt(jnp.mean(h1 * h1, axis=-1, keepdims=True) + epsilon)
    n2 = (h1 * r2 * gain_ref[1:2]).astype(bf16)
    n2_ref[...] = n2.reshape(kind)
    g = flat(g_ref)
    out = h1 + out_bias_ref[1:2]
    dn2 = 0.0
    for k in range(spread):
        u = mm(n2, wi[k][...], cols_cols) + bias_refs[k][...]
        gate = 1.0 / (1.0 + jnp.exp(-u))
        a = (u * gate).astype(bf16)
        out = out + mm(a, wd[k][...])
        ga = mm(g, wd[k][...], cols_cols)
        du = (ga * gate * (1.0 + u * (1.0 - gate))).astype(bf16)
        dn2 = dn2 + mm(du, wi[k][...])
        hidden_refs[k][0] = a
        hidden_refs[k][1] = du
        du_sum_ref[pl.ds(k ^ lax.axis_index("fsdp"), 1), :] = jnp.sum(du.astype(f32), axis=0, keepdims=True)
    out_ref[...] = out.astype(bf16).reshape(kind)
    z2 = gain_ref[1:2] * dn2
    g = g.astype(f32)
    grad = g + r2 * z2 - h1 * (r2 * r2 * r2 * jnp.mean(z2 * h1, axis=-1, keepdims=True))
    grad_ref[...] = grad.reshape(kind)
    dy = grad.astype(bf16)
    dy_ref[...] = dy.reshape(kind)
    sums_ref[0:1] = jnp.sum(dn2 * h1 * r2, axis=0, keepdims=True)
    sums_ref[1:2] = jnp.sum(grad, axis=0, keepdims=True)
    sums_ref[2:3] = jnp.sum(g, axis=0, keepdims=True)
    for k in range(spread):
        do_refs[k][...] = mm(dy, wo[k][...], cols_cols).astype(bf16).reshape(do_refs[k].shape)


def cut_rows(value, out_ref, kind):
    chunks, _, rows, _ = out_ref.shape
    for c in range(chunks):
        out_ref[c, kind] = value[c * rows : (c + 1) * rows].astype(bf16)


def grads_kernel(spread, sums, sc, *refs):
    o_refs, hidden_refs, dy_refs, n2_refs, g_refs = [refs[i * spread : (i + 1) * spread] for i in range(5)]
    *out_refs, cut_ref = refs[5 * spread :]
    stack = lambda parts: jnp.concatenate([p[...].reshape(-1, p.shape[-1]) for p in parts])
    target = cut_ref if sums else out_refs[0]
    cut_rows(mm(stack([h.at[0] for h in hidden_refs]), stack(g_refs), rows_rows), target, 2)
    cut_rows(mm(stack([h.at[1] for h in hidden_refs]), stack(n2_refs), rows_rows), target, 1)
    cut_rows(mm(stack(o_refs), stack(dy_refs), rows_rows), target, 0)
    if sums:
        deal_cuts(sums, cut_ref, out_refs)


def deal_cuts(sums, cut_ref, out_refs):
    half = len(out_refs) // 2
    lanes = sums.block[2]
    read = lambda stream, index: cut_ref[index, :, :, stream * lanes : (stream + 1) * lanes]
    sums.deal(read, out_refs[:half], out_refs[half:], 0)


def close_kernel(terms, sc, *refs):
    part_refs, (x_ref, grad_ref, gain_ref, out_ref) = refs[:terms], refs[terms:]
    dn1 = sum(flat(p).astype(f32) for p in part_refs)
    x = flat(x_ref).astype(f32)
    r1 = lax.rsqrt(jnp.mean(x * x, axis=-1, keepdims=True) + epsilon)
    z1 = gain_ref[0:1] * dn1
    out = flat(grad_ref) + r1 * z1 - x * (r1 * r1 * r1 * jnp.mean(z1 * x, axis=-1, keepdims=True))
    out_ref[...] = out.astype(bf16).reshape(out_ref.shape)


def ahead_kernel(plan, spread, sc, *refs):
    do_refs, (send_ref, held_ref) = refs[:spread], refs[spread:]
    rows = do_refs[0].shape[1]
    parity = first_parity(sc)
    for b in range(plan[6]):
        for k in range(spread):
            held_ref[b, chunk(k, rows), :] = do_refs[k][b]
        store_parts(plan, parity, held_ref[b].T, send_ref, b, 0)


def back_kernel(plan, spread, sums, sc, got_ref, w_ref, n1_ref, gain_ref, small_ref, out_small_ref, *refs):
    size, heads, group, members, dim, piece, batches = plan
    part_refs, refs = refs[:spread], refs[spread:]
    *out_refs, held_ref, turned_ref, cut_ref = refs
    local = heads * dim
    even = first_parity(sc)
    out_small_ref[...] = small_ref[...]
    total = 0.0
    bias = []
    n1 = flat(n1_ref)
    target = cut_ref if sums else out_refs[0]
    for kind in range(3):
        for b in range(batches):
            for s in range(2):
                at = (2 * b + s) * piece
                turned_ref[:, at : at + piece] = collect(plan, even, got_ref, b, s, kind)
        turned_rows = turned_ref[...]
        rows = turned_rows.T
        if kind != 1:
            bias.append(jnp.sum(rows.astype(f32), axis=0, keepdims=True))
        total = total + mm(rows, w_ref[kind])
        cut_rows(mm(turned_rows, n1), target, kind)
    give_rows(total, held_ref, part_refs)
    out_small_ref[0:1] = jnp.sum(total * n1.astype(f32), axis=0, keepdims=True) / gain_ref[...]
    slots = spread // 2
    for f in range(spread):

        @pl.when(lax.axis_index("fsdp") == f)
        def _():
            for i in range(2):
                first = (f % slots) * 2 * local + i * local
                out_small_ref[5 + f // slots : 6 + f // slots, first : first + local] = bias[i]

    if sums:
        deal_cuts(sums, cut_ref, out_refs)


def shards(
    layer_input, output_cotangent, qkv_weight, out_weight, in_weight, down_weight, qv_bias, in_bias,
    out_bias, norm_gains, query_scale, block_table, block_marks,
):
    batches, own, width = layer_input.shape
    local = qkv_weight.shape[2]
    dim = query_scale.shape[0]
    heads = local // dim
    size = lax.axis_size("context")
    spread = lax.axis_size("fsdp")
    pieces = block_table.shape[0] * 2
    seq = block_marks.shape[1]
    piece = seq // pieces
    group = size // heads
    members = group // (batches - 1)
    plan = (size, heads, group, members, dim, piece, batches)
    rows = own * spread
    me = lax.axis_index("context")
    member = me % group
    scalars = block_table.T
    here = jnp.arange(1, seq + 1, dtype=jnp.int32)
    closing = jnp.concatenate([block_marks[:, 1:] != block_marks[:, :-1], jnp.ones((batches, 1), bool)], axis=1)
    ends = lax.cummin(jnp.where(closing, here, seq), axis=1, reverse=True)
    main_end = lax.dynamic_index_in_dim(ends, member // members, 0, keepdims=False)
    main_end = main_end.reshape(-1, members, piece)
    main_end = lax.dynamic_index_in_dim(main_end, member % members, 1, keepdims=False).reshape(1, -1)
    last_end = ends[batches - 1].reshape(-1, group, piece)
    last_end = lax.dynamic_index_in_dim(last_end, member, 1, keepdims=False).reshape(1, -1)
    factor = base_rate / math.sqrt(dim) * jax.nn.softplus(query_scale)
    factor_row = jnp.tile(factor, heads).reshape(1, local)
    factor_col = factor.reshape(dim, 1)
    gain_one, gain_two = norm_gains[0:1], norm_gains[1:2]

    tokens = batches * rows
    weight_flops = 2 * tokens * width * local
    qkv_turned = jnp.swapaxes(qkv_weight, 1, 2)
    in_turned = in_weight.T
    whole = shape((batches, rows, width), bf16)
    narrow = shape((batches, rows, local), bf16)
    parts = [shape((batches, own, width), bf16)] * spread
    thin_parts = [shape((batches, own, local), bf16)] * spread
    held = [pltpu.VMEM((batches, rows, width), bf16)]
    thin_held = [pltpu.VMEM((batches, rows, local), bf16)]
    asked = [pieces // members * piece, pieces // group * piece]
    mine = batches * own

    x_parts = gather_rows(layer_input, "fsdp", spread)
    n1, send = call(
        functools.partial(project_kernel, plan, spread),
        [whole, shape((size, 11, dim, piece), bf16)],
        [*x_parts, qkv_turned, gain_one, qv_bias, factor_row],
        scalars,
        tokens=[main_end, last_end],
    )
    got = swap_all(send, "context")
    plans = [(pieces, piece, dim, members, 2, 0, 0), (pieces, piece, dim, group, 1, 6, 2)]
    o_send, main_wide, main_lse, last_wide, last_lse = call(
        functools.partial(attend_kernel, plans),
        [shape((size, 3, dim, piece), bf16)] + [shape((r, a), f32) for a in asked for r in (dim, 1)],
        [got, main_end, last_end],
        scalars,
        [
            pltpu.SMEM((pieces,), jnp.int32), pltpu.VMEM((seq, 128), bf16), pltpu.VMEM((dim, seq), bf16),
            pltpu.VMEM((128, asked[0]), bf16),
        ],
    )
    others = [out_weight, in_turned, down_weight, in_bias.reshape(1, local), output_cotangent]
    others = call(copy_kernel, [shape(v.shape, v.dtype) for v in others], others, scalars, tokens=[send])
    *others, g_copy = others
    others = [gather_rows(v, "fsdp", spread, o_send) for v in others]
    g_first = exchange(g_copy, "fsdp", spread, bits_of(spread) - 1)
    o_parts = call(
        functools.partial(rows_kernel, plan), thin_parts, [swap_all(o_send, "context")], scalars, thin_held,
        tokens=[g_first],
    )
    g_parts = spread_rows(g_copy, g_first, "fsdp", spread, o_parts[0])
    o_local, o_parts = o_parts, swap_parts(o_parts, "fsdp", spread)
    even_cuts = local % (8 * size) == 0
    cuts = size if even_cuts else 1
    cut_shape = shape((cuts, 3, local // cuts, width), bf16)
    own_kind = shape((batches, own, width), bf16)
    layer_output, grad_one, n2, dy, sums, du_sum, *rest = call(
        functools.partial(middle_kernel, spread),
        [own_kind, shape((batches, own, width), f32), own_kind, own_kind, shape((3, width), f32), shape((spread, local), f32)]
        + [shape((2, mine, local), bf16)] * spread
        + thin_parts,
        [*o_parts, *others[0], *others[1], *others[2], *others[3], layer_input, output_cotangent, norm_gains, out_bias],
        scalars,
    )
    hidden_parts, do_parts = rest[:spread], swap_parts(rest[spread:], "fsdp", spread)
    (do_send,) = call(
        functools.partial(ahead_kernel, plan, spread),
        [shape((size, 3, dim, piece), bf16)],
        do_parts,
        scalars,
        thin_held,
    )
    do_got = swap_all(do_send, "context")
    hidden_parts = swap_parts(hidden_parts, "fsdp", spread)
    n2_first = exchange(n2, "fsdp", spread, bits_of(spread) - 1)
    dy_first = exchange(dy, "fsdp", spread, bits_of(spread) - 1)
    d_send, scale_sum = call(
        functools.partial(attend_back_kernel, plans),
        [shape((size, 11, dim, piece), bf16), shape((dim, 1), f32)],
        [got, do_got, factor_col, main_end, main_wide, main_lse, last_end, last_wide, last_lse],
        scalars,
        [
            pltpu.SMEM((pieces,), jnp.int32),
            pltpu.VMEM((seq, 128), bf16), pltpu.VMEM((dim, min(seq, key_tile)), bf16), pltpu.VMEM((seq, 128), bf16),
            pltpu.VMEM((128, asked[0]), bf16), pltpu.VMEM((asked[0], 128), bf16),
            pltpu.VMEM((128, asked[0]), bf16), pltpu.VMEM((asked[0], 128), bf16),
            pltpu.VMEM((seq, 128), f32), pltpu.VMEM((seq, 128), f32),
        ],
    )
    n2_parts = spread_rows(n2, n2_first, "fsdp", spread, scale_sum)
    dy_parts = spread_rows(dy, dy_first, "fsdp", spread, scale_sum)
    new_sums = lambda: Sums(size, 3, local // size, width // 2) if even_cuts else None
    early, last = new_sums(), new_sums()
    dealt = early.shapes(0) * 2 if even_cuts else [cut_shape]
    cut_scratch = [pltpu.VMEM(cut_shape.shape, bf16)]
    early_made = call(
        functools.partial(grads_kernel, spread, early),
        dealt,
        [*o_local, *hidden_parts, *dy_parts, *n2_parts, *g_parts],
        scalars,
        cut_scratch,
        tokens=[scale_sum],
    )
    d_got = swap_all(after(d_send, hidden_parts[1:], n2_first), "context")
    small = [jnp.zeros((1, width), f32), sums, du_sum.reshape(1, width), jnp.zeros((2, width), f32)]
    small.append(jnp.pad(scale_sum.reshape(1, dim) / factor, ((0, 0), (0, width - dim))))
    small = jnp.concatenate(small)
    if even_cuts:
        early.start(early_made[: len(early_made) // 2], early_made[len(early_made) // 2 :])
        for _ in range(ahead_rounds):
            early.fold(scalars)
    small, *made = call(
        functools.partial(back_kernel, plan, spread, last),
        [shape(small.shape, f32)] + parts + dealt,
        [d_got, qkv_turned, n1, gain_one, small],
        scalars,
        held + [pltpu.VMEM((local, tokens), bf16)] + cut_scratch,
        tokens=[early.token] if even_cuts and ahead_rounds else [],
    )
    part, made = made[:spread], made[spread:]
    steps = [("fsdp", spread, bit) for bit in range(bits_of(spread))]
    steps += [("context", size, bit) for bit in range(bits_of(size))]
    dn1_terms, _ = scatter_parts(part, "fsdp", spread)

    def close(*tokens):
        return call(
            functools.partial(close_kernel, len(dn1_terms)),
            [own_kind],
            [*dn1_terms, layer_input, grad_one, norm_gains],
            scalars,
            tokens=tokens,
        )[0]

    qkv_kind = shape((3, local, width), f32)
    if even_cuts:
        last.start(made[: len(made) // 2], made[len(made) // 2 :])
        order = ["early"] * (2 - ahead_rounds) + ["last", "early"] * (2 * early.bits - 2) + ["last"] * 2
        order = [early if name == "early" else last for name in order]
        ends = {early: [shape((local, width), f32)] * 3, last: [qkv_kind]}
        adds = (1, 2, 4, 6, 8)
        seen, pending, done = small, None, 0
        for index, flow in enumerate(order):
            if pending is None and done < len(steps):
                pending = exchange(small, *steps[done])
            extra = [(small, pending)] if pending is not None and index in adds else []
            finals = ends[flow] if flow.step == 2 * flow.bits - 1 else []
            added = flow.fold(scalars, finals, extra, [seen])
            seen = flow.token
            if extra:
                small, pending, done = added[0], None, done + 1
            if index == 4:
                input_grad = close(seen)
                seen = input_grad
        if pending is not None:
            small, done = small + pending, done + 1
        steps = steps[done:]
        for axis, count, bit in steps:
            small = small + exchange(small, axis, count, bit)
        (qkv,) = last.result
        out_grad, *feed_grads = early.result
    else:
        for axis, count, bit in steps:
            small = small + exchange(small, axis, count, bit)
        input_grad = close()
        whole_sum = lambda v: lax.psum(v, "context").astype(f32).reshape(3, local, width)
        qkv = whole_sum(made[0])
        out_grad, *feed_grads = whole_sum(early_made[0])
    gains_grad = small[0:2]
    out_bias_grad = small[2:4]
    own_slot = lambda v: lax.dynamic_index_in_dim(v.reshape(spread, -1), lax.axis_index("fsdp"), 0, keepdims=False)
    in_bias_grad = own_slot(small[4])
    qv_grad = own_slot(small[5:7]).reshape(2, local)
    scale_grad = small[7, :dim] * (base_rate / math.sqrt(dim)) * jax.nn.sigmoid(query_scale)
    return (
        layer_output,
        input_grad,
        jnp.swapaxes(qkv, 1, 2),
        out_grad,
        feed_grads[0].T,
        feed_grads[1],
        qv_grad,
        in_bias_grad,
        out_bias_grad,
        gains_grad,
        scale_grad,
    )


def solution(mesh):
    in_specs = (
        P(None, ("context", "fsdp"), None),
        P(None, ("context", "fsdp"), None),
        P(None, None, "fsdp"),
        P("fsdp", None),
        P(None, "fsdp"),
        P("fsdp", None),
        P(None, "fsdp"),
        P("fsdp"),
        P(),
        P(),
        P(),
        P(),
        P(),
    )
    out_specs = (
        P(None, ("context", "fsdp"), None),
        P(None, ("context", "fsdp"), None),
        P(None, None, "fsdp"),
        P("fsdp", None),
        P(None, "fsdp"),
        P("fsdp", None),
        P(None, "fsdp"),
        P("fsdp"),
        P(),
        P(),
        P(),
    )
    return jax.shard_map(shards, mesh=mesh, in_specs=in_specs, out_specs=out_specs, check_vma=False)
```

```python
import functools
import math

import jax
import jax.numpy as jnp
from jax import lax
from jax.experimental import pallas as pl
from jax.experimental.pallas import tpu as pltpu
from jax.sharding import PartitionSpec as P

epsilon = 1e-06
negative = -1e30
base_rate = 1.442695041
key_tile = 2048
vmem_bytes = 60 * 1024 * 1024
loop_tile = 1024
spare_bytes = 36 * 1024 * 1024
kernel_us = {
    "project_kernel": 7, "attend_kernel": 11, "middle_kernel": 14, "attend_back_kernel": 15, "grads_kernel": 7, "back_kernel": 11,
}
lead = 3
ahead_rounds = 1
flops_per_us = 1153500000
bf16 = jnp.bfloat16
f32 = jnp.float32

rows_cols = (((1,), (0,)), ((), ()))
cols_cols = (((1,), (1,)), ((), ()))
rows_rows = (((0,), (0,)), ((), ()))


def mm(left, right, dims=rows_cols):
    return lax.dot_general(left, right, dims, preferred_element_type=f32)


def padded_bytes(value):
    *rest, last = value.shape
    return math.prod(rest) * -(-last // 128) * 128 * jnp.dtype(value.dtype).itemsize


def call(kernel, out_shape, operands, scalars, scratch=(), tokens=(), weight=1):
    specs = [pl.BlockSpec(memory_space=pltpu.SMEM)]
    specs += [pl.BlockSpec(memory_space=pltpu.VMEM)] * len(operands)
    specs += [pl.BlockSpec(memory_space=pl.ANY)] * len(tokens)
    used = 1 + len(operands)
    room = spare_bytes + 2 * sum(padded_bytes(v) for v in [*operands, *out_shape, *scratch])
    weight = kernel_us.get(getattr(kernel, "func", kernel).__name__, weight)
    return pl.pallas_call(
        lambda *refs: kernel(*refs[:used], *refs[used + len(tokens) :]),
        out_shape=tuple(out_shape),
        in_specs=specs,
        out_specs=tuple(pl.BlockSpec(memory_space=pltpu.VMEM) for _ in out_shape),
        scratch_shapes=list(scratch),
        compiler_params=pltpu.CompilerParams(vmem_limit_bytes=min(vmem_bytes, room)),
        cost_estimate=pl.CostEstimate(flops=int(weight * flops_per_us), bytes_accessed=0, transcendentals=0),
    )(scalars, *operands, *tokens)


def loop(count, body):
    if count <= 16:
        for i in range(count):
            body(i)
    else:
        lax.fori_loop(0, count, lambda i, c: (body(i), c)[1], 0)


def shape(dims, kind):
    return jax.ShapeDtypeStruct(tuple(dims), kind)


def exchange(values, axis, size, bit):
    return lax.ppermute(values, axis, [(i, i ^ (1 << bit)) for i in range(size)])


def bits_of(size):
    return size.bit_length() - 1


def after(values, *tokens):
    leaves, tree = jax.tree.flatten(values)
    marks = jax.tree.leaves(tokens)
    anywhere = pl.BlockSpec(memory_space=pl.ANY)
    kept = pl.pallas_call(
        lambda *refs: None,
        out_shape=tuple(shape(v.shape, v.dtype) for v in leaves),
        in_specs=[anywhere] * (len(leaves) + len(marks)),
        out_specs=tuple(anywhere for _ in leaves),
        input_output_aliases={i: i for i in range(len(leaves))},
        cost_estimate=pl.CostEstimate(flops=0, bytes_accessed=0, transcendentals=0),
    )(*leaves, *marks)
    return jax.tree.unflatten(tree, kept)


def gather_rows(own, axis, size, token=None):
    held = {0: own}
    for bit in reversed(range(bits_of(size))):
        if token is not None:
            held = {k: after(v, token) if k else v for k, v in held.items()}
        held.update({k | (1 << bit): exchange(v, axis, size, bit) for k, v in list(held.items())})
    return [held[k] for k in range(size)]


def spread_rows(own, first, axis, size, token):
    top = bits_of(size) - 1
    held = {0: own}
    for bit in reversed(range(top)):
        held.update({k | (1 << bit): exchange(v, axis, size, bit) for k, v in list(held.items())})
    held[1 << top] = after(first, token)
    for bit in reversed(range(top)):
        more = [k for k in held if k >> top and not k & ((1 << (bit + 1)) - 1)]
        held.update({k | (1 << bit): exchange(held[k], axis, size, bit) for k in more})
    return [held[k] for k in range(size)]


def scatter_parts(parts, axis, size):
    held = {k: [v] for k, v in enumerate(parts)}
    sent = parts[0]
    for bit in range(bits_of(size)):
        step = 1 << bit
        for k in reversed([k for k in held if k & step]):
            terms = held.pop(k)
            if len(terms) > 1:
                terms = [sum(t.astype(f32) for t in terms).astype(bf16)]
            sent = terms[0]
            held[k ^ step].append(exchange(sent, axis, size, bit))
    return held[0], sent


def swap_parts(parts, axis, size):
    return [parts[0]] + [lax.ppermute(parts[k], axis, [(i, i ^ k) for i in range(size)]) for k in range(1, size)]


def swap_all(parts, axis):
    return lax.all_to_all(parts, axis, 0, 0, tiled=True)


def with_bit(index, place, bit):
    low = index & ((1 << place) - 1)
    return low | (bit << place) | ((index >> place) << (place + 1))


class Sums:
    def __init__(self, size, kinds, rows, lanes, tail=0):
        self.size, self.bits = size, bits_of(size)
        self.kinds, self.rows, self.tail = kinds, rows, tail
        self.block = (1, kinds * rows + tail, lanes) if tail else (kinds, rows, lanes)
        first = list(range(self.bits))
        second = first[:]
        if self.bits > 1:
            second[0], second[1] = 1, 0
        self.orders = [first, second]
        self.step, self.result = 0, None

    def bit(self, stream, step):
        return self.orders[stream][step if step < self.bits else 2 * self.bits - 1 - step]

    def left(self, stream, step):
        order = self.orders[stream]
        return sorted(order[step + 1 :] if step < self.bits else order[2 * self.bits - step :])

    def groups(self, step):
        found = {}
        for stream in range(2):
            found.setdefault(self.bit(stream, step), []).append(stream)
        return [(bit, streams, 1 << len(self.left(streams[0], step))) for bit, streams in found.items()]

    def shapes(self, step):
        return [shape((len(streams) * count,) + self.block, bf16) for _, streams, count in self.groups(step)]

    def at(self, refs, stream, step, index):
        for ref, (_, streams, count) in zip(refs, self.groups(step)):
            if stream in streams:
                return ref.at[streams.index(stream) * count + index]

    def deal(self, read, send_refs, keep_refs, step):
        me = lax.axis_index("context")
        for stream in range(2):
            bit, left = self.bit(stream, step), self.left(stream, step)
            place = sorted(left + [bit]).index(bit)
            mine = (me >> bit) & 1
            for j in range(1 << len(left)):
                self.at(send_refs, stream, step, j)[...] = read(stream, with_bit(j, place, 1 - mine)).astype(bf16)
                self.at(keep_refs, stream, step, j)[...] = read(stream, with_bit(j, place, mine)).astype(bf16)

    def start(self, send, keep):
        self.keep = keep
        self.got = [exchange(v, "context", self.size, bit) for v, (bit, _, _) in zip(send, self.groups(self.step))]

    def fold(self, scalars, finals=(), tokens=(), group=None):
        step, last = self.step, self.step == 2 * self.bits - 1
        halving = step + 1 < self.bits
        summed = self.tail and step + 1 == self.bits
        outs = list(finals) if last else self.shapes(step + 1) * (2 if halving else 1)
        count, width = len(self.keep), len(outs)
        lanes = self.block[2]

        def kernel(sc, *refs):
            keep, got = refs[:count], refs[count : 2 * count]
            out = refs[2 * count :]

            def total(stream, index):
                return self.at(keep, stream, step, index)[...].astype(f32) + self.at(got, stream, step, index)[...].astype(f32)

            if halving:
                half = len(outs) // 2
                self.deal(total, out[:half], out[half:width], step + 1)
                return
            me = lax.axis_index("context")
            for stream in range(2):
                if step < self.bits:
                    value = total(stream, 0)
                    self.at(out, stream, step + 1, 0)[...] = value.astype(bf16)
                    if summed:
                        out[width][:, stream * lanes : (stream + 1) * lanes] = value[0, -self.tail :]
                    continue
                bit, left = self.bit(stream, step), self.left(stream, step)
                place = sorted(left + [bit]).index(bit)
                mine = (me >> bit) & 1
                for j in range(1 << len(left)):
                    for refs_in, side in ((keep, mine), (got, 1 - mine)):
                        value = self.at(refs_in, stream, step, j)[...]
                        index = with_bit(j, place, side)
                        if not last:
                            self.at(out, stream, step + 1, index)[...] = value
                            continue
                        kinds, rows = self.kinds, self.rows
                        span = pl.ds(pl.multiple_of(index * rows, rows), rows)
                        value = value.astype(f32)
                        for kind in range(kinds):
                            to = out[kind] if width > 1 else out[0].at[kind]
                            part = value[0, kind * rows : (kind + 1) * rows] if self.tail else value[kind]
                            to[span, stream * lanes : (stream + 1) * lanes] = part

        if summed:
            outs = outs + [shape((self.tail, 2 * lanes), f32)]
        operands = [*self.keep, *self.got]
        made = list(call(kernel, outs, operands, scalars, tokens=tokens, weight=8))
        self.step += 1
        self.token = made[0]
        if last:
            self.result = made[:width]
        elif halving:
            self.start(made[: width // 2], made[width // 2 : width])
        else:
            self.start(made[:width], made[:width])
        return made[width] if summed else None


def chunk(k, rows):
    return pl.ds(pl.multiple_of((k ^ lax.axis_index("fsdp")) * rows, rows), rows)


def first_parity(table):
    return lax.rem(table[0, lax.axis_index("context")], 2)


def invert(table, inverse_ref):
    def note(i):
        half = i % 2 if isinstance(i, int) else lax.rem(i, 2)
        inverse_ref[table[half, i // 2]] = i

    loop(2 * table.shape[1], note)


def store_parts(plan, parity, t, out_ref, b, kind):
    size, heads, group, members, dim, piece, batches = plan
    for h in range(heads):
        block = t[h * dim : (h + 1) * dim]
        cut = [block[:, s * piece : (s + 1) * piece] for s in range(2)]
        if b < batches - 1:
            for u in range(members):
                for s in range(2):
                    out_ref[h * group + b * members + u, 2 * kind + s] = cut[s]
        else:
            base = out_ref.shape[1] // 2 + 1
            for e in range(group):
                if kind == 0:
                    out_ref[h * group + e, base] = jnp.where(parity == e % 2, cut[0], cut[1])
                else:
                    for s in range(2):
                        out_ref[h * group + e, base + 2 * kind - 1 + s] = cut[s]


def project_kernel(plan, spread, sc, *refs):
    x_refs, (w_ref, gain_ref, bias_ref, factor_ref, n1_ref, send_ref) = refs[:spread], refs[spread:]
    batches = plan[6]
    rows = x_refs[0].shape[1]
    parity = first_parity(sc)
    for b in range(batches):
        for k in range(spread):
            x = x_refs[k][b].astype(f32)
            r = lax.rsqrt(jnp.mean(x * x, axis=-1, keepdims=True) + epsilon)
            n1_ref[b, chunk(k, rows), :] = (x * r * gain_ref[...]).astype(bf16)
    n1 = n1_ref[...].reshape(-1, n1_ref.shape[2])
    for i in range(3):
        y = mm(w_ref[i], n1, cols_cols)
        if i == 0:
            y = (y + bias_ref[:, 0:1]) * factor_ref[...]
        elif i == 2:
            y = y + bias_ref[:, 1:2]
        y = y.astype(bf16)
        for b in range(batches):
            store_parts(plan, parity, y[:, b * spread * rows : (b + 1) * spread * rows], send_ref, b, i)


def place(inverse_ref, index):
    slot = inverse_ref[index]
    return slot // 2, lax.rem(slot, 2)


def turned(block):
    filled = jnp.concatenate([block, jnp.zeros((128 - block.shape[0], block.shape[1]), block.dtype)], 0)
    return filled.T


def key_parts(block_index, stride, piece, seq):
    free = 2 * block_index * stride * piece
    last = min(((2 * block_index + 2) * stride + 2) * piece, seq)
    return free, last


def attend_kernel(plans, sc, got_ref, *refs):
    units = len(plans)
    ends, o_ref, outs, scratch = refs[:units], refs[units], refs[units + 1 : -4], refs[-4:]
    invert(sc, scratch[0])
    for i, plan in enumerate(plans):
        attend_unit(plan, got_ref, ends[i], o_ref, outs[2 * i], outs[2 * i + 1], *scratch)


def attend_unit(plan, got_ref, end_ref, o_ref, wide_ref, lse_ref, inverse_ref, k_ref, vt_ref, qt_ref):
    pieces, piece, dim, stride, q_parts, base, o_base = plan
    offset = lax.rem(lax.axis_index("context"), stride)
    seq = pieces * piece
    asked = pieces // stride

    def fill(p):
        at, which = place(inverse_ref, p)
        span = pl.ds(p * piece if isinstance(p, int) else pl.multiple_of(p * piece, piece), piece)
        k_ref[span, :] = turned(got_ref[at, base + q_parts + which])
        vt_ref[:, span] = got_ref[at, base + q_parts + 2 + which]

    loop(pieces, fill)
    for j in range(asked):
        at, which = place(inverse_ref, j * stride + offset)
        qt_ref[0:dim, j * piece : (j + 1) * piece] = got_ref[at, base + (which if q_parts == 2 else 0)]
    qt_ref[dim:, :] = jnp.zeros_like(qt_ref[dim:, :])
    if asked != o_ref.shape[0] * q_parts:
        for part in range(q_parts):
            o_ref[:, o_base + part] = jnp.zeros_like(o_ref[:, o_base + part])
    wide = 2 * piece
    for i in range(asked // 2):
        span = slice(i * wide, (i + 1) * wide)
        qt = qt_ref[:, span]
        end = end_ref[:, span]
        free, last = key_parts(i, stride, piece, seq)
        if last <= key_tile:
            masked = mm(k_ref[free:last, :], qt)
            at = lax.broadcasted_iota(jnp.int32, masked.shape, 0) + free
            masked = jnp.where(at < end, masked, negative)
            top = jnp.max(masked, axis=0, keepdims=True)
            if free:
                plain = mm(k_ref[0:free, :], qt)
                top = jnp.maximum(top, jnp.max(plain, axis=0, keepdims=True))
            weight = jnp.exp(masked - top)
            total = jnp.sum(weight, axis=0, keepdims=True)
            out = mm(vt_ref[:, free:last], weight.astype(bf16))
            if free:
                weight = jnp.exp(plain - top)
                total = total + jnp.sum(weight, axis=0, keepdims=True)
                out = out + mm(vt_ref[:, 0:free], weight.astype(bf16))
        else:

            def tile(t, carry):
                top, total, out = carry
                first = pl.multiple_of(t * loop_tile, loop_tile)
                scores = mm(k_ref[pl.ds(first, loop_tile), :], qt)
                at = lax.broadcasted_iota(jnp.int32, scores.shape, 0) + first
                scores = jnp.where(at < end, scores, negative)
                new = jnp.maximum(top, jnp.max(scores, axis=0, keepdims=True))
                weight = jnp.exp(scores - new)
                change = jnp.exp(top - new)
                total = total * change + jnp.sum(weight, axis=0, keepdims=True)
                out = out * change + mm(vt_ref[:, pl.ds(first, loop_tile)], weight.astype(bf16))
                return new, total, out

            start = (jnp.full((1, wide), negative, f32), jnp.zeros((1, wide), f32), jnp.zeros((dim, wide), f32))
            tiles = min(-(-last // loop_tile), seq // loop_tile)
            top, total, out = lax.fori_loop(0, tiles, tile, start)
        out = out / total
        wide_ref[:, span] = out
        lse_ref[:, span] = top + jnp.log(total)
        for s in range(2):
            at, which = place(inverse_ref, (2 * i + s) * stride + offset)
            o_ref[at, o_base + (which if q_parts == 2 else 0)] = out[:, s * piece : (s + 1) * piece].astype(bf16)


def attend_back_kernel(plans, sc, got_ref, do_ref, factor_ref, *refs):
    units = len(plans)
    saved, d_ref, scale_ref, scratch = refs[: 3 * units], refs[3 * units], refs[3 * units + 1], refs[3 * units + 2 :]
    scale = 0.0
    invert(sc, scratch[0])
    for i, plan in enumerate(plans):
        own = saved[3 * i : 3 * i + 3]
        scale = scale + attend_back_unit(plan, got_ref, do_ref, factor_ref, *own, d_ref, *scratch)
    scale_ref[...] = scale


def attend_back_unit(
    plan, got_ref, do_ref, factor_ref, end_ref, wide_ref, lse_ref, d_ref,
    inverse_ref, k_ref, kt_ref, v_ref, qt_ref, q_ref, dot_ref, dor_ref, dk_ref, dv_ref,
):
    pieces, piece, dim, stride, q_parts, base, o_base = plan
    offset = lax.rem(lax.axis_index("context"), stride)
    seq = pieces * piece
    asked = pieces // stride

    def fill(p):
        at, which = place(inverse_ref, p)
        span = pl.ds(p * piece if isinstance(p, int) else pl.multiple_of(p * piece, piece), piece)
        kt = got_ref[at, base + q_parts + which]
        if seq <= key_tile:
            kt_ref[:, span] = kt
        k_ref[span, :] = turned(kt)
        v_ref[span, :] = turned(got_ref[at, base + q_parts + 2 + which])

    loop(pieces, fill)
    for j in range(asked):
        at, which = place(inverse_ref, j * stride + offset)
        span = slice(j * piece, (j + 1) * piece)
        qt = got_ref[at, base + (which if q_parts == 2 else 0)]
        qt_ref[0:dim, span] = qt
        q_ref[span, :] = turned(qt)
        do = do_ref[at, o_base + (which if q_parts == 2 else 0)]
        dot_ref[0:dim, span] = do
        dor_ref[span, :] = turned(do)
    qt_ref[dim:, :] = jnp.zeros_like(qt_ref[dim:, :])
    dot_ref[dim:, :] = jnp.zeros_like(dot_ref[dim:, :])
    dk_ref[...] = jnp.zeros_like(dk_ref)
    dv_ref[...] = jnp.zeros_like(dv_ref)
    if asked != d_ref.shape[0] * q_parts:
        for part in range(q_parts):
            d_ref[:, base + part] = jnp.zeros_like(d_ref[:, base + part])
    wide = 2 * piece
    scale = jnp.zeros((dim, 1), f32)
    for i in range(asked // 2):
        span = slice(i * wide, (i + 1) * wide)
        qt, q, do, dor = qt_ref[:, span], q_ref[span, :], dot_ref[:, span], dor_ref[span, :]
        end, lse = end_ref[:, span], lse_ref[:, span]
        delta = jnp.sum(do[0:dim].astype(f32) * wide_ref[:, span], axis=0, keepdims=True)
        free, last = key_parts(i, stride, piece, seq)

        def visit(keys, masked_from):
            scores = mm(k_ref[keys, :], qt)
            if masked_from is not None:
                at = lax.broadcasted_iota(jnp.int32, scores.shape, 0) + masked_from
                scores = jnp.where(at < end, scores, negative)
            prob = jnp.exp(scores - lse)
            ds = (prob * (mm(v_ref[keys, :], do) - delta)).astype(bf16)
            dv_ref[keys, :] += mm(prob.astype(bf16), dor)
            dk_ref[keys, :] += mm(ds, q)
            return mm(kt_ref[:, keys] if seq <= key_tile else k_ref[keys, :].T[0:dim], ds)

        if last <= key_tile:
            dq = visit(pl.ds(free, last - free), free)
            if free:
                dq = dq + visit(pl.ds(0, free), None)
        else:

            def tile(t, dq):
                first = pl.multiple_of(t * loop_tile, loop_tile)
                return dq + visit(pl.ds(first, loop_tile), first)

            tiles = min(-(-last // loop_tile), seq // loop_tile)
            dq = lax.fori_loop(0, tiles, tile, jnp.zeros((dim, wide), f32))
        scale = scale + jnp.sum(dq * qt[0:dim].astype(f32), axis=1, keepdims=True)
        dq = (dq * factor_ref[...]).astype(bf16)
        for s in range(2):
            at, which = place(inverse_ref, (2 * i + s) * stride + offset)
            d_ref[at, base + (which if q_parts == 2 else 0)] = dq[:, s * piece : (s + 1) * piece]

    def give(p):
        at, which = place(inverse_ref, p)
        span = pl.ds(p * piece if isinstance(p, int) else pl.multiple_of(p * piece, piece), piece)
        d_ref[at, base + q_parts + which] = dk_ref[span, :].T[0:dim].astype(bf16)
        d_ref[at, base + q_parts + 2 + which] = dv_ref[span, :].T[0:dim].astype(bf16)

    loop(pieces, give)
    return scale


def total_of(blocks):
    if len(blocks) == 1:
        return blocks[0]
    return sum(b.astype(f32) for b in blocks[1:]) + blocks[0].astype(f32)


def collect(plan, even, got_ref, b, which, kind):
    size, heads, group, members, dim, piece, batches = plan
    base = got_ref.shape[1] // 2 + 1
    parts = []
    for h in range(heads):
        if b < batches - 1:
            blocks = [got_ref[h * group + b * members + u, 2 * kind + which] for u in range(members)]
        elif kind == 0:
            parity = even if which == 0 else 1 - even
            blocks = [got_ref[h * group + 2 * u + parity, base] for u in range(group // 2)]
        else:
            blocks = [got_ref[h * group + e, base + 2 * kind - 1 + which] for e in range(group)]
        parts.append(total_of(blocks).astype(bf16))
    return jnp.concatenate(parts, axis=0)


def give_rows(value, held_ref, out_refs):
    batches, rows, _ = out_refs[0].shape
    held_ref[...] = value.astype(bf16).reshape(held_ref.shape)
    for k, out_ref in enumerate(out_refs):
        for b in range(batches):
            out_ref[b] = held_ref[b, chunk(k, rows), :]


def flat(ref):
    return ref[...].reshape(-1, ref.shape[-1])


def rows_kernel(plan, sc, got_ref, *refs):
    piece, batches = plan[5], plan[6]
    *out_refs, held_ref = refs
    rows = out_refs[0].shape[1]
    even = first_parity(sc)
    for b in range(batches):
        for s in range(2):
            held_ref[b, s * piece : (s + 1) * piece] = collect(plan, even, got_ref, b, s, 0).T
        for k, out_ref in enumerate(out_refs):
            out_ref[b] = held_ref[b, chunk(k, rows), :]


def middle_kernel(spread, sc, *refs):
    o_refs, wo, wi, wd, bias_refs = [refs[i * spread : (i + 1) * spread] for i in range(5)]
    refs = refs[5 * spread :]
    x_ref, g_ref, gain_ref, out_bias_ref, out_ref, grad_ref, n2_ref, dy_ref, sums_ref, du_sum_ref = refs[:10]
    hidden_refs, do_refs = [refs[10 + i * spread : 10 + (i + 1) * spread] for i in range(2)]
    kind = out_ref.shape
    h1 = flat(x_ref).astype(f32) + out_bias_ref[0:1]
    for k in range(spread):
        h1 = h1 + mm(flat(o_refs[k]), wo[k][...])
    r2 = lax.rsqrt(jnp.mean(h1 * h1, axis=-1, keepdims=True) + epsilon)
    n2 = (h1 * r2 * gain_ref[1:2]).astype(bf16)
    n2_ref[...] = n2.reshape(kind)
    g = flat(g_ref)
    out = h1 + out_bias_ref[1:2]
    dn2 = 0.0
    for k in range(spread):
        u = mm(n2, wi[k][...], cols_cols) + bias_refs[k][...]
        gate = 1.0 / (1.0 + jnp.exp(-u))
        a = (u * gate).astype(bf16)
        out = out + mm(a, wd[k][...])
        ga = mm(g, wd[k][...], cols_cols)
        du = (ga * gate * (1.0 + u * (1.0 - gate))).astype(bf16)
        dn2 = dn2 + mm(du, wi[k][...])
        hidden_refs[k][0] = a
        hidden_refs[k][1] = du
        du_sum_ref[pl.ds(k ^ lax.axis_index("fsdp"), 1), :] = jnp.sum(du.astype(f32), axis=0, keepdims=True)
    out_ref[...] = out.astype(bf16).reshape(kind)
    z2 = gain_ref[1:2] * dn2
    g = g.astype(f32)
    grad = g + r2 * z2 - h1 * (r2 * r2 * r2 * jnp.mean(z2 * h1, axis=-1, keepdims=True))
    grad_ref[...] = grad.reshape(kind)
    dy = grad.astype(bf16)
    dy_ref[...] = dy.reshape(kind)
    sums_ref[0:1] = jnp.sum(dn2 * h1 * r2, axis=0, keepdims=True)
    sums_ref[1:2] = jnp.sum(grad, axis=0, keepdims=True)
    sums_ref[2:3] = jnp.sum(g, axis=0, keepdims=True)
    for k in range(spread):
        do_refs[k][...] = mm(dy, wo[k][...], cols_cols).astype(bf16).reshape(do_refs[k].shape)


def cut_rows(value, out_ref, kind):
    chunks = out_ref.shape[0]
    rows = value.shape[0] // chunks
    for c in range(chunks):
        part = value[c * rows : (c + 1) * rows]
        if out_ref.shape[1] == 1:
            out_ref[c, 0, kind * rows : (kind + 1) * rows] = part.astype(out_ref.dtype)
        else:
            out_ref[c, kind] = part.astype(out_ref.dtype)


def grads_kernel(spread, sums, sc, *refs):
    o_refs, hidden_refs, dy_refs, n2_refs, g_refs = [refs[i * spread : (i + 1) * spread] for i in range(5)]
    *out_refs, cut_ref = refs[5 * spread :]
    stack = lambda parts: jnp.concatenate([p[...].reshape(-1, p.shape[-1]) for p in parts])
    target = cut_ref if sums else out_refs[0]
    cut_rows(mm(stack([h.at[0] for h in hidden_refs]), stack(g_refs), rows_rows), target, 2)
    cut_rows(mm(stack([h.at[1] for h in hidden_refs]), stack(n2_refs), rows_rows), target, 1)
    cut_rows(mm(stack(o_refs), stack(dy_refs), rows_rows), target, 0)
    if sums:
        deal_cuts(sums, cut_ref, out_refs)


def deal_cuts(sums, cut_ref, out_refs):
    half = len(out_refs) // 2
    lanes = sums.block[2]
    read = lambda stream, index: cut_ref[index, :, :, stream * lanes : (stream + 1) * lanes]
    sums.deal(read, out_refs[:half], out_refs[half:], 0)


def close_kernel(terms, sc, *refs):
    part_refs, (x_ref, grad_ref, gain_ref, out_ref) = refs[:terms], refs[terms:]
    dn1 = sum(flat(p).astype(f32) for p in part_refs)
    x = flat(x_ref).astype(f32)
    r1 = lax.rsqrt(jnp.mean(x * x, axis=-1, keepdims=True) + epsilon)
    z1 = gain_ref[0:1] * dn1
    out = flat(grad_ref) + r1 * z1 - x * (r1 * r1 * r1 * jnp.mean(z1 * x, axis=-1, keepdims=True))
    out_ref[...] = out.astype(bf16).reshape(out_ref.shape)


def ahead_kernel(plan, spread, sc, *refs):
    do_refs, (send_ref, held_ref) = refs[:spread], refs[spread:]
    rows = do_refs[0].shape[1]
    parity = first_parity(sc)
    for b in range(plan[6]):
        for k in range(spread):
            held_ref[b, chunk(k, rows), :] = do_refs[k][b]
        store_parts(plan, parity, held_ref[b].T, send_ref, b, 0)


def back_kernel(plan, spread, sums, sc, got_ref, w_ref, n1_ref, gain_ref, small_ref, out_small_ref, *refs):
    size, heads, group, members, dim, piece, batches = plan
    part_refs, refs = refs[:spread], refs[spread:]
    *out_refs, held_ref, turned_ref, cut_ref = refs
    local = heads * dim
    even = first_parity(sc)
    out_small_ref[...] = small_ref[...]
    total = 0.0
    bias = []
    n1 = flat(n1_ref)
    target = cut_ref if sums else out_refs[0]
    for kind in range(3):
        for b in range(batches):
            for s in range(2):
                at = (2 * b + s) * piece
                turned_ref[:, at : at + piece] = collect(plan, even, got_ref, b, s, kind)
        turned_rows = turned_ref[...]
        rows = turned_rows.T
        if kind != 1:
            bias.append(jnp.sum(rows.astype(f32), axis=0, keepdims=True))
        total = total + mm(rows, w_ref[kind])
        cut_rows(mm(turned_rows, n1), target, kind)
    give_rows(total, held_ref, part_refs)
    out_small_ref[0:1] = jnp.sum(total * n1.astype(f32), axis=0, keepdims=True) / gain_ref[...]
    for i in range(2):
        out_small_ref[5:6, i * local : (i + 1) * local] = bias[i]
    if sums:
        for c in range(cut_ref.shape[0]):
            cut_ref[c, 0, sums.kinds * sums.rows :] = out_small_ref[...]
    if sums:
        deal_cuts(sums, cut_ref, out_refs)


def shards(
    layer_input, output_cotangent, qkv_weight, out_weight, in_weight, down_weight, qv_bias, in_bias,
    out_bias, norm_gains, query_scale, block_table, block_marks,
):
    batches, own, width = layer_input.shape
    local = qkv_weight.shape[2]
    dim = query_scale.shape[0]
    heads = local // dim
    size = lax.axis_size("context")
    spread = lax.axis_size("fsdp")
    pieces = block_table.shape[0] * 2
    seq = block_marks.shape[1]
    piece = seq // pieces
    group = size // heads
    members = group // (batches - 1)
    plan = (size, heads, group, members, dim, piece, batches)
    rows = own * spread
    me = lax.axis_index("context")
    member = me % group
    scalars = block_table.T
    here = jnp.arange(1, seq + 1, dtype=jnp.int32)
    closing = jnp.concatenate([block_marks[:, 1:] != block_marks[:, :-1], jnp.ones((batches, 1), bool)], axis=1)
    ends = lax.cummin(jnp.where(closing, here, seq), axis=1, reverse=True)
    main_end = lax.dynamic_index_in_dim(ends, member // members, 0, keepdims=False)
    main_end = main_end.reshape(-1, members, piece)
    main_end = lax.dynamic_index_in_dim(main_end, member % members, 1, keepdims=False).reshape(1, -1)
    last_end = ends[batches - 1].reshape(-1, group, piece)
    last_end = lax.dynamic_index_in_dim(last_end, member, 1, keepdims=False).reshape(1, -1)
    factor = base_rate / math.sqrt(dim) * jax.nn.softplus(query_scale)
    factor_rows = jnp.tile(factor, heads).reshape(local, 1)
    factor_col = factor.reshape(dim, 1)
    gain_one, gain_two = norm_gains[0:1], norm_gains[1:2]

    tokens = batches * rows
    weight_flops = 2 * tokens * width * local
    qkv_turned = jnp.swapaxes(qkv_weight, 1, 2)
    in_turned = in_weight.T
    whole = shape((batches, rows, width), bf16)
    narrow = shape((batches, rows, local), bf16)
    parts = [shape((batches, own, width), bf16)] * spread
    thin_parts = [shape((batches, own, local), bf16)] * spread
    held = [pltpu.VMEM((batches, rows, width), bf16)]
    thin_held = [pltpu.VMEM((batches, rows, local), bf16)]
    asked = [pieces // members * piece, pieces // group * piece]
    mine = batches * own

    x_parts = gather_rows(layer_input, "fsdp", spread)
    n1, send = call(
        functools.partial(project_kernel, plan, spread),
        [whole, shape((size, 11, dim, piece), bf16)],
        [*x_parts, qkv_turned, gain_one, qv_bias.T, factor_rows],
        scalars,
        tokens=[main_end, last_end],
    )
    got = swap_all(send, "context")
    plans = [(pieces, piece, dim, members, 2, 0, 0), (pieces, piece, dim, group, 1, 6, 2)]
    o_send, main_wide, main_lse, last_wide, last_lse = call(
        functools.partial(attend_kernel, plans),
        [shape((size, 3, dim, piece), bf16)] + [shape((r, a), f32) for a in asked for r in (dim, 1)],
        [got, main_end, last_end],
        scalars,
        [
            pltpu.SMEM((pieces,), jnp.int32), pltpu.VMEM((seq, 128), bf16), pltpu.VMEM((dim, seq), bf16),
            pltpu.VMEM((128, asked[0]), bf16),
        ],
    )
    others = [out_weight, in_turned, down_weight, in_bias.reshape(1, local), output_cotangent]
    *others, g_copy = others
    others = [gather_rows(v, "fsdp", spread, o_send) for v in others]
    g_first = exchange(g_copy, "fsdp", spread, bits_of(spread) - 1)
    o_parts = call(
        functools.partial(rows_kernel, plan), thin_parts, [swap_all(o_send, "context")], scalars, thin_held,
        tokens=[g_first],
    )
    g_parts = spread_rows(g_copy, g_first, "fsdp", spread, o_parts[0])
    o_local, o_parts = o_parts, swap_parts(o_parts, "fsdp", spread)
    even_cuts = local % (8 * size) == 0
    cuts = size if even_cuts else 1
    cut_shape = shape((cuts, 3, local // cuts, width), bf16)
    own_kind = shape((batches, own, width), bf16)
    layer_output, grad_one, n2, dy, sums, du_sum, *rest = call(
        functools.partial(middle_kernel, spread),
        [own_kind, shape((batches, own, width), f32), own_kind, own_kind, shape((3, width), f32), shape((spread, local), f32)]
        + [shape((2, mine, local), bf16)] * spread
        + thin_parts,
        [*o_parts, *others[0], *others[1], *others[2], *others[3], layer_input, output_cotangent, norm_gains, out_bias],
        scalars,
    )
    hidden_parts, do_parts = rest[:spread], swap_parts(rest[spread:], "fsdp", spread)
    (do_send,) = call(
        functools.partial(ahead_kernel, plan, spread),
        [shape((size, 3, dim, piece), bf16)],
        do_parts,
        scalars,
        thin_held,
    )
    do_got = swap_all(do_send, "context")
    hidden_parts = swap_parts(hidden_parts, "fsdp", spread)
    n2_first = exchange(n2, "fsdp", spread, bits_of(spread) - 1)
    dy_first = exchange(dy, "fsdp", spread, bits_of(spread) - 1)
    d_send, scale_sum = call(
        functools.partial(attend_back_kernel, plans),
        [shape((size, 11, dim, piece), bf16), shape((dim, 1), f32)],
        [got, do_got, factor_col, main_end, main_wide, main_lse, last_end, last_wide, last_lse],
        scalars,
        [
            pltpu.SMEM((pieces,), jnp.int32),
            pltpu.VMEM((seq, 128), bf16), pltpu.VMEM((dim, min(seq, key_tile)), bf16), pltpu.VMEM((seq, 128), bf16),
            pltpu.VMEM((128, asked[0]), bf16), pltpu.VMEM((asked[0], 128), bf16),
            pltpu.VMEM((128, asked[0]), bf16), pltpu.VMEM((asked[0], 128), bf16),
            pltpu.VMEM((seq, 128), f32), pltpu.VMEM((seq, 128), f32),
        ],
    )
    n2_parts = spread_rows(n2, n2_first, "fsdp", spread, scale_sum)
    dy_parts = spread_rows(dy, dy_first, "fsdp", spread, scale_sum)
    new_sums = lambda: Sums(size, 3, local // size, width // 2) if even_cuts else None
    early = new_sums()
    last = Sums(size, 3, local // size, width // 2, 8) if even_cuts else None
    last_cut = (size, 1, 3 * local // size + 8, width) if even_cuts else (8, 128)
    dealt = early.shapes(0) * 2 if even_cuts else [cut_shape]
    cut_scratch = [pltpu.VMEM(cut_shape.shape, bf16)]
    early_made = call(
        functools.partial(grads_kernel, spread, early),
        dealt,
        [*o_local, *hidden_parts, *dy_parts, *n2_parts, *g_parts],
        scalars,
        cut_scratch,
        tokens=[scale_sum],
    )
    d_got = swap_all(after(d_send, hidden_parts[1:], n2_first), "context")
    small = [jnp.zeros((1, width), f32), sums, du_sum.reshape(1, width), jnp.zeros((2, width), f32)]
    small.append(jnp.pad(scale_sum.reshape(1, dim) / factor, ((0, 0), (0, width - dim))))
    small = jnp.concatenate(small)
    for bit in range(bits_of(spread)):
        small = small + exchange(small, "fsdp", spread, bit)
    if even_cuts:
        early.start(early_made[: len(early_made) // 2], early_made[len(early_made) // 2 :])
        for _ in range(ahead_rounds):
            early.fold(scalars)
    small, *made = call(
        functools.partial(back_kernel, plan, spread, last),
        [shape(small.shape, f32)] + parts + (last.shapes(0) * 2 if even_cuts else [cut_shape]),
        [d_got, qkv_turned, n1, gain_one, small],
        scalars,
        held + [pltpu.VMEM((local, tokens), bf16), pltpu.VMEM(last_cut, f32)],
        tokens=[early.token] if even_cuts and ahead_rounds else [],
    )
    part, made = made[:spread], made[spread:]
    dn1_terms, _ = scatter_parts(part, "fsdp", spread)

    def close(*tokens):
        return call(
            functools.partial(close_kernel, len(dn1_terms)),
            [own_kind],
            [*dn1_terms, layer_input, grad_one, norm_gains],
            scalars,
            tokens=tokens,
        )[0]

    qkv_kind = shape((3, local, width), f32)
    if even_cuts:
        last.start(made[: len(made) // 2], made[len(made) // 2 :])
        order = ["early"] * (lead - ahead_rounds) + ["last", "early"] * (2 * early.bits - lead) + ["last"] * lead
        order = [early if name == "early" else last for name in order]
        ends = {early: [shape((local, width), f32)] * 3, last: [qkv_kind]}
        seen = small
        for index, flow in enumerate(order):
            finals = ends[flow] if flow.step == 2 * flow.bits - 1 else []
            added = flow.fold(scalars, finals, [seen])
            seen = flow.token
            if added is not None:
                small = added
            if index == 5:
                input_grad = close(seen)
                seen = input_grad
        (qkv,) = last.result
        out_grad, *feed_grads = early.result
    else:
        small = lax.psum(small, "context")
        input_grad = close()
        whole_sum = lambda v: lax.psum(v, "context").astype(f32).reshape(3, local, width)
        qkv = whole_sum(made[0])
        out_grad, *feed_grads = whole_sum(early_made[0])
    first_gain = small[0:1]
    for bit in range(bits_of(spread)):
        first_gain = first_gain + exchange(first_gain, "fsdp", spread, bit)
    gains_grad = jnp.concatenate([first_gain, small[1:2]])
    out_bias_grad = small[2:4]
    in_bias_grad = small[4].reshape(spread, local)
    in_bias_grad = lax.dynamic_index_in_dim(in_bias_grad, lax.axis_index("fsdp"), 0, keepdims=False)
    qv_grad = small[5, : 2 * local].reshape(2, local)
    scale_grad = small[7, :dim] * (base_rate / math.sqrt(dim)) * jax.nn.sigmoid(query_scale)
    return (
        layer_output,
        input_grad,
        jnp.swapaxes(qkv, 1, 2),
        out_grad,
        feed_grads[0].T,
        feed_grads[1],
        qv_grad,
        in_bias_grad,
        out_bias_grad,
        gains_grad,
        scale_grad,
    )


def solution(mesh):
    in_specs = (
        P(None, ("context", "fsdp"), None),
        P(None, ("context", "fsdp"), None),
        P(None, None, "fsdp"),
        P("fsdp", None),
        P(None, "fsdp"),
        P("fsdp", None),
        P(None, "fsdp"),
        P("fsdp"),
        P(),
        P(),
        P(),
        P(),
        P(),
    )
    out_specs = (
        P(None, ("context", "fsdp"), None),
        P(None, ("context", "fsdp"), None),
        P(None, None, "fsdp"),
        P("fsdp", None),
        P(None, "fsdp"),
        P("fsdp", None),
        P(None, "fsdp"),
        P("fsdp"),
        P(),
        P(),
        P(),
    )
    return jax.shard_map(shards, mesh=mesh, in_specs=in_specs, out_specs=out_specs, check_vma=False)
```

```python
import functools
import math

import jax
import jax.numpy as jnp
from jax import lax
from jax.experimental import pallas as pl
from jax.experimental.pallas import tpu as pltpu
from jax.sharding import PartitionSpec as P

epsilon = 1e-06
negative = -1e30
base_rate = 1.442695041
key_tile = 2048
vmem_bytes = 60 * 1024 * 1024
loop_tile = 512
full_bytes = 62 * 1024 * 1024
spare_bytes = 36 * 1024 * 1024
kernel_us = {
    "project_kernel": 7, "attend_kernel": 11, "middle_kernel": 14, "attend_back_kernel": 15, "grads_kernel": 7, "back_kernel": 11,
}
round_order = "EEQEQEQQEQQ"
first_share = 768
ahead_rounds = 1
flops_per_us = 1153500000
bf16 = jnp.bfloat16
f32 = jnp.float32

rows_cols = (((1,), (0,)), ((), ()))
cols_cols = (((1,), (1,)), ((), ()))
rows_rows = (((0,), (0,)), ((), ()))


def mm(left, right, dims=rows_cols):
    return lax.dot_general(left, right, dims, preferred_element_type=f32)


def padded_bytes(value):
    *rest, last = value.shape
    return math.prod(rest) * -(-last // 128) * 128 * jnp.dtype(value.dtype).itemsize


def call(kernel, out_shape, operands, scalars, scratch=(), tokens=(), weight=1, most=vmem_bytes):
    specs = [pl.BlockSpec(memory_space=pltpu.SMEM)]
    specs += [pl.BlockSpec(memory_space=pltpu.VMEM)] * len(operands)
    specs += [pl.BlockSpec(memory_space=pl.ANY)] * len(tokens)
    used = 1 + len(operands)
    room = spare_bytes + 2 * sum(padded_bytes(v) for v in [*operands, *out_shape, *scratch])
    weight = kernel_us.get(getattr(kernel, "func", kernel).__name__, weight)
    return pl.pallas_call(
        lambda *refs: kernel(*refs[:used], *refs[used + len(tokens) :]),
        out_shape=tuple(out_shape),
        in_specs=specs,
        out_specs=tuple(pl.BlockSpec(memory_space=pltpu.VMEM) for _ in out_shape),
        scratch_shapes=list(scratch),
        compiler_params=pltpu.CompilerParams(vmem_limit_bytes=min(most, room)),
        cost_estimate=pl.CostEstimate(flops=int(weight * flops_per_us), bytes_accessed=0, transcendentals=0),
    )(scalars, *operands, *tokens)


def loop(count, body):
    if count <= 16:
        for i in range(count):
            body(i)
    else:
        lax.fori_loop(0, count, lambda i, c: (body(i), c)[1], 0)


def shape(dims, kind):
    return jax.ShapeDtypeStruct(tuple(dims), kind)


def exchange(values, axis, size, bit):
    return lax.ppermute(values, axis, [(i, i ^ (1 << bit)) for i in range(size)])


def bits_of(size):
    return size.bit_length() - 1


def after(values, *tokens):
    leaves, tree = jax.tree.flatten(values)
    marks = jax.tree.leaves(tokens)
    anywhere = pl.BlockSpec(memory_space=pl.ANY)
    kept = pl.pallas_call(
        lambda *refs: None,
        out_shape=tuple(shape(v.shape, v.dtype) for v in leaves),
        in_specs=[anywhere] * (len(leaves) + len(marks)),
        out_specs=tuple(anywhere for _ in leaves),
        input_output_aliases={i: i for i in range(len(leaves))},
        cost_estimate=pl.CostEstimate(flops=0, bytes_accessed=0, transcendentals=0),
    )(*leaves, *marks)
    return jax.tree.unflatten(tree, kept)


def gather_rows(own, axis, size, token=None):
    held = {0: own}
    for bit in reversed(range(bits_of(size))):
        if token is not None:
            held = {k: after(v, token) if k else v for k, v in held.items()}
        held.update({k | (1 << bit): exchange(v, axis, size, bit) for k, v in list(held.items())})
    return [held[k] for k in range(size)]


def spread_rows(own, first, axis, size, token):
    top = bits_of(size) - 1
    held = {0: own}
    for bit in reversed(range(top)):
        held.update({k | (1 << bit): exchange(v, axis, size, bit) for k, v in list(held.items())})
    held[1 << top] = after(first, token)
    for bit in reversed(range(top)):
        more = [k for k in held if k >> top and not k & ((1 << (bit + 1)) - 1)]
        held.update({k | (1 << bit): exchange(held[k], axis, size, bit) for k in more})
    return [held[k] for k in range(size)]


def scatter_parts(parts, axis, size):
    held = {k: [v] for k, v in enumerate(parts)}
    sent = parts[0]
    for bit in range(bits_of(size)):
        step = 1 << bit
        for k in reversed([k for k in held if k & step]):
            terms = held.pop(k)
            if len(terms) > 1:
                terms = [sum(t.astype(f32) for t in terms).astype(bf16)]
            sent = terms[0]
            held[k ^ step].append(exchange(sent, axis, size, bit))
    return held[0], sent


def swap_parts(parts, axis, size):
    return [parts[0]] + [lax.ppermute(parts[k], axis, [(i, i ^ k) for i in range(size)]) for k in range(1, size)]


def swap_all(parts, axis):
    return lax.all_to_all(parts, axis, 0, 0, tiled=True)


def with_bit(index, place, bit):
    low = index & ((1 << place) - 1)
    return low | (bit << place) | ((index >> place) << (place + 1))


class Sums:
    def __init__(self, size, kinds, rows, lanes, cut, tail=0):
        self.size, self.bits = size, bits_of(size)
        self.kinds, self.rows, self.tail = kinds, rows, tail
        self.block = (1, kinds * rows + tail) if tail else (kinds, rows)
        self.spans = [slice(0, cut), slice(cut, lanes)]
        first = list(range(self.bits))
        second = first[:]
        if self.bits > 1:
            second[0], second[1] = 1, 0
        self.orders = [first, second]
        self.step, self.result = 0, None

    def bit(self, stream, step):
        return self.orders[stream][step if step < self.bits else 2 * self.bits - 1 - step]

    def left(self, stream, step):
        order = self.orders[stream]
        return sorted(order[step + 1 :] if step < self.bits else order[2 * self.bits - step :])

    def groups(self, step):
        found = {}
        for stream in range(2):
            found.setdefault(self.bit(stream, step), []).append(stream)
        return [(bit, streams, 1 << len(self.left(streams[0], step))) for bit, streams in found.items()]

    def shapes(self, step):
        width = [span.stop - span.start for span in self.spans]
        return [
            shape((count,) + self.block + (sum(width[v] for v in streams),), bf16)
            for _, streams, count in self.groups(step)
        ]

    def at(self, refs, stream, step, index):
        span = self.spans[stream]
        for ref, (_, streams, _) in zip(refs, self.groups(step)):
            if stream in streams:
                first = span.start if len(streams) > 1 else 0
                return ref.at[index, :, :, first : first + span.stop - span.start]

    def deal(self, read, send_refs, keep_refs, step):
        me = lax.axis_index("context")
        for stream in range(2):
            bit, left = self.bit(stream, step), self.left(stream, step)
            place = sorted(left + [bit]).index(bit)
            mine = (me >> bit) & 1
            for j in range(1 << len(left)):
                self.at(send_refs, stream, step, j)[...] = read(stream, with_bit(j, place, 1 - mine)).astype(bf16)
                self.at(keep_refs, stream, step, j)[...] = read(stream, with_bit(j, place, mine)).astype(bf16)

    def start(self, send, keep):
        self.keep = keep
        self.got = [exchange(v, "context", self.size, bit) for v, (bit, _, _) in zip(send, self.groups(self.step))]

    def fold(self, scalars, finals=(), tokens=(), group=None):
        step, last = self.step, self.step == 2 * self.bits - 1
        halving = step + 1 < self.bits
        summed = self.tail and step + 1 == self.bits
        outs = list(finals) if last else self.shapes(step + 1) * (2 if halving else 1)
        count, width = len(self.keep), len(outs)
        lanes = self.spans[1].stop

        def kernel(sc, *refs):
            keep, got = refs[:count], refs[count : 2 * count]
            out = refs[2 * count :]

            def total(stream, index):
                return self.at(keep, stream, step, index)[...].astype(f32) + self.at(got, stream, step, index)[...].astype(f32)

            if halving:
                half = len(outs) // 2
                self.deal(total, out[:half], out[half:width], step + 1)
                return
            me = lax.axis_index("context")
            for stream in range(2):
                if step < self.bits:
                    value = total(stream, 0)
                    self.at(out, stream, step + 1, 0)[...] = value.astype(bf16)
                    if summed:
                        out[width][:, self.spans[stream]] = value[0, -self.tail :]
                    continue
                bit, left = self.bit(stream, step), self.left(stream, step)
                place = sorted(left + [bit]).index(bit)
                mine = (me >> bit) & 1
                for j in range(1 << len(left)):
                    for refs_in, side in ((keep, mine), (got, 1 - mine)):
                        value = self.at(refs_in, stream, step, j)[...]
                        index = with_bit(j, place, side)
                        if not last:
                            self.at(out, stream, step + 1, index)[...] = value
                            continue
                        kinds, rows = self.kinds, self.rows
                        span = pl.ds(pl.multiple_of(index * rows, rows), rows)
                        value = value.astype(f32)
                        for kind in range(kinds):
                            to = out[kind] if width > 1 else out[0].at[kind]
                            part = value[0, kind * rows : (kind + 1) * rows] if self.tail else value[kind]
                            to[span, self.spans[stream]] = part

        if summed:
            outs = outs + [shape((self.tail, lanes), f32)]
        operands = [*self.keep, *self.got]
        made = list(call(kernel, outs, operands, scalars, tokens=tokens, weight=8))
        self.step += 1
        self.token = made[0]
        if last:
            self.result = made[:width]
        elif halving:
            self.start(made[: width // 2], made[width // 2 : width])
        else:
            self.start(made[:width], made[:width])
        return made[width] if summed else None


def chunk(k, rows):
    return pl.ds(pl.multiple_of((k ^ lax.axis_index("fsdp")) * rows, rows), rows)


def first_parity(table):
    return lax.rem(table[0, lax.axis_index("context")], 2)


def invert(table, inverse_ref):
    def note(i):
        half = i % 2 if isinstance(i, int) else lax.rem(i, 2)
        inverse_ref[table[half, i // 2]] = i

    loop(2 * table.shape[1], note)


def store_parts(plan, parity, t, out_ref, b, kind):
    size, heads, group, members, dim, piece, batches = plan
    for h in range(heads):
        block = t[h * dim : (h + 1) * dim]
        cut = [block[:, s * piece : (s + 1) * piece] for s in range(2)]
        if b < batches - 1:
            for u in range(members):
                for s in range(2):
                    out_ref[h * group + b * members + u, 2 * kind + s] = cut[s]
        else:
            base = out_ref.shape[1] // 2 + 1
            for e in range(group):
                if kind == 0:
                    out_ref[h * group + e, base] = jnp.where(parity == e % 2, cut[0], cut[1])
                else:
                    for s in range(2):
                        out_ref[h * group + e, base + 2 * kind - 1 + s] = cut[s]


def project_kernel(plan, spread, sc, *refs):
    x_refs, (w_ref, gain_ref, bias_ref, factor_ref, n1_ref, send_ref) = refs[:spread], refs[spread:]
    batches = plan[6]
    rows = x_refs[0].shape[1]
    parity = first_parity(sc)
    for b in range(batches):
        for k in range(spread):
            x = x_refs[k][b].astype(f32)
            r = lax.rsqrt(jnp.mean(x * x, axis=-1, keepdims=True) + epsilon)
            n1_ref[b, chunk(k, rows), :] = (x * r * gain_ref[...]).astype(bf16)
    n1 = n1_ref[...].reshape(-1, n1_ref.shape[2])
    for i in range(3):
        y = mm(w_ref[i], n1, cols_cols)
        if i == 0:
            y = (y + bias_ref[:, 0:1]) * factor_ref[...]
        elif i == 2:
            y = y + bias_ref[:, 1:2]
        y = y.astype(bf16)
        for b in range(batches):
            store_parts(plan, parity, y[:, b * spread * rows : (b + 1) * spread * rows], send_ref, b, i)


def place(inverse_ref, index):
    slot = inverse_ref[index]
    return slot // 2, lax.rem(slot, 2)


def turned(block):
    filled = jnp.concatenate([block, jnp.zeros((128 - block.shape[0], block.shape[1]), block.dtype)], 0)
    return filled.T


def key_parts(block_index, stride, piece, seq):
    free = 2 * block_index * stride * piece
    last = min(((2 * block_index + 2) * stride + 2) * piece, seq)
    return free, last


def attend_kernel(plans, sc, got_ref, *refs):
    units = len(plans)
    ends, o_ref, outs, scratch = refs[:units], refs[units], refs[units + 1 : -4], refs[-4:]
    invert(sc, scratch[0])
    for i, plan in enumerate(plans):
        attend_unit(plan, got_ref, ends[i], o_ref, outs[i], *scratch)


def attend_unit(plan, got_ref, end_ref, o_ref, lse_ref, inverse_ref, k_ref, vt_ref, qt_ref):
    pieces, piece, dim, stride, q_parts, base, o_base = plan
    offset = lax.rem(lax.axis_index("context"), stride)
    seq = pieces * piece
    asked = pieces // stride

    def fill(p):
        at, which = place(inverse_ref, p)
        span = pl.ds(p * piece if isinstance(p, int) else pl.multiple_of(p * piece, piece), piece)
        k_ref[span, :] = turned(got_ref[at, base + q_parts + which])
        vt_ref[:, span] = got_ref[at, base + q_parts + 2 + which]

    loop(pieces, fill)
    for j in range(asked):
        at, which = place(inverse_ref, j * stride + offset)
        qt_ref[0:dim, j * piece : (j + 1) * piece] = got_ref[at, base + (which if q_parts == 2 else 0)]
    qt_ref[dim:, :] = jnp.zeros_like(qt_ref[dim:, :])
    if asked != o_ref.shape[0] * q_parts:
        for part in range(q_parts):
            o_ref[:, o_base + part] = jnp.zeros_like(o_ref[:, o_base + part])
    wide = 2 * piece
    for i in range(asked // 2):
        span = slice(i * wide, (i + 1) * wide)
        qt = qt_ref[:, span]
        end = end_ref[:, span]
        free, last = key_parts(i, stride, piece, seq)
        if last <= key_tile:
            masked = mm(k_ref[free:last, :], qt)
            at = lax.broadcasted_iota(jnp.int32, masked.shape, 0) + free
            masked = jnp.where(at < end, masked, negative)
            top = jnp.max(masked, axis=0, keepdims=True)
            if free:
                plain = mm(k_ref[0:free, :], qt)
                top = jnp.maximum(top, jnp.max(plain, axis=0, keepdims=True))
            weight = jnp.exp(masked - top)
            total = jnp.sum(weight, axis=0, keepdims=True)
            out = mm(vt_ref[:, free:last], weight.astype(bf16))
            if free:
                weight = jnp.exp(plain - top)
                total = total + jnp.sum(weight, axis=0, keepdims=True)
                out = out + mm(vt_ref[:, 0:free], weight.astype(bf16))
        else:

            def tile(t, carry):
                top, total, out = carry
                first = pl.multiple_of(t * loop_tile, loop_tile)
                scores = mm(k_ref[pl.ds(first, loop_tile), :], qt)
                at = lax.broadcasted_iota(jnp.int32, scores.shape, 0) + first
                scores = jnp.where(at < end, scores, negative)
                new = jnp.maximum(top, jnp.max(scores, axis=0, keepdims=True))
                weight = jnp.exp(scores - new)
                change = jnp.exp(top - new)
                total = total * change + jnp.sum(weight, axis=0, keepdims=True)
                out = out * change + mm(vt_ref[:, pl.ds(first, loop_tile)], weight.astype(bf16))
                return new, total, out

            start = (jnp.full((1, wide), negative, f32), jnp.zeros((1, wide), f32), jnp.zeros((dim, wide), f32))
            tiles = min(-(-last // loop_tile), seq // loop_tile)
            top, total, out = lax.fori_loop(0, tiles, tile, start)
        out = out / total
        lse_ref[:, span] = top + jnp.log(total)
        for s in range(2):
            at, which = place(inverse_ref, (2 * i + s) * stride + offset)
            o_ref[at, o_base + (which if q_parts == 2 else 0)] = out[:, s * piece : (s + 1) * piece].astype(bf16)


def attend_back_kernel(plans, sc, got_ref, do_ref, factor_ref, *refs):
    units = len(plans)
    o_ref, saved, (d_ref, scale_ref), scratch = refs[0], refs[1 : 1 + 2 * units], refs[1 + 2 * units : 3 + 2 * units], refs[3 + 2 * units :]
    scale = 0.0
    invert(sc, scratch[0])
    for i, plan in enumerate(plans):
        own = saved[2 * i : 2 * i + 2]
        scale = scale + attend_back_unit(plan, got_ref, do_ref, factor_ref, o_ref, *own, d_ref, *scratch)
    scale_ref[...] = scale


def attend_back_unit(
    plan, got_ref, do_ref, factor_ref, o_ref, end_ref, lse_ref, d_ref,
    inverse_ref, k_ref, kt_ref, v_ref, qt_ref, q_ref, dot_ref, dor_ref, dk_ref, dv_ref,
):
    pieces, piece, dim, stride, q_parts, base, o_base = plan
    offset = lax.rem(lax.axis_index("context"), stride)
    seq = pieces * piece
    asked = pieces // stride

    def fill(p):
        at, which = place(inverse_ref, p)
        span = pl.ds(p * piece if isinstance(p, int) else pl.multiple_of(p * piece, piece), piece)
        kt = got_ref[at, base + q_parts + which]
        if seq <= key_tile:
            kt_ref[:, span] = kt
        k_ref[span, :] = turned(kt)
        v_ref[span, :] = turned(got_ref[at, base + q_parts + 2 + which])

    loop(pieces, fill)
    for j in range(asked):
        at, which = place(inverse_ref, j * stride + offset)
        span = slice(j * piece, (j + 1) * piece)
        qt = got_ref[at, base + (which if q_parts == 2 else 0)]
        qt_ref[0:dim, span] = qt
        q_ref[span, :] = turned(qt)
        do = do_ref[at, o_base + (which if q_parts == 2 else 0)]
        dot_ref[0:dim, span] = do
        dor_ref[span, :] = turned(do)
    qt_ref[dim:, :] = jnp.zeros_like(qt_ref[dim:, :])
    dot_ref[dim:, :] = jnp.zeros_like(dot_ref[dim:, :])
    dk_ref[...] = jnp.zeros_like(dk_ref)
    dv_ref[...] = jnp.zeros_like(dv_ref)
    if asked != d_ref.shape[0] * q_parts:
        for part in range(q_parts):
            d_ref[:, base + part] = jnp.zeros_like(d_ref[:, base + part])
    wide = 2 * piece
    scale = jnp.zeros((dim, 1), f32)
    for i in range(asked // 2):
        span = slice(i * wide, (i + 1) * wide)
        qt, q, do, dor = qt_ref[:, span], q_ref[span, :], dot_ref[:, span], dor_ref[span, :]
        end, lse = end_ref[:, span], lse_ref[:, span]
        owners = [place(inverse_ref, (2 * i + s) * stride + offset) for s in range(2)]
        o = jnp.concatenate([o_ref[at, o_base + (which if q_parts == 2 else 0)] for at, which in owners], axis=1)
        delta = jnp.sum(do[0:dim].astype(f32) * o.astype(f32), axis=0, keepdims=True)
        free, last = key_parts(i, stride, piece, seq)

        def visit(keys, masked_from):
            scores = mm(k_ref[keys, :], qt)
            if masked_from is not None:
                at = lax.broadcasted_iota(jnp.int32, scores.shape, 0) + masked_from
                scores = jnp.where(at < end, scores, negative)
            prob = jnp.exp(scores - lse)
            ds = (prob * (mm(v_ref[keys, :], do) - delta)).astype(bf16)
            dv_ref[keys, :] += mm(prob.astype(bf16), dor)
            dk_ref[keys, :] += mm(ds, q)
            return mm(kt_ref[:, keys] if seq <= key_tile else k_ref[keys, :].T[0:dim], ds)

        if last <= key_tile:
            dq = visit(pl.ds(free, last - free), free)
            if free:
                dq = dq + visit(pl.ds(0, free), None)
        else:

            def tile(t, dq):
                first = pl.multiple_of(t * loop_tile, loop_tile)
                return dq + visit(pl.ds(first, loop_tile), first)

            tiles = min(-(-last // loop_tile), seq // loop_tile)
            dq = lax.fori_loop(0, tiles, tile, jnp.zeros((dim, wide), f32))
        scale = scale + jnp.sum(dq * qt[0:dim].astype(f32), axis=1, keepdims=True)
        dq = (dq * factor_ref[...]).astype(bf16)
        for s in range(2):
            at, which = place(inverse_ref, (2 * i + s) * stride + offset)
            d_ref[at, base + (which if q_parts == 2 else 0)] = dq[:, s * piece : (s + 1) * piece]

    def give(p):
        at, which = place(inverse_ref, p)
        span = pl.ds(p * piece if isinstance(p, int) else pl.multiple_of(p * piece, piece), piece)
        d_ref[at, base + q_parts + which] = dk_ref[span, :].T[0:dim].astype(bf16)
        d_ref[at, base + q_parts + 2 + which] = dv_ref[span, :].T[0:dim].astype(bf16)

    loop(pieces, give)
    return scale


def total_of(blocks):
    if len(blocks) == 1:
        return blocks[0]
    return sum(b.astype(f32) for b in blocks[1:]) + blocks[0].astype(f32)


def collect(plan, even, got_ref, b, which, kind):
    size, heads, group, members, dim, piece, batches = plan
    base = got_ref.shape[1] // 2 + 1
    parts = []
    for h in range(heads):
        if b < batches - 1:
            blocks = [got_ref[h * group + b * members + u, 2 * kind + which] for u in range(members)]
        elif kind == 0:
            parity = even if which == 0 else 1 - even
            blocks = [got_ref[h * group + 2 * u + parity, base] for u in range(group // 2)]
        else:
            blocks = [got_ref[h * group + e, base + 2 * kind - 1 + which] for e in range(group)]
        parts.append(total_of(blocks).astype(bf16))
    return jnp.concatenate(parts, axis=0)


def give_rows(value, held_ref, out_refs):
    batches, rows, _ = out_refs[0].shape
    held_ref[...] = value.astype(bf16).reshape(held_ref.shape)
    for k, out_ref in enumerate(out_refs):
        for b in range(batches):
            out_ref[b] = held_ref[b, chunk(k, rows), :]


def flat(ref):
    return ref[...].reshape(-1, ref.shape[-1])


def rows_kernel(plan, sc, got_ref, *refs):
    piece, batches = plan[5], plan[6]
    *out_refs, held_ref = refs
    rows = out_refs[0].shape[1]
    even = first_parity(sc)
    for b in range(batches):
        for s in range(2):
            held_ref[b, s * piece : (s + 1) * piece] = collect(plan, even, got_ref, b, s, 0).T
        for k, out_ref in enumerate(out_refs):
            out_ref[b] = held_ref[b, chunk(k, rows), :]


def middle_kernel(spread, sc, *refs):
    o_refs, wo, wi, wd, bias_refs = [refs[i * spread : (i + 1) * spread] for i in range(5)]
    refs = refs[5 * spread :]
    x_ref, g_ref, gain_ref, out_bias_ref, out_ref, grad_ref, n2_ref, dy_ref, sums_ref, du_sum_ref = refs[:10]
    hidden_refs, do_refs = [refs[10 + i * spread : 10 + (i + 1) * spread] for i in range(2)]
    kind = out_ref.shape
    h1 = flat(x_ref).astype(f32) + out_bias_ref[0:1]
    for k in range(spread):
        h1 = h1 + mm(flat(o_refs[k]), wo[k][...])
    r2 = lax.rsqrt(jnp.mean(h1 * h1, axis=-1, keepdims=True) + epsilon)
    n2 = (h1 * r2 * gain_ref[1:2]).astype(bf16)
    n2_ref[...] = n2.reshape(kind)
    g = flat(g_ref)
    out = h1 + out_bias_ref[1:2]
    dn2 = 0.0
    for k in range(spread):
        u = mm(n2, wi[k][...], cols_cols) + bias_refs[k][...]
        gate = 1.0 / (1.0 + jnp.exp(-u))
        a = (u * gate).astype(bf16)
        out = out + mm(a, wd[k][...])
        ga = mm(g, wd[k][...], cols_cols)
        du = (ga * gate * (1.0 + u * (1.0 - gate))).astype(bf16)
        dn2 = dn2 + mm(du, wi[k][...])
        hidden_refs[k][0] = a
        hidden_refs[k][1] = du
        du_sum_ref[pl.ds(k ^ lax.axis_index("fsdp"), 1), :] = jnp.sum(du.astype(f32), axis=0, keepdims=True)
    out_ref[...] = out.astype(bf16).reshape(kind)
    z2 = gain_ref[1:2] * dn2
    g = g.astype(f32)
    grad = g + r2 * z2 - h1 * (r2 * r2 * r2 * jnp.mean(z2 * h1, axis=-1, keepdims=True))
    grad_ref[...] = grad.reshape(kind)
    dy = grad.astype(bf16)
    dy_ref[...] = dy.reshape(kind)
    sums_ref[0:1] = jnp.sum(dn2 * h1 * r2, axis=0, keepdims=True)
    sums_ref[1:2] = jnp.sum(grad, axis=0, keepdims=True)
    sums_ref[2:3] = jnp.sum(g, axis=0, keepdims=True)
    for k in range(spread):
        do_refs[k][...] = mm(dy, wo[k][...], cols_cols).astype(bf16).reshape(do_refs[k].shape)


def cut_rows(value, out_ref, kind):
    chunks = out_ref.shape[0]
    rows = value.shape[0] // chunks
    for c in range(chunks):
        part = value[c * rows : (c + 1) * rows]
        if out_ref.shape[1] == 1:
            out_ref[c, 0, kind * rows : (kind + 1) * rows] = part.astype(out_ref.dtype)
        else:
            out_ref[c, kind] = part.astype(out_ref.dtype)


def grads_kernel(spread, sums, sc, *refs):
    o_refs, hidden_refs, dy_refs, n2_refs, g_refs = [refs[i * spread : (i + 1) * spread] for i in range(5)]
    *out_refs, cut_ref = refs[5 * spread :]
    stack = lambda parts: jnp.concatenate([p[...].reshape(-1, p.shape[-1]) for p in parts])
    target = cut_ref if sums else out_refs[0]
    cut_rows(mm(stack([h.at[0] for h in hidden_refs]), stack(g_refs), rows_rows), target, 2)
    cut_rows(mm(stack([h.at[1] for h in hidden_refs]), stack(n2_refs), rows_rows), target, 1)
    cut_rows(mm(stack(o_refs), stack(dy_refs), rows_rows), target, 0)
    if sums:
        deal_cuts(sums, cut_ref, out_refs)


def deal_cuts(sums, cut_ref, out_refs):
    half = len(out_refs) // 2
    read = lambda stream, index: cut_ref[index, :, :, sums.spans[stream]]
    sums.deal(read, out_refs[:half], out_refs[half:], 0)


def close_kernel(terms, sc, *refs):
    part_refs, (x_ref, grad_ref, gain_ref, out_ref) = refs[:terms], refs[terms:]
    dn1 = sum(flat(p).astype(f32) for p in part_refs)
    x = flat(x_ref).astype(f32)
    r1 = lax.rsqrt(jnp.mean(x * x, axis=-1, keepdims=True) + epsilon)
    z1 = gain_ref[0:1] * dn1
    out = flat(grad_ref) + r1 * z1 - x * (r1 * r1 * r1 * jnp.mean(z1 * x, axis=-1, keepdims=True))
    out_ref[...] = out.astype(bf16).reshape(out_ref.shape)


def ahead_kernel(plan, spread, sc, *refs):
    do_refs, (send_ref, held_ref) = refs[:spread], refs[spread:]
    rows = do_refs[0].shape[1]
    parity = first_parity(sc)
    for b in range(plan[6]):
        for k in range(spread):
            held_ref[b, chunk(k, rows), :] = do_refs[k][b]
        store_parts(plan, parity, held_ref[b].T, send_ref, b, 0)


def back_kernel(plan, spread, sums, sc, got_ref, w_ref, n1_ref, gain_ref, small_ref, out_small_ref, *refs):
    size, heads, group, members, dim, piece, batches = plan
    part_refs, refs = refs[:spread], refs[spread:]
    *out_refs, held_ref, turned_ref, cut_ref = refs
    local = heads * dim
    even = first_parity(sc)
    out_small_ref[...] = small_ref[...]
    total = 0.0
    bias = []
    n1 = flat(n1_ref)
    target = cut_ref if sums else out_refs[0]
    for kind in range(3):
        for b in range(batches):
            for s in range(2):
                at = (2 * b + s) * piece
                turned_ref[:, at : at + piece] = collect(plan, even, got_ref, b, s, kind)
        turned_rows = turned_ref[...]
        rows = turned_rows.T
        if kind != 1:
            bias.append(jnp.sum(rows.astype(f32), axis=0, keepdims=True))
        total = total + mm(rows, w_ref[kind])
        cut_rows(mm(turned_rows, n1), target, kind)
    give_rows(total, held_ref, part_refs)
    out_small_ref[0:1] = jnp.sum(total * n1.astype(f32), axis=0, keepdims=True) / gain_ref[...]
    for i in range(2):
        out_small_ref[5:6, i * local : (i + 1) * local] = bias[i]
    if sums:
        for c in range(cut_ref.shape[0]):
            cut_ref[c, 0, sums.kinds * sums.rows :] = out_small_ref[...]
    if sums:
        deal_cuts(sums, cut_ref, out_refs)


def shards(
    layer_input, output_cotangent, qkv_weight, out_weight, in_weight, down_weight, qv_bias, in_bias,
    out_bias, norm_gains, query_scale, block_table, block_marks,
):
    batches, own, width = layer_input.shape
    local = qkv_weight.shape[2]
    dim = query_scale.shape[0]
    heads = local // dim
    size = lax.axis_size("context")
    spread = lax.axis_size("fsdp")
    pieces = block_table.shape[0] * 2
    seq = block_marks.shape[1]
    piece = seq // pieces
    group = size // heads
    members = group // (batches - 1)
    plan = (size, heads, group, members, dim, piece, batches)
    rows = own * spread
    me = lax.axis_index("context")
    member = me % group
    scalars = block_table.T
    here = jnp.arange(1, seq + 1, dtype=jnp.int32)
    closing = jnp.concatenate([block_marks[:, 1:] != block_marks[:, :-1], jnp.ones((batches, 1), bool)], axis=1)
    ends = lax.cummin(jnp.where(closing, here, seq), axis=1, reverse=True)
    main_end = lax.dynamic_index_in_dim(ends, member // members, 0, keepdims=False)
    main_end = main_end.reshape(-1, members, piece)
    main_end = lax.dynamic_index_in_dim(main_end, member % members, 1, keepdims=False).reshape(1, -1)
    last_end = ends[batches - 1].reshape(-1, group, piece)
    last_end = lax.dynamic_index_in_dim(last_end, member, 1, keepdims=False).reshape(1, -1)
    factor = base_rate / math.sqrt(dim) * jax.nn.softplus(query_scale)
    factor_rows = jnp.tile(factor, heads).reshape(local, 1)
    factor_col = factor.reshape(dim, 1)
    gain_one, gain_two = norm_gains[0:1], norm_gains[1:2]

    tokens = batches * rows
    weight_flops = 2 * tokens * width * local
    qkv_turned = jnp.swapaxes(qkv_weight, 1, 2)
    in_turned = in_weight.T
    whole = shape((batches, rows, width), bf16)
    narrow = shape((batches, rows, local), bf16)
    parts = [shape((batches, own, width), bf16)] * spread
    thin_parts = [shape((batches, own, local), bf16)] * spread
    held = [pltpu.VMEM((batches, rows, width), bf16)]
    thin_held = [pltpu.VMEM((batches, rows, local), bf16)]
    asked = [pieces // members * piece, pieces // group * piece]
    mine = batches * own

    x_parts = gather_rows(layer_input, "fsdp", spread)
    n1, send = call(
        functools.partial(project_kernel, plan, spread),
        [whole, shape((size, 11, dim, piece), bf16)],
        [*x_parts, qkv_turned, gain_one, qv_bias.T, factor_rows],
        scalars,
        tokens=[main_end, last_end],
    )
    got = swap_all(send, "context")
    plans = [(pieces, piece, dim, members, 2, 0, 0), (pieces, piece, dim, group, 1, 6, 2)]
    o_send, main_lse, last_lse = call(
        functools.partial(attend_kernel, plans),
        [shape((size, 3, dim, piece), bf16)] + [shape((1, a), f32) for a in asked],
        [got, main_end, last_end],
        scalars,
        [
            pltpu.SMEM((pieces,), jnp.int32), pltpu.VMEM((seq, 128), bf16), pltpu.VMEM((dim, seq), bf16),
            pltpu.VMEM((128, asked[0]), bf16),
        ],
    )
    others = [out_weight, in_turned, down_weight, in_bias.reshape(1, local), output_cotangent]
    *others, g_copy = others
    others = [gather_rows(v, "fsdp", spread, o_send) for v in others]
    g_first = exchange(g_copy, "fsdp", spread, bits_of(spread) - 1)
    o_parts = call(
        functools.partial(rows_kernel, plan), thin_parts, [swap_all(o_send, "context")], scalars, thin_held,
        tokens=[g_first],
    )
    g_parts = spread_rows(g_copy, g_first, "fsdp", spread, o_parts[0])
    o_local, o_parts = o_parts, swap_parts(o_parts, "fsdp", spread)
    even_cuts = local % (8 * size) == 0
    cuts = size if even_cuts else 1
    cut_shape = shape((cuts, 3, local // cuts, width), bf16)
    own_kind = shape((batches, own, width), bf16)
    layer_output, grad_one, n2, dy, sums, du_sum, *rest = call(
        functools.partial(middle_kernel, spread),
        [own_kind, shape((batches, own, width), f32), own_kind, own_kind, shape((3, width), f32), shape((spread, local), f32)]
        + [shape((2, mine, local), bf16)] * spread
        + thin_parts,
        [*o_parts, *others[0], *others[1], *others[2], *others[3], layer_input, output_cotangent, norm_gains, out_bias],
        scalars,
    )
    hidden_parts, do_parts = rest[:spread], swap_parts(rest[spread:], "fsdp", spread)
    (do_send,) = call(
        functools.partial(ahead_kernel, plan, spread),
        [shape((size, 3, dim, piece), bf16)],
        do_parts,
        scalars,
        thin_held,
    )
    do_got = swap_all(do_send, "context")
    hidden_parts = swap_parts(hidden_parts, "fsdp", spread)
    n2_first = exchange(n2, "fsdp", spread, bits_of(spread) - 1)
    dy_first = exchange(dy, "fsdp", spread, bits_of(spread) - 1)
    d_send, scale_sum = call(
        functools.partial(attend_back_kernel, plans),
        [shape((size, 11, dim, piece), bf16), shape((dim, 1), f32)],
        [got, do_got, factor_col, o_send, main_end, main_lse, last_end, last_lse],
        scalars,
        most=vmem_bytes if seq <= key_tile else full_bytes,
        scratch=[
            pltpu.SMEM((pieces,), jnp.int32),
            pltpu.VMEM((seq, 128), bf16), pltpu.VMEM((dim, min(seq, key_tile)), bf16), pltpu.VMEM((seq, 128), bf16),
            pltpu.VMEM((128, asked[0]), bf16), pltpu.VMEM((asked[0], 128), bf16),
            pltpu.VMEM((128, asked[0]), bf16), pltpu.VMEM((asked[0], 128), bf16),
            pltpu.VMEM((seq, 128), f32), pltpu.VMEM((seq, 128), f32),
        ],
    )
    n2_parts = spread_rows(n2, n2_first, "fsdp", spread, scale_sum)
    dy_parts = spread_rows(dy, dy_first, "fsdp", spread, scale_sum)
    cut = width * first_share // 1280 // 128 * 128
    new_sums = lambda tail: Sums(size, 3, local // size, width, cut, tail) if even_cuts else None
    early, last = new_sums(0), new_sums(8)
    last_cut = (size, 1, 3 * local // size + 8, width) if even_cuts else (8, 128)
    dealt = early.shapes(0) * 2 if even_cuts else [cut_shape]
    cut_scratch = [pltpu.VMEM(cut_shape.shape, bf16)]
    early_made = call(
        functools.partial(grads_kernel, spread, early),
        dealt,
        [*o_local, *hidden_parts, *dy_parts, *n2_parts, *g_parts],
        scalars,
        cut_scratch,
        tokens=[scale_sum],
    )
    d_got = swap_all(after(d_send, hidden_parts[1:], n2_first), "context")
    small = [jnp.zeros((1, width), f32), sums, du_sum.reshape(1, width), jnp.zeros((2, width), f32)]
    small.append(jnp.pad(scale_sum.reshape(1, dim) / factor, ((0, 0), (0, width - dim))))
    small = jnp.concatenate(small)
    for bit in range(bits_of(spread)):
        small = small + exchange(small, "fsdp", spread, bit)
    if even_cuts:
        early.start(early_made[: len(early_made) // 2], early_made[len(early_made) // 2 :])
        for _ in range(ahead_rounds):
            early.fold(scalars)
    small, *made = call(
        functools.partial(back_kernel, plan, spread, last),
        [shape(small.shape, f32)] + parts + (last.shapes(0) * 2 if even_cuts else [cut_shape]),
        [d_got, qkv_turned, n1, gain_one, small],
        scalars,
        held + [pltpu.VMEM((local, tokens), bf16), pltpu.VMEM(last_cut, f32)],
        tokens=[early.token] if even_cuts and ahead_rounds else [],
    )
    part, made = made[:spread], made[spread:]
    dn1_terms, _ = scatter_parts(part, "fsdp", spread)

    def close(*tokens):
        return call(
            functools.partial(close_kernel, len(dn1_terms)),
            [own_kind],
            [*dn1_terms, layer_input, grad_one, norm_gains],
            scalars,
            tokens=tokens,
        )[0]

    qkv_kind = shape((3, local, width), f32)
    if even_cuts:
        last.start(made[: len(made) // 2], made[len(made) // 2 :])
        order = round_order
        order = [early if name == "E" else last for name in order]
        ends = {early: [shape((local, width), f32)] * 3, last: [qkv_kind]}
        seen = small
        for index, flow in enumerate(order):
            finals = ends[flow] if flow.step == 2 * flow.bits - 1 else []
            added = flow.fold(scalars, finals, [seen])
            seen = flow.token
            if added is not None:
                small = added
            if index == 5:
                input_grad = close(seen)
                seen = input_grad
        (qkv,) = last.result
        out_grad, *feed_grads = early.result
    else:
        small = lax.psum(small, "context")
        input_grad = close()
        whole_sum = lambda v: lax.psum(v, "context").astype(f32).reshape(3, local, width)
        qkv = whole_sum(made[0])
        out_grad, *feed_grads = whole_sum(early_made[0])
    first_gain = small[0:1]
    for bit in range(bits_of(spread)):
        first_gain = first_gain + exchange(first_gain, "fsdp", spread, bit)
    gains_grad = jnp.concatenate([first_gain, small[1:2]])
    out_bias_grad = small[2:4]
    in_bias_grad = small[4].reshape(spread, local)
    in_bias_grad = lax.dynamic_index_in_dim(in_bias_grad, lax.axis_index("fsdp"), 0, keepdims=False)
    qv_grad = small[5, : 2 * local].reshape(2, local)
    scale_grad = small[7, :dim] * (base_rate / math.sqrt(dim)) * jax.nn.sigmoid(query_scale)
    return (
        layer_output,
        input_grad,
        jnp.swapaxes(qkv, 1, 2),
        out_grad,
        feed_grads[0].T,
        feed_grads[1],
        qv_grad,
        in_bias_grad,
        out_bias_grad,
        gains_grad,
        scale_grad,
    )


def solution(mesh):
    in_specs = (
        P(None, ("context", "fsdp"), None),
        P(None, ("context", "fsdp"), None),
        P(None, None, "fsdp"),
        P("fsdp", None),
        P(None, "fsdp"),
        P("fsdp", None),
        P(None, "fsdp"),
        P("fsdp"),
        P(),
        P(),
        P(),
        P(),
        P(),
    )
    out_specs = (
        P(None, ("context", "fsdp"), None),
        P(None, ("context", "fsdp"), None),
        P(None, None, "fsdp"),
        P("fsdp", None),
        P(None, "fsdp"),
        P("fsdp", None),
        P(None, "fsdp"),
        P("fsdp"),
        P(),
        P(),
        P(),
    )
    return jax.shard_map(shards, mesh=mesh, in_specs=in_specs, out_specs=out_specs, check_vma=False)
```

```python
import functools
import math

import jax
import jax.numpy as jnp
from jax import lax
from jax.experimental import pallas as pl
from jax.experimental.pallas import tpu as pltpu
from jax.sharding import PartitionSpec as P

epsilon = 1e-06
negative = -1e30
base_rate = 1.442695041
key_tile = 2048
vmem_bytes = 60 * 1024 * 1024
loop_tile = 512
full_bytes = 62 * 1024 * 1024
spare_bytes = 36 * 1024 * 1024
kernel_us = {
    "project_kernel": 7, "attend_kernel": 11, "middle_kernel": 14, "attend_back_kernel": 15, "grads_kernel": 7, "back_kernel": 11,
}
round_order = "EEQEQEQQQEQ"
first_share = 768
ahead_rounds = 1
flops_per_us = 1153500000
bf16 = jnp.bfloat16
f32 = jnp.float32

rows_cols = (((1,), (0,)), ((), ()))
cols_cols = (((1,), (1,)), ((), ()))
rows_rows = (((0,), (0,)), ((), ()))


def mm(left, right, dims=rows_cols):
    return lax.dot_general(left, right, dims, preferred_element_type=f32)


def padded_bytes(value):
    *rest, last = value.shape
    return math.prod(rest) * -(-last // 128) * 128 * jnp.dtype(value.dtype).itemsize


def call(kernel, out_shape, operands, scalars, scratch=(), tokens=(), weight=1, most=vmem_bytes, loose=()):
    specs = [pl.BlockSpec(memory_space=pltpu.SMEM)]
    specs += [pl.BlockSpec(memory_space=pl.ANY if i in loose else pltpu.VMEM) for i in range(len(operands))]
    specs += [pl.BlockSpec(memory_space=pl.ANY)] * len(tokens)
    used = 1 + len(operands)
    room = spare_bytes + 2 * sum(padded_bytes(v) for v in [*operands, *out_shape, *scratch] if "sem" not in str(v.dtype))
    weight = kernel_us.get(getattr(kernel, "func", kernel).__name__, weight)
    return pl.pallas_call(
        lambda *refs: kernel(*refs[:used], *refs[used + len(tokens) :]),
        out_shape=tuple(out_shape),
        in_specs=specs,
        out_specs=tuple(pl.BlockSpec(memory_space=pltpu.VMEM) for _ in out_shape),
        scratch_shapes=list(scratch),
        compiler_params=pltpu.CompilerParams(vmem_limit_bytes=min(most, room)),
        cost_estimate=pl.CostEstimate(flops=int(weight * flops_per_us), bytes_accessed=0, transcendentals=0),
    )(scalars, *operands, *tokens)


def loop(count, body):
    if count <= 16:
        for i in range(count):
            body(i)
    else:
        lax.fori_loop(0, count, lambda i, c: (body(i), c)[1], 0)


def shape(dims, kind):
    return jax.ShapeDtypeStruct(tuple(dims), kind)


def exchange(values, axis, size, bit):
    return lax.ppermute(values, axis, [(i, i ^ (1 << bit)) for i in range(size)])


def bits_of(size):
    return size.bit_length() - 1


def after(values, *tokens):
    leaves, tree = jax.tree.flatten(values)
    marks = jax.tree.leaves(tokens)
    anywhere = pl.BlockSpec(memory_space=pl.ANY)
    kept = pl.pallas_call(
        lambda *refs: None,
        out_shape=tuple(shape(v.shape, v.dtype) for v in leaves),
        in_specs=[anywhere] * (len(leaves) + len(marks)),
        out_specs=tuple(anywhere for _ in leaves),
        input_output_aliases={i: i for i in range(len(leaves))},
        cost_estimate=pl.CostEstimate(flops=0, bytes_accessed=0, transcendentals=0),
    )(*leaves, *marks)
    return jax.tree.unflatten(tree, kept)


def gather_rows(own, axis, size, token=None):
    held = {0: own}
    for bit in reversed(range(bits_of(size))):
        if token is not None:
            held = {k: after(v, token) if k else v for k, v in held.items()}
        held.update({k | (1 << bit): exchange(v, axis, size, bit) for k, v in list(held.items())})
    return [held[k] for k in range(size)]


def spread_rows(own, first, axis, size, token):
    top = bits_of(size) - 1
    held = {0: own}
    for bit in reversed(range(top)):
        held.update({k | (1 << bit): exchange(v, axis, size, bit) for k, v in list(held.items())})
    held[1 << top] = after(first, token)
    for bit in reversed(range(top)):
        more = [k for k in held if k >> top and not k & ((1 << (bit + 1)) - 1)]
        held.update({k | (1 << bit): exchange(held[k], axis, size, bit) for k in more})
    return [held[k] for k in range(size)]


def scatter_parts(parts, axis, size):
    held = {k: [v] for k, v in enumerate(parts)}
    sent = parts[0]
    for bit in range(bits_of(size)):
        step = 1 << bit
        for k in reversed([k for k in held if k & step]):
            terms = held.pop(k)
            if len(terms) > 1:
                terms = [sum(t.astype(f32) for t in terms).astype(bf16)]
            sent = terms[0]
            held[k ^ step].append(exchange(sent, axis, size, bit))
    return held[0], sent


def swap_parts(parts, axis, size):
    return [parts[0]] + [lax.ppermute(parts[k], axis, [(i, i ^ k) for i in range(size)]) for k in range(1, size)]


def swap_all(parts, axis):
    return lax.all_to_all(parts, axis, 0, 0, tiled=True)


def with_bit(index, place, bit):
    low = index & ((1 << place) - 1)
    return low | (bit << place) | ((index >> place) << (place + 1))


class Sums:
    def __init__(self, size, kinds, rows, lanes, cut, tail=0):
        self.size, self.bits = size, bits_of(size)
        self.kinds, self.rows, self.tail = kinds, rows, tail
        self.block = (1, kinds * rows + tail) if tail else (kinds, rows)
        self.spans = [slice(0, cut), slice(cut, lanes)]
        first = list(range(self.bits))
        second = first[:]
        if self.bits > 1:
            second[0], second[1] = 1, 0
        self.orders = [first, second]
        self.step, self.result = 0, None

    def bit(self, stream, step):
        return self.orders[stream][step if step < self.bits else 2 * self.bits - 1 - step]

    def left(self, stream, step):
        order = self.orders[stream]
        return sorted(order[step + 1 :] if step < self.bits else order[2 * self.bits - step :])

    def groups(self, step):
        found = {}
        for stream in range(2):
            found.setdefault(self.bit(stream, step), []).append(stream)
        return [(bit, streams, 1 << len(self.left(streams[0], step))) for bit, streams in found.items()]

    def shapes(self, step):
        width = [span.stop - span.start for span in self.spans]
        return [
            shape((count,) + self.block + (sum(width[v] for v in streams),), bf16)
            for _, streams, count in self.groups(step)
        ]

    def at(self, refs, stream, step, index):
        span = self.spans[stream]
        for ref, (_, streams, _) in zip(refs, self.groups(step)):
            if stream in streams:
                first = span.start if len(streams) > 1 else 0
                return ref.at[index, :, :, first : first + span.stop - span.start]

    def deal(self, read, send_refs, keep_refs, step):
        me = lax.axis_index("context")
        for stream in range(2):
            bit, left = self.bit(stream, step), self.left(stream, step)
            place = sorted(left + [bit]).index(bit)
            mine = (me >> bit) & 1
            for j in range(1 << len(left)):
                self.at(send_refs, stream, step, j)[...] = read(stream, with_bit(j, place, 1 - mine)).astype(bf16)
                self.at(keep_refs, stream, step, j)[...] = read(stream, with_bit(j, place, mine)).astype(bf16)

    def start(self, send, keep):
        self.keep = keep
        self.got = [exchange(v, "context", self.size, bit) for v, (bit, _, _) in zip(send, self.groups(self.step))]

    def fold(self, scalars, finals=(), tokens=(), group=None):
        step, last = self.step, self.step == 2 * self.bits - 1
        halving = step + 1 < self.bits
        summed = self.tail and step + 1 == self.bits
        outs = list(finals) if last else self.shapes(step + 1) * (2 if halving else 1)
        count, width = len(self.keep), len(outs)
        lanes = self.spans[1].stop

        def kernel(sc, *refs):
            keep, got = refs[:count], refs[count : 2 * count]
            out = refs[2 * count :]

            def total(stream, index):
                return self.at(keep, stream, step, index)[...].astype(f32) + self.at(got, stream, step, index)[...].astype(f32)

            if halving:
                half = len(outs) // 2
                self.deal(total, out[:half], out[half:width], step + 1)
                return
            me = lax.axis_index("context")
            for stream in range(2):
                if step < self.bits:
                    value = total(stream, 0)
                    self.at(out, stream, step + 1, 0)[...] = value.astype(bf16)
                    if summed:
                        out[width][:, self.spans[stream]] = value[0, -self.tail :]
                    continue
                bit, left = self.bit(stream, step), self.left(stream, step)
                place = sorted(left + [bit]).index(bit)
                mine = (me >> bit) & 1
                for j in range(1 << len(left)):
                    for refs_in, side in ((keep, mine), (got, 1 - mine)):
                        value = self.at(refs_in, stream, step, j)[...]
                        index = with_bit(j, place, side)
                        if not last:
                            self.at(out, stream, step + 1, index)[...] = value
                            continue
                        kinds, rows = self.kinds, self.rows
                        span = pl.ds(pl.multiple_of(index * rows, rows), rows)
                        value = value.astype(f32)
                        for kind in range(kinds):
                            to = out[kind] if width > 1 else out[0].at[kind]
                            part = value[0, kind * rows : (kind + 1) * rows] if self.tail else value[kind]
                            to[span, self.spans[stream]] = part

        if summed:
            outs = outs + [shape((self.tail, lanes), f32)]
        operands = [*self.keep, *self.got]
        made = list(call(kernel, outs, operands, scalars, tokens=tokens, weight=8))
        self.step += 1
        self.token = made[0]
        if last:
            self.result = made[:width]
        elif halving:
            self.start(made[: width // 2], made[width // 2 : width])
        else:
            self.start(made[:width], made[:width])
        return made[width] if summed else None


def chunk(k, rows):
    return pl.ds(pl.multiple_of((k ^ lax.axis_index("fsdp")) * rows, rows), rows)


def first_parity(table):
    return lax.rem(table[0, lax.axis_index("context")], 2)


def invert(table, inverse_ref):
    def note(i):
        half = i % 2 if isinstance(i, int) else lax.rem(i, 2)
        inverse_ref[table[half, i // 2]] = i

    loop(2 * table.shape[1], note)


def store_parts(plan, parity, t, out_ref, b, kind):
    size, heads, group, members, dim, piece, batches = plan
    for h in range(heads):
        block = t[h * dim : (h + 1) * dim]
        cut = [block[:, s * piece : (s + 1) * piece] for s in range(2)]
        if b < batches - 1:
            for u in range(members):
                for s in range(2):
                    out_ref[h * group + b * members + u, 2 * kind + s] = cut[s]
        else:
            base = out_ref.shape[1] // 2 + 1
            for e in range(group):
                if kind == 0:
                    out_ref[h * group + e, base] = jnp.where(parity == e % 2, cut[0], cut[1])
                else:
                    for s in range(2):
                        out_ref[h * group + e, base + 2 * kind - 1 + s] = cut[s]


def project_kernel(plan, spread, sc, *refs):
    x_refs, (w_ref, gain_ref, bias_ref, factor_ref, n1_ref, send_ref) = refs[:spread], refs[spread:]
    batches = plan[6]
    rows = x_refs[0].shape[1]
    parity = first_parity(sc)
    for b in range(batches):
        for k in range(spread):
            x = x_refs[k][b].astype(f32)
            r = lax.rsqrt(jnp.mean(x * x, axis=-1, keepdims=True) + epsilon)
            n1_ref[b, chunk(k, rows), :] = (x * r * gain_ref[...]).astype(bf16)
    n1 = n1_ref[...].reshape(-1, n1_ref.shape[2])
    for i in range(3):
        y = mm(w_ref[i], n1, cols_cols)
        if i == 0:
            y = (y + bias_ref[:, 0:1]) * factor_ref[...]
        elif i == 2:
            y = y + bias_ref[:, 1:2]
        y = y.astype(bf16)
        for b in range(batches):
            store_parts(plan, parity, y[:, b * spread * rows : (b + 1) * spread * rows], send_ref, b, i)


def place(inverse_ref, index):
    slot = inverse_ref[index]
    return slot // 2, lax.rem(slot, 2)


def turned(block):
    filled = jnp.concatenate([block, jnp.zeros((128 - block.shape[0], block.shape[1]), block.dtype)], 0)
    return filled.T


def key_parts(block_index, stride, piece, seq):
    free = 2 * block_index * stride * piece
    last = min(((2 * block_index + 2) * stride + 2) * piece, seq)
    return free, last


def attend_kernel(plans, sc, got_ref, *refs):
    units = len(plans)
    ends, o_ref, outs, scratch = refs[:units], refs[units], refs[units + 1 : -4], refs[-4:]
    invert(sc, scratch[0])
    for i, plan in enumerate(plans):
        attend_unit(plan, got_ref, ends[i], o_ref, outs[i], *scratch)


def attend_unit(plan, got_ref, end_ref, o_ref, lse_ref, inverse_ref, k_ref, vt_ref, qt_ref):
    pieces, piece, dim, stride, q_parts, base, o_base = plan
    offset = lax.rem(lax.axis_index("context"), stride)
    seq = pieces * piece
    asked = pieces // stride

    def fill(p):
        at, which = place(inverse_ref, p)
        span = pl.ds(p * piece if isinstance(p, int) else pl.multiple_of(p * piece, piece), piece)
        k_ref[span, :] = turned(got_ref[at, base + q_parts + which])
        vt_ref[:, span] = got_ref[at, base + q_parts + 2 + which]

    loop(pieces, fill)
    for j in range(asked):
        at, which = place(inverse_ref, j * stride + offset)
        qt_ref[0:dim, j * piece : (j + 1) * piece] = got_ref[at, base + (which if q_parts == 2 else 0)]
    qt_ref[dim:, :] = jnp.zeros_like(qt_ref[dim:, :])
    if asked != o_ref.shape[0] * q_parts:
        for part in range(q_parts):
            o_ref[:, o_base + part] = jnp.zeros_like(o_ref[:, o_base + part])
    wide = 2 * piece
    for i in range(asked // 2):
        span = slice(i * wide, (i + 1) * wide)
        qt = qt_ref[:, span]
        end = end_ref[:, span]
        free, last = key_parts(i, stride, piece, seq)
        if last <= key_tile:
            masked = mm(k_ref[free:last, :], qt)
            at = lax.broadcasted_iota(jnp.int32, masked.shape, 0) + free
            masked = jnp.where(at < end, masked, negative)
            top = jnp.max(masked, axis=0, keepdims=True)
            if free:
                plain = mm(k_ref[0:free, :], qt)
                top = jnp.maximum(top, jnp.max(plain, axis=0, keepdims=True))
            weight = jnp.exp(masked - top)
            total = jnp.sum(weight, axis=0, keepdims=True)
            out = mm(vt_ref[:, free:last], weight.astype(bf16))
            if free:
                weight = jnp.exp(plain - top)
                total = total + jnp.sum(weight, axis=0, keepdims=True)
                out = out + mm(vt_ref[:, 0:free], weight.astype(bf16))
        else:

            def tile(t, carry):
                top, total, out = carry
                first = pl.multiple_of(t * loop_tile, loop_tile)
                scores = mm(k_ref[pl.ds(first, loop_tile), :], qt)
                at = lax.broadcasted_iota(jnp.int32, scores.shape, 0) + first
                scores = jnp.where(at < end, scores, negative)
                new = jnp.maximum(top, jnp.max(scores, axis=0, keepdims=True))
                weight = jnp.exp(scores - new)
                change = jnp.exp(top - new)
                total = total * change + jnp.sum(weight, axis=0, keepdims=True)
                out = out * change + mm(vt_ref[:, pl.ds(first, loop_tile)], weight.astype(bf16))
                return new, total, out

            start = (jnp.full((1, wide), negative, f32), jnp.zeros((1, wide), f32), jnp.zeros((dim, wide), f32))
            tiles = min(-(-last // loop_tile), seq // loop_tile)
            top, total, out = lax.fori_loop(0, tiles, tile, start)
        out = out / total
        lse_ref[:, span] = top + jnp.log(total)
        for s in range(2):
            at, which = place(inverse_ref, (2 * i + s) * stride + offset)
            o_ref[at, o_base + (which if q_parts == 2 else 0)] = out[:, s * piece : (s + 1) * piece].astype(bf16)


def attend_back_kernel(plans, sc, got_ref, do_ref, factor_ref, *refs):
    units = len(plans)
    o_ref, saved, (d_ref, scale_ref), scratch = refs[0], refs[1 : 1 + 2 * units], refs[1 + 2 * units : 3 + 2 * units], refs[3 + 2 * units :]
    scale = 0.0
    invert(sc, scratch[0])
    for i, plan in enumerate(plans):
        own = saved[2 * i : 2 * i + 2]
        scale = scale + attend_back_unit(plan, got_ref, do_ref, factor_ref, o_ref, *own, d_ref, *scratch)
    scale_ref[...] = scale


def attend_back_unit(
    plan, got_ref, do_ref, factor_ref, o_ref, end_ref, lse_ref, d_ref,
    inverse_ref, k_ref, kt_ref, v_ref, qt_ref, q_ref, dot_ref, dor_ref, dk_ref, dv_ref,
):
    pieces, piece, dim, stride, q_parts, base, o_base = plan
    offset = lax.rem(lax.axis_index("context"), stride)
    seq = pieces * piece
    asked = pieces // stride

    def fill(p):
        at, which = place(inverse_ref, p)
        span = pl.ds(p * piece if isinstance(p, int) else pl.multiple_of(p * piece, piece), piece)
        kt = got_ref[at, base + q_parts + which]
        if seq <= key_tile:
            kt_ref[:, span] = kt
        k_ref[span, :] = turned(kt)
        v_ref[span, :] = turned(got_ref[at, base + q_parts + 2 + which])

    loop(pieces, fill)
    for j in range(asked):
        at, which = place(inverse_ref, j * stride + offset)
        span = slice(j * piece, (j + 1) * piece)
        qt = got_ref[at, base + (which if q_parts == 2 else 0)]
        qt_ref[0:dim, span] = qt
        q_ref[span, :] = turned(qt)
        do = do_ref[at, o_base + (which if q_parts == 2 else 0)]
        dot_ref[0:dim, span] = do
        dor_ref[span, :] = turned(do)
    qt_ref[dim:, :] = jnp.zeros_like(qt_ref[dim:, :])
    dot_ref[dim:, :] = jnp.zeros_like(dot_ref[dim:, :])
    dk_ref[...] = jnp.zeros_like(dk_ref)
    dv_ref[...] = jnp.zeros_like(dv_ref)
    if asked != d_ref.shape[0] * q_parts:
        for part in range(q_parts):
            d_ref[:, base + part] = jnp.zeros_like(d_ref[:, base + part])
    wide = 2 * piece
    scale = jnp.zeros((dim, 1), f32)
    for i in range(asked // 2):
        span = slice(i * wide, (i + 1) * wide)
        qt, q, do, dor = qt_ref[:, span], q_ref[span, :], dot_ref[:, span], dor_ref[span, :]
        end, lse = end_ref[:, span], lse_ref[:, span]
        owners = [place(inverse_ref, (2 * i + s) * stride + offset) for s in range(2)]
        o = jnp.concatenate([o_ref[at, o_base + (which if q_parts == 2 else 0)] for at, which in owners], axis=1)
        delta = jnp.sum(do[0:dim].astype(f32) * o.astype(f32), axis=0, keepdims=True)
        free, last = key_parts(i, stride, piece, seq)

        def visit(keys, masked_from):
            scores = mm(k_ref[keys, :], qt)
            if masked_from is not None:
                at = lax.broadcasted_iota(jnp.int32, scores.shape, 0) + masked_from
                scores = jnp.where(at < end, scores, negative)
            prob = jnp.exp(scores - lse)
            ds = (prob * (mm(v_ref[keys, :], do) - delta)).astype(bf16)
            dv_ref[keys, :] += mm(prob.astype(bf16), dor)
            dk_ref[keys, :] += mm(ds, q)
            return mm(kt_ref[:, keys] if seq <= key_tile else k_ref[keys, :].T[0:dim], ds)

        if last <= key_tile:
            dq = visit(pl.ds(free, last - free), free)
            if free:
                dq = dq + visit(pl.ds(0, free), None)
        else:

            def tile(t, dq):
                first = pl.multiple_of(t * loop_tile, loop_tile)
                return dq + visit(pl.ds(first, loop_tile), first)

            tiles = min(-(-last // loop_tile), seq // loop_tile)
            dq = lax.fori_loop(0, tiles, tile, jnp.zeros((dim, wide), f32))
        scale = scale + jnp.sum(dq * qt[0:dim].astype(f32), axis=1, keepdims=True)
        dq = (dq * factor_ref[...]).astype(bf16)
        for s in range(2):
            at, which = place(inverse_ref, (2 * i + s) * stride + offset)
            d_ref[at, base + (which if q_parts == 2 else 0)] = dq[:, s * piece : (s + 1) * piece]

    def give(p):
        at, which = place(inverse_ref, p)
        span = pl.ds(p * piece if isinstance(p, int) else pl.multiple_of(p * piece, piece), piece)
        d_ref[at, base + q_parts + which] = dk_ref[span, :].T[0:dim].astype(bf16)
        d_ref[at, base + q_parts + 2 + which] = dv_ref[span, :].T[0:dim].astype(bf16)

    loop(pieces, give)
    return scale


def total_of(blocks):
    if len(blocks) == 1:
        return blocks[0]
    return sum(b.astype(f32) for b in blocks[1:]) + blocks[0].astype(f32)


def collect(plan, even, got_ref, b, which, kind):
    size, heads, group, members, dim, piece, batches = plan
    base = got_ref.shape[1] // 2 + 1
    parts = []
    for h in range(heads):
        if b < batches - 1:
            blocks = [got_ref[h * group + b * members + u, 2 * kind + which] for u in range(members)]
        elif kind == 0:
            parity = even if which == 0 else 1 - even
            blocks = [got_ref[h * group + 2 * u + parity, base] for u in range(group // 2)]
        else:
            blocks = [got_ref[h * group + e, base + 2 * kind - 1 + which] for e in range(group)]
        parts.append(total_of(blocks).astype(bf16))
    return jnp.concatenate(parts, axis=0)


def give_rows(value, held_ref, out_refs):
    batches, rows, _ = out_refs[0].shape
    held_ref[...] = value.astype(bf16).reshape(held_ref.shape)
    for k, out_ref in enumerate(out_refs):
        for b in range(batches):
            out_ref[b] = held_ref[b, chunk(k, rows), :]


def flat(ref):
    return ref[...].reshape(-1, ref.shape[-1])


def rows_kernel(plan, sc, got_ref, *refs):
    piece, batches = plan[5], plan[6]
    *out_refs, held_ref = refs
    rows = out_refs[0].shape[1]
    even = first_parity(sc)
    for b in range(batches):
        for s in range(2):
            held_ref[b, s * piece : (s + 1) * piece] = collect(plan, even, got_ref, b, s, 0).T
        for k, out_ref in enumerate(out_refs):
            out_ref[b] = held_ref[b, chunk(k, rows), :]


def middle_kernel(spread, sc, *refs):
    o_refs, *far, bias_refs = [refs[i * spread : (i + 1) * spread] for i in range(5)]
    *refs, near_ref, arrived = refs[5 * spread :]
    copies = [
        [pltpu.make_async_copy(far[i][k], near_ref.at[i, k], arrived.at[i, k]) for k in range(spread)] for i in range(3)
    ]
    for copy in copies[0] + [copies[i][k] for k in range(spread) for i in (1, 2)]:
        copy.start()
    wo, wi, wd = [[near_ref.at[i, k] for k in range(spread)] for i in range(3)]
    x_ref, g_ref, gain_ref, out_bias_ref, out_ref, grad_ref, n2_ref, dy_ref, sums_ref, du_sum_ref = refs[:10]
    hidden_refs, do_refs = [refs[10 + i * spread : 10 + (i + 1) * spread] for i in range(2)]
    kind = out_ref.shape
    h1 = flat(x_ref).astype(f32) + out_bias_ref[0:1]
    for k in range(spread):
        copies[0][k].wait()
        h1 = h1 + mm(flat(o_refs[k]), wo[k][...])
    r2 = lax.rsqrt(jnp.mean(h1 * h1, axis=-1, keepdims=True) + epsilon)
    n2 = (h1 * r2 * gain_ref[1:2]).astype(bf16)
    n2_ref[...] = n2.reshape(kind)
    g = flat(g_ref)
    out = h1 + out_bias_ref[1:2]
    dn2 = 0.0
    for k in range(spread):
        copies[1][k].wait()
        copies[2][k].wait()
        u = mm(n2, wi[k][...], cols_cols) + bias_refs[k][...]
        gate = 1.0 / (1.0 + jnp.exp(-u))
        a = (u * gate).astype(bf16)
        out = out + mm(a, wd[k][...])
        ga = mm(g, wd[k][...], cols_cols)
        du = (ga * gate * (1.0 + u * (1.0 - gate))).astype(bf16)
        dn2 = dn2 + mm(du, wi[k][...])
        hidden_refs[k][0] = a
        hidden_refs[k][1] = du
        du_sum_ref[pl.ds(k ^ lax.axis_index("fsdp"), 1), :] = jnp.sum(du.astype(f32), axis=0, keepdims=True)
    out_ref[...] = out.astype(bf16).reshape(kind)
    z2 = gain_ref[1:2] * dn2
    g = g.astype(f32)
    grad = g + r2 * z2 - h1 * (r2 * r2 * r2 * jnp.mean(z2 * h1, axis=-1, keepdims=True))
    grad_ref[...] = grad.reshape(kind)
    dy = grad.astype(bf16)
    dy_ref[...] = dy.reshape(kind)
    sums_ref[0:1] = jnp.sum(dn2 * h1 * r2, axis=0, keepdims=True)
    sums_ref[1:2] = jnp.sum(grad, axis=0, keepdims=True)
    sums_ref[2:3] = jnp.sum(g, axis=0, keepdims=True)
    for k in range(spread):
        do_refs[k][...] = mm(dy, wo[k][...], cols_cols).astype(bf16).reshape(do_refs[k].shape)


def cut_rows(value, out_ref, kind):
    chunks = out_ref.shape[0]
    rows = value.shape[0] // chunks
    for c in range(chunks):
        part = value[c * rows : (c + 1) * rows]
        if out_ref.shape[1] == 1:
            out_ref[c, 0, kind * rows : (kind + 1) * rows] = part.astype(out_ref.dtype)
        else:
            out_ref[c, kind] = part.astype(out_ref.dtype)


def grads_kernel(spread, sums, sc, *refs):
    o_refs, hidden_refs, dy_refs, n2_refs, g_refs = [refs[i * spread : (i + 1) * spread] for i in range(5)]
    *out_refs, cut_ref = refs[5 * spread :]
    stack = lambda parts: jnp.concatenate([p[...].reshape(-1, p.shape[-1]) for p in parts])
    target = cut_ref if sums else out_refs[0]
    cut_rows(mm(stack([h.at[0] for h in hidden_refs]), stack(g_refs), rows_rows), target, 2)
    cut_rows(mm(stack([h.at[1] for h in hidden_refs]), stack(n2_refs), rows_rows), target, 1)
    cut_rows(mm(stack(o_refs), stack(dy_refs), rows_rows), target, 0)
    if sums:
        deal_cuts(sums, cut_ref, out_refs)


def deal_cuts(sums, cut_ref, out_refs):
    half = len(out_refs) // 2
    read = lambda stream, index: cut_ref[index, :, :, sums.spans[stream]]
    sums.deal(read, out_refs[:half], out_refs[half:], 0)


def close_kernel(terms, sc, *refs):
    part_refs, (x_ref, grad_ref, gain_ref, out_ref) = refs[:terms], refs[terms:]
    dn1 = sum(flat(p).astype(f32) for p in part_refs)
    x = flat(x_ref).astype(f32)
    r1 = lax.rsqrt(jnp.mean(x * x, axis=-1, keepdims=True) + epsilon)
    z1 = gain_ref[0:1] * dn1
    out = flat(grad_ref) + r1 * z1 - x * (r1 * r1 * r1 * jnp.mean(z1 * x, axis=-1, keepdims=True))
    out_ref[...] = out.astype(bf16).reshape(out_ref.shape)


def ahead_kernel(plan, spread, sc, *refs):
    do_refs, (send_ref, held_ref) = refs[:spread], refs[spread:]
    rows = do_refs[0].shape[1]
    parity = first_parity(sc)
    for b in range(plan[6]):
        for k in range(spread):
            held_ref[b, chunk(k, rows), :] = do_refs[k][b]
        store_parts(plan, parity, held_ref[b].T, send_ref, b, 0)


def back_kernel(plan, spread, sums, sc, got_ref, w_ref, n1_ref, gain_ref, small_ref, out_small_ref, *refs):
    size, heads, group, members, dim, piece, batches = plan
    part_refs, refs = refs[:spread], refs[spread:]
    *out_refs, held_ref, turned_ref, cut_ref = refs
    local = heads * dim
    even = first_parity(sc)
    out_small_ref[...] = small_ref[...]
    total = 0.0
    bias = []
    n1 = flat(n1_ref)
    target = cut_ref if sums else out_refs[0]
    for kind in range(3):
        for b in range(batches):
            for s in range(2):
                at = (2 * b + s) * piece
                turned_ref[:, at : at + piece] = collect(plan, even, got_ref, b, s, kind)
        turned_rows = turned_ref[...]
        rows = turned_rows.T
        if kind != 1:
            bias.append(jnp.sum(rows.astype(f32), axis=0, keepdims=True))
        total = total + mm(rows, w_ref[kind])
        cut_rows(mm(turned_rows, n1), target, kind)
    give_rows(total, held_ref, part_refs)
    out_small_ref[0:1] = jnp.sum(total * n1.astype(f32), axis=0, keepdims=True) / gain_ref[...]
    for i in range(2):
        out_small_ref[5:6, i * local : (i + 1) * local] = bias[i]
    if sums:
        for c in range(cut_ref.shape[0]):
            cut_ref[c, 0, sums.kinds * sums.rows :] = out_small_ref[...]
    if sums:
        deal_cuts(sums, cut_ref, out_refs)


def shards(
    layer_input, output_cotangent, qkv_weight, out_weight, in_weight, down_weight, qv_bias, in_bias,
    out_bias, norm_gains, query_scale, block_table, block_marks,
):
    batches, own, width = layer_input.shape
    local = qkv_weight.shape[2]
    dim = query_scale.shape[0]
    heads = local // dim
    size = lax.axis_size("context")
    spread = lax.axis_size("fsdp")
    pieces = block_table.shape[0] * 2
    seq = block_marks.shape[1]
    piece = seq // pieces
    group = size // heads
    members = group // (batches - 1)
    plan = (size, heads, group, members, dim, piece, batches)
    rows = own * spread
    me = lax.axis_index("context")
    member = me % group
    scalars = block_table.T
    here = jnp.arange(1, seq + 1, dtype=jnp.int32)
    closing = jnp.concatenate([block_marks[:, 1:] != block_marks[:, :-1], jnp.ones((batches, 1), bool)], axis=1)
    ends = lax.cummin(jnp.where(closing, here, seq), axis=1, reverse=True)
    main_end = lax.dynamic_index_in_dim(ends, member // members, 0, keepdims=False)
    main_end = main_end.reshape(-1, members, piece)
    main_end = lax.dynamic_index_in_dim(main_end, member % members, 1, keepdims=False).reshape(1, -1)
    last_end = ends[batches - 1].reshape(-1, group, piece)
    last_end = lax.dynamic_index_in_dim(last_end, member, 1, keepdims=False).reshape(1, -1)
    factor = base_rate / math.sqrt(dim) * jax.nn.softplus(query_scale)
    factor_rows = jnp.tile(factor, heads).reshape(local, 1)
    factor_col = factor.reshape(dim, 1)
    gain_one, gain_two = norm_gains[0:1], norm_gains[1:2]

    tokens = batches * rows
    weight_flops = 2 * tokens * width * local
    qkv_turned = jnp.swapaxes(qkv_weight, 1, 2)
    in_turned = in_weight.T
    whole = shape((batches, rows, width), bf16)
    narrow = shape((batches, rows, local), bf16)
    parts = [shape((batches, own, width), bf16)] * spread
    thin_parts = [shape((batches, own, local), bf16)] * spread
    held = [pltpu.VMEM((batches, rows, width), bf16)]
    thin_held = [pltpu.VMEM((batches, rows, local), bf16)]
    asked = [pieces // members * piece, pieces // group * piece]
    mine = batches * own

    x_parts = gather_rows(layer_input, "fsdp", spread)
    n1, send = call(
        functools.partial(project_kernel, plan, spread),
        [whole, shape((size, 11, dim, piece), bf16)],
        [*x_parts, qkv_turned, gain_one, qv_bias.T, factor_rows],
        scalars,
        tokens=[main_end, last_end],
    )
    got = swap_all(send, "context")
    plans = [(pieces, piece, dim, members, 2, 0, 0), (pieces, piece, dim, group, 1, 6, 2)]
    o_send, main_lse, last_lse = call(
        functools.partial(attend_kernel, plans),
        [shape((size, 3, dim, piece), bf16)] + [shape((1, a), f32) for a in asked],
        [got, main_end, last_end],
        scalars,
        [
            pltpu.SMEM((pieces,), jnp.int32), pltpu.VMEM((seq, 128), bf16), pltpu.VMEM((dim, seq), bf16),
            pltpu.VMEM((128, asked[0]), bf16),
        ],
    )
    others = [out_weight, in_turned, down_weight, in_bias.reshape(1, local), output_cotangent]
    *others, g_copy = others
    others = [gather_rows(v, "fsdp", spread, o_send) for v in others]
    g_first = exchange(g_copy, "fsdp", spread, bits_of(spread) - 1)
    o_parts = call(
        functools.partial(rows_kernel, plan), thin_parts, [swap_all(o_send, "context")], scalars, thin_held,
        tokens=[g_first],
    )
    g_parts = spread_rows(g_copy, g_first, "fsdp", spread, o_parts[0])
    o_local, o_parts = o_parts, swap_parts(o_parts, "fsdp", spread)
    even_cuts = local % (8 * size) == 0
    cuts = size if even_cuts else 1
    cut_shape = shape((cuts, 3, local // cuts, width), bf16)
    own_kind = shape((batches, own, width), bf16)
    layer_output, grad_one, n2, dy, sums, du_sum, *rest = call(
        functools.partial(middle_kernel, spread),
        [own_kind, shape((batches, own, width), f32), own_kind, own_kind, shape((3, width), f32), shape((spread, local), f32)]
        + [shape((2, mine, local), bf16)] * spread
        + thin_parts,
        [*o_parts, *others[0], *others[1], *others[2], *others[3], layer_input, output_cotangent, norm_gains, out_bias],
        scalars,
        scratch=[pltpu.VMEM((3, spread, local, width), bf16), pltpu.SemaphoreType.DMA((3, spread))],
        loose=range(spread, 4 * spread),
    )
    hidden_parts, do_parts = rest[:spread], swap_parts(rest[spread:], "fsdp", spread)
    (do_send,) = call(
        functools.partial(ahead_kernel, plan, spread),
        [shape((size, 3, dim, piece), bf16)],
        do_parts,
        scalars,
        thin_held,
    )
    do_got = swap_all(do_send, "context")
    hidden_parts = swap_parts(hidden_parts, "fsdp", spread)
    n2_first = exchange(n2, "fsdp", spread, bits_of(spread) - 1)
    dy_first = exchange(dy, "fsdp", spread, bits_of(spread) - 1)
    d_send, scale_sum = call(
        functools.partial(attend_back_kernel, plans),
        [shape((size, 11, dim, piece), bf16), shape((dim, 1), f32)],
        [got, do_got, factor_col, o_send, main_end, main_lse, last_end, last_lse],
        scalars,
        most=vmem_bytes if seq <= key_tile else full_bytes,
        scratch=[
            pltpu.SMEM((pieces,), jnp.int32),
            pltpu.VMEM((seq, 128), bf16), pltpu.VMEM((dim, min(seq, key_tile)), bf16), pltpu.VMEM((seq, 128), bf16),
            pltpu.VMEM((128, asked[0]), bf16), pltpu.VMEM((asked[0], 128), bf16),
            pltpu.VMEM((128, asked[0]), bf16), pltpu.VMEM((asked[0], 128), bf16),
            pltpu.VMEM((seq, 128), f32), pltpu.VMEM((seq, 128), f32),
        ],
    )
    n2_parts = spread_rows(n2, n2_first, "fsdp", spread, scale_sum)
    dy_parts = spread_rows(dy, dy_first, "fsdp", spread, scale_sum)
    cut = width * first_share // 1280 // 128 * 128
    new_sums = lambda tail: Sums(size, 3, local // size, width, cut, tail) if even_cuts else None
    early, last = new_sums(0), new_sums(8)
    last_cut = (size, 1, 3 * local // size + 8, width) if even_cuts else (8, 128)
    dealt = early.shapes(0) * 2 if even_cuts else [cut_shape]
    cut_scratch = [pltpu.VMEM(cut_shape.shape, bf16)]
    early_made = call(
        functools.partial(grads_kernel, spread, early),
        dealt,
        [*o_local, *hidden_parts, *dy_parts, *n2_parts, *g_parts],
        scalars,
        cut_scratch,
        tokens=[scale_sum],
    )
    d_got = swap_all(after(d_send, hidden_parts[1:], n2_first), "context")
    small = [jnp.zeros((1, width), f32), sums, du_sum.reshape(1, width), jnp.zeros((2, width), f32)]
    small.append(jnp.pad(scale_sum.reshape(1, dim) / factor, ((0, 0), (0, width - dim))))
    small = jnp.concatenate(small)
    for bit in range(bits_of(spread)):
        small = small + exchange(small, "fsdp", spread, bit)
    if even_cuts:
        early.start(early_made[: len(early_made) // 2], early_made[len(early_made) // 2 :])
        for _ in range(ahead_rounds):
            early.fold(scalars)
    small, *made = call(
        functools.partial(back_kernel, plan, spread, last),
        [shape(small.shape, f32)] + parts + (last.shapes(0) * 2 if even_cuts else [cut_shape]),
        [d_got, qkv_turned, n1, gain_one, small],
        scalars,
        held + [pltpu.VMEM((local, tokens), bf16), pltpu.VMEM(last_cut, f32)],
        tokens=[early.token] if even_cuts and ahead_rounds else [],
    )
    part, made = made[:spread], made[spread:]
    dn1_terms, _ = scatter_parts(part, "fsdp", spread)

    def close(*tokens):
        return call(
            functools.partial(close_kernel, len(dn1_terms)),
            [own_kind],
            [*dn1_terms, layer_input, grad_one, norm_gains],
            scalars,
            tokens=tokens,
        )[0]

    qkv_kind = shape((3, local, width), f32)
    if even_cuts:
        last.start(made[: len(made) // 2], made[len(made) // 2 :])
        order = round_order
        order = [early if name == "E" else last for name in order]
        ends = {early: [shape((local, width), f32)] * 3, last: [qkv_kind]}
        seen = small
        for index, flow in enumerate(order):
            finals = ends[flow] if flow.step == 2 * flow.bits - 1 else []
            added = flow.fold(scalars, finals, [seen])
            seen = flow.token
            if added is not None:
                small = added
            if index == 5:
                input_grad = close(seen)
                seen = input_grad
        (qkv,) = last.result
        out_grad, *feed_grads = early.result
    else:
        small = lax.psum(small, "context")
        input_grad = close()
        whole_sum = lambda v: lax.psum(v, "context").astype(f32).reshape(3, local, width)
        qkv = whole_sum(made[0])
        out_grad, *feed_grads = whole_sum(early_made[0])
    first_gain = small[0:1]
    for bit in range(bits_of(spread)):
        first_gain = first_gain + exchange(first_gain, "fsdp", spread, bit)
    gains_grad = jnp.concatenate([first_gain, small[1:2]])
    out_bias_grad = small[2:4]
    in_bias_grad = small[4].reshape(spread, local)
    in_bias_grad = lax.dynamic_index_in_dim(in_bias_grad, lax.axis_index("fsdp"), 0, keepdims=False)
    qv_grad = small[5, : 2 * local].reshape(2, local)
    scale_grad = small[7, :dim] * (base_rate / math.sqrt(dim)) * jax.nn.sigmoid(query_scale)
    return (
        layer_output,
        input_grad,
        jnp.swapaxes(qkv, 1, 2),
        out_grad,
        feed_grads[0].T,
        feed_grads[1],
        qv_grad,
        in_bias_grad,
        out_bias_grad,
        gains_grad,
        scale_grad,
    )


def solution(mesh):
    in_specs = (
        P(None, ("context", "fsdp"), None),
        P(None, ("context", "fsdp"), None),
        P(None, None, "fsdp"),
        P("fsdp", None),
        P(None, "fsdp"),
        P("fsdp", None),
        P(None, "fsdp"),
        P("fsdp"),
        P(),
        P(),
        P(),
        P(),
        P(),
    )
    out_specs = (
        P(None, ("context", "fsdp"), None),
        P(None, ("context", "fsdp"), None),
        P(None, None, "fsdp"),
        P("fsdp", None),
        P(None, "fsdp"),
        P("fsdp", None),
        P(None, "fsdp"),
        P("fsdp"),
        P(),
        P(),
        P(),
    )
    return jax.shard_map(shards, mesh=mesh, in_specs=in_specs, out_specs=out_specs, check_vma=False)
```
